128 devices in a mesh: row: 8 (over y, z_hi), col: 16 (over z_lo, x, core).
Axes of the slice: x: 4, y: 4, z: 4 (z_hi: 2, z_lo: 2; z = z_hi * 2 + z_lo), core: 2. Of those that a mesh axis runs over, the one named last changes fastest.
Arguments:
- alignment: bfloat16 [256, 1024, 256], P(('row', 'col')), may hold values from -6 to 6
- left_weight: bfloat16 [256, 32], replicated, may hold values from -0.375 to 0.375
- right_weight: bfloat16 [256, 32], replicated, may hold values from -0.375 to 0.375
- out_weight: bfloat16 [1024, 128], replicated, may hold values from -1 to 1
- out_bias: bfloat16 [128], replicated, may hold values from -3 to 3
- pair_cotangent: bfloat16 [1024, 1024, 128], P('row', 'col'), may hold values from -6 to 6
Outputs:
- pair_update: bfloat16 [1024, 1024, 128], P('row', 'col')
- grad_alignment: bfloat16 [256, 1024, 256], P(('row', 'col'))
- grad_out_weight: float32 [1024, 128], P(('row', 'col'))
- grad_left_weight: float32 [256, 32], replicated
- grad_right_weight: float32 [256, 32], replicated
The draws below stay inside these ranges and needn't reach their ends.
All inputs are finite; a program needn't handle non-finite values.
Results may differ from the reference program's by a relative error of at most 0.024.
Values may be sent and summed in bfloat16 or wider, within the bound.
No kernel may reach another device: no remote copies, remote signals or barrier semaphores. Data moves between devices by JAX's collectives and lax.ppermute only.
A program may use at most 192 MiB of HBM per device.

```python
import jax
import jax.numpy as jnp
from jax import lax

CM = 256
CH = 32
CZ = 128
ROW_RES = 128
SEQS = 256
RESIDUES = 1024


def level_of(key, shape, cuts, smallest, high):
    def one(dim, shards_of):
        heights = jax.random.uniform(jax.random.fold_in(jax.random.fold_in(key, 6), dim), (shards_of,), jnp.float32, smallest / len(cuts), high / len(cuts))
        return jnp.repeat(jnp.exp(heights), shape[dim] // shards_of).reshape((-1,) + (1,) * (len(shape) - dim - 1))

    factor_of = one(*cuts[0])
    for cut in cuts[1:]:
        factor_of = factor_of * one(*cut)
    return factor_of


def normal_values(stream_key, extent, width, bound, split=(), held_as=jnp.bfloat16):
    result = width * jax.random.normal(stream_key, extent, jnp.float32)
    if split:
        result = result * level_of(stream_key, extent, split, -0.22, 0.18)
    return jnp.clip(result, -bound, bound).astype(held_as)


def setup_inputs(seed: int = 0) -> dict:
    keys = jax.random.split(jax.random.key(seed), 7)
    alignment = normal_values(keys[0], (SEQS, RESIDUES, CM), 1.0, 6.0, ((0, 128),))
    left_weight = normal_values(keys[1], (CM, CH), CM ** -0.5, 0.375)
    right_weight = normal_values(keys[2], (CM, CH), CM ** -0.5, 0.375)
    out_weight = normal_values(keys[3], (CH * CH, CZ), CH ** -0.5, 1.0)
    out_bias = normal_values(keys[4], (CZ,), 0.5, 3.0)
    pair_cotangent = normal_values(keys[5], (RESIDUES, RESIDUES, CZ), 1.0, 6.0, ((0, 8), (1, 16)))
    return {"alignment": alignment, "left_weight": left_weight, "right_weight": right_weight, "out_weight": out_weight, "out_bias": out_bias, "pair_cotangent": pair_cotangent}


def layer_norm(values):
    centered = values - lax.optimization_barrier(jnp.mean(values, axis=-1, keepdims=True))
    inv_sigma = lax.rsqrt(lax.optimization_barrier(jnp.mean(centered * centered, axis=-1, keepdims=True)) + 1e-05)
    return (centered * inv_sigma, inv_sigma)

def norm_backward(upstream, normed, inv_sigma):
    first = lax.optimization_barrier(jnp.mean(upstream, axis=-1, keepdims=True))
    second = lax.optimization_barrier(jnp.mean(upstream * normed, axis=-1, keepdims=True))
    return inv_sigma * (upstream - first - normed * second)

def reference(alignment, left_weight, right_weight, out_weight, out_bias, pair_cotangent):
    normed, inv_sigma = layer_norm(alignment.astype(jnp.float32))
    normed_low = normed.astype(jnp.bfloat16)
    left = jnp.einsum('src,ch->srh', normed_low.astype(jnp.float32), left_weight.astype(jnp.float32)).astype(jnp.bfloat16)
    right = jnp.einsum('src,ch->srh', normed_low.astype(jnp.float32), right_weight.astype(jnp.float32)).astype(jnp.bfloat16)
    inverse_count = 1.0 / SEQS
    blocks = RESIDUES // ROW_RES
    left_blocks = left.reshape(SEQS, blocks, ROW_RES, CH).transpose(1, 0, 2, 3)
    cot_blocks = pair_cotangent.reshape(blocks, ROW_RES, RESIDUES, CZ)
    right_wide = right.astype(jnp.float32)

    def step(carry, item):
        weight_grad, right_grad = carry
        left_block, cot_block = item
        left_wide = left_block.astype(jnp.float32)
        outer_mean = jnp.einsum('sic,sje->ijce', left_wide, right_wide) * inverse_count
        outer_low = outer_mean.astype(jnp.bfloat16).reshape(ROW_RES * RESIDUES, CH * CH)
        update = jnp.dot(outer_low, out_weight, preferred_element_type=jnp.float32) + out_bias.astype(jnp.float32)
        cot_flat = cot_block.reshape(ROW_RES * RESIDUES, CZ)
        weight_grad = weight_grad + jnp.dot(outer_low.T, cot_flat, preferred_element_type=jnp.float32)
        outer_grad = (jnp.dot(cot_flat, out_weight.T, preferred_element_type=jnp.float32) * inverse_count).astype(jnp.bfloat16)
        outer_grad = outer_grad.reshape(ROW_RES, RESIDUES, CH, CH).astype(jnp.float32)
        left_grad = jnp.einsum('ijce,sje->sic', outer_grad, right_wide)
        right_grad = right_grad + jnp.einsum('ijce,sic->sje', outer_grad, left_wide)
        return ((weight_grad, right_grad), (update.astype(jnp.bfloat16).reshape(ROW_RES, RESIDUES, CZ), left_grad))
    init = (jnp.zeros((CH * CH, CZ), jnp.float32), jnp.zeros((SEQS, RESIDUES, CH), jnp.float32))
    (weight_grad, right_sum), (updates, left_parts) = lax.scan(step, init, (left_blocks, cot_blocks))
    pair_update = updates.reshape(RESIDUES, RESIDUES, CZ)
    left_grad = left_parts.transpose(1, 0, 2, 3).reshape(SEQS, RESIDUES, CH).astype(jnp.bfloat16)
    right_grad = right_sum.astype(jnp.bfloat16)
    flat_normed = normed_low.reshape(SEQS * RESIDUES, CM)
    flat_left = left_grad.reshape(SEQS * RESIDUES, CH)
    flat_right = right_grad.reshape(SEQS * RESIDUES, CH)
    grad_left_weight = jnp.dot(flat_normed.T, flat_left, preferred_element_type=jnp.float32)
    grad_right_weight = jnp.dot(flat_normed.T, flat_right, preferred_element_type=jnp.float32)
    upstream = jnp.dot(flat_left, left_weight.T, preferred_element_type=jnp.float32) + jnp.dot(flat_right, right_weight.T, preferred_element_type=jnp.float32)
    upstream = upstream.reshape(SEQS, RESIDUES, CM)
    grad_alignment = norm_backward(upstream, normed, inv_sigma).astype(jnp.bfloat16)
    return (pair_update, grad_alignment, weight_grad, grad_left_weight, grad_right_weight)
```

```python
import functools

import jax
import jax.numpy as jnp
from jax import lax
from jax.experimental import pallas as pl
from jax.experimental.pallas import tpu as pltpu
from jax.sharding import PartitionSpec as P

BOTH = ("row", "col")
TILE = 16
VMEM_BYTES = 48 * 1024 * 1024
NT = (((1,), (1,)), ((), ()))


def layer_norm(values):
    centered = values - jnp.mean(values, axis=-1, keepdims=True)
    inv_sigma = lax.rsqrt(jnp.mean(centered * centered, axis=-1, keepdims=True) + 1e-05)
    return (centered * inv_sigma, inv_sigma)


def norm_backward(upstream, normed, inv_sigma):
    first = jnp.mean(upstream, axis=-1, keepdims=True)
    second = jnp.mean(upstream * normed, axis=-1, keepdims=True)
    return inv_sigma * (upstream - first - normed * second)


def outer_grad_tile(weight_ref, cot_ref, grad_ref, width):
    tile, rows, pair_width = cot_ref.shape
    flat = cot_ref[...].reshape(tile * rows, pair_width)
    step = 2
    for j in range(0, tile, step):
        grads = lax.dot_general(
            weight_ref[...], flat[j * rows:(j + step) * rows], NT, preferred_element_type=jnp.float32
        ).astype(jnp.bfloat16)
        for k in range(step):
            for c in range(width):
                grad_ref[(j + k) * width:(j + k + 1) * width, c * rows:(c + 1) * rows] = grads[
                    c * width:(c + 1) * width, k * rows:(k + 1) * rows
                ]


def left_kernel(inverse, width, right_ref, weight_ref, cot_ref, out_ref, grad_ref, acc_ref):
    step = pl.program_id(0)
    outer_grad_tile(weight_ref, cot_ref, grad_ref, width)
    chunk = 1024

    @pl.when(step == 0)
    def _():
        acc_ref[...] = jnp.zeros_like(acc_ref)

    for n in range(0, acc_ref.shape[1], chunk):
        acc_ref[:, n:n + chunk] += jnp.dot(
            right_ref[...], grad_ref[:, n:n + chunk], preferred_element_type=jnp.float32
        )

    @pl.when(step == pl.num_programs(0) - 1)
    def _():
        out_ref[...] = (acc_ref[...] * inverse).astype(out_ref.dtype)


def right_kernel(inverse, width, left_ref, weight_ref, cot_ref, out_ref, grad_ref, left_t_ref):
    @pl.when(pl.program_id(0) == 0)
    def _():
        left_t_ref[...] = left_ref[...].T

    outer_grad_tile(weight_ref, cot_ref, grad_ref, width)
    grads = jnp.dot(grad_ref[...], left_t_ref[...], preferred_element_type=jnp.float32)
    out_ref[...] = (grads * inverse).T.astype(out_ref.dtype)


def forward_kernel(
    inverse, width, left_ref, right_ref, weight_t_ref, bias_ref, cot_ref, update_ref, wgrad_ref, outer_ref
):
    tile, rows, pair_width = cot_ref.shape
    right_t = right_ref[...].T
    step = 2
    for c in range(0, width, step):
        outer = jnp.dot(
            right_t, left_ref[:, c * rows:(c + step) * rows], preferred_element_type=jnp.float32
        ).astype(jnp.bfloat16)
        for k in range(step):
            for j in range(tile):
                outer_ref[(c + k) * width:(c + k + 1) * width, j * rows:(j + 1) * rows] = outer[
                    j * width:(j + 1) * width, k * rows:(k + 1) * rows
                ]
    for j in range(0, tile, step):
        update = jnp.dot(
            weight_t_ref[...], outer_ref[:, j * rows:(j + step) * rows], preferred_element_type=jnp.float32
        )
        for k in range(step):
            one = update[:, k * rows:(k + 1) * rows].T
            update_ref[j + k] = (one * inverse + bias_ref[...]).astype(update_ref.dtype)

    @pl.when(pl.program_id(0) == 0)
    def _():
        wgrad_ref[...] = jnp.zeros_like(wgrad_ref)

    flat = cot_ref[...].reshape(tile * rows, pair_width)
    wgrad_ref[...] += inverse * jnp.dot(outer_ref[...], flat, preferred_element_type=jnp.float32)


def whole(shape):
    return pl.BlockSpec(shape, lambda j: (0,) * len(shape))


def params():
    return pltpu.CompilerParams(dimension_semantics=("arbitrary",), vmem_limit_bytes=VMEM_BYTES)


def left_grads(right, weight, cot, width, interpret=False):
    seqs, cols, rows, pair_width = right.shape[0], cot.shape[0], cot.shape[1], cot.shape[2]
    flops = 2 * cols * rows * width * width * (pair_width + seqs)
    return pl.pallas_call(
        functools.partial(left_kernel, 1.0 / seqs, width),
        grid=(cols // TILE,),
        in_specs=[
            pl.BlockSpec((seqs, TILE * width), lambda j: (0, j)),
            whole(weight.shape),
            pl.BlockSpec((TILE, rows, pair_width), lambda j: (j, 0, 0)),
        ],
        out_specs=whole((seqs, width * rows)),
        out_shape=jax.ShapeDtypeStruct((seqs, width * rows), jnp.bfloat16),
        scratch_shapes=[
            pltpu.VMEM((TILE * width, width * rows), jnp.bfloat16),
            pltpu.VMEM((seqs, width * rows), jnp.float32),
        ],
        compiler_params=params(),
        cost_estimate=pl.CostEstimate(flops=flops, bytes_accessed=5 * 2**20, transcendentals=0),
        interpret=interpret,
        name="left_grads",
    )(right, weight, cot)


def right_grads(left, weight, cot, width, interpret=False):
    seqs, cols, rows, pair_width = left.shape[0], cot.shape[0], cot.shape[1], cot.shape[2]
    flops = 2 * cols * rows * width * width * (pair_width + seqs)
    return pl.pallas_call(
        functools.partial(right_kernel, 1.0 / seqs, width),
        grid=(cols // TILE,),
        in_specs=[
            whole(left.shape),
            whole(weight.shape),
            pl.BlockSpec((TILE, rows, pair_width), lambda j: (j, 0, 0)),
        ],
        out_specs=pl.BlockSpec((seqs, TILE * width), lambda j: (0, j)),
        out_shape=jax.ShapeDtypeStruct((seqs, cols * width), jnp.bfloat16),
        scratch_shapes=[
            pltpu.VMEM((TILE * width, width * rows), jnp.bfloat16),
            pltpu.VMEM((width * rows, seqs), jnp.bfloat16),
        ],
        compiler_params=params(),
        cost_estimate=pl.CostEstimate(flops=flops, bytes_accessed=5 * 2**20, transcendentals=0),
        interpret=interpret,
        name="right_grads",
    )(left, weight, cot)


def forward(left, right, weight_t, bias, cot, width, interpret=False):
    seqs, cols, rows, pair_width = left.shape[0], cot.shape[0], cot.shape[1], cot.shape[2]
    flops = 2 * cols * rows * width * width * (2 * pair_width + seqs)
    return pl.pallas_call(
        functools.partial(forward_kernel, 1.0 / seqs, width),
        grid=(cols // TILE,),
        in_specs=[
            whole(left.shape),
            pl.BlockSpec((seqs, TILE * width), lambda j: (0, j)),
            whole(weight_t.shape),
            whole(bias.shape),
            pl.BlockSpec((TILE, rows, pair_width), lambda j: (j, 0, 0)),
        ],
        out_specs=[
            pl.BlockSpec((TILE, rows, pair_width), lambda j: (j, 0, 0)),
            whole((width * width, pair_width)),
        ],
        out_shape=[
            jax.ShapeDtypeStruct((cols, rows, pair_width), jnp.bfloat16),
            jax.ShapeDtypeStruct((width * width, pair_width), jnp.float32),
        ],
        scratch_shapes=[pltpu.VMEM((width * width, TILE * rows), jnp.bfloat16)],
        compiler_params=params(),
        cost_estimate=pl.CostEstimate(flops=flops, bytes_accessed=8 * 2**20, transcendentals=0),
        interpret=interpret,
        name="forward",
    )(left, right, weight_t, bias, cot)


def exchange(blocks):
    return lax.all_to_all(blocks, BOTH, 0, 0, tiled=True)


def body(alignment, left_weight, right_weight, out_weight, out_bias, pair_cotangent):
    row_count = lax.axis_size("row")
    col_count = lax.axis_size("col")
    devices = row_count * col_count
    local, residues, model_width = alignment.shape
    width = left_weight.shape[1]
    row_block, col_block, pair_width = pair_cotangent.shape
    seqs = local * devices

    normed, inv_sigma = layer_norm(alignment.astype(jnp.float32))
    normed_low = normed.astype(jnp.bfloat16)
    left = jnp.einsum("src,ch->shr", normed_low, left_weight, preferred_element_type=jnp.float32).astype(
        jnp.bfloat16
    )
    right = jnp.einsum("src,ch->srh", normed_low, right_weight, preferred_element_type=jnp.float32).astype(
        jnp.bfloat16
    )
    left_out = left.reshape(local, width, row_count, row_block).transpose(2, 0, 1, 3)
    left_out = left_out.reshape(row_count, 1, local, width * row_block)
    left_out = jnp.broadcast_to(left_out, (row_count, col_count) + left_out.shape[2:])
    right_out = right.reshape(local, col_count, col_block * width).transpose(1, 0, 2)[None]
    right_out = jnp.broadcast_to(right_out, (row_count,) + right_out.shape[1:])
    right_panel = exchange(right_out.reshape(devices, local, col_block * width)).reshape(seqs, -1)
    left_panel = exchange(left_out.reshape(devices, local, width * row_block)).reshape(seqs, -1)

    cot = pair_cotangent.transpose(1, 0, 2)
    bias = out_bias.astype(jnp.float32).reshape(1, pair_width)
    left_part = left_grads(right_panel, out_weight, cot, width)
    left_back = exchange(left_part.reshape(devices, local, width * row_block))
    right_part = right_grads(left_panel, out_weight, cot, width)
    right_back = exchange(right_part.reshape(devices, local, col_block * width))
    update, weight_term = forward(left_panel, right_panel, out_weight.T, bias, cot, width)
    pair_update = update.transpose(1, 0, 2)
    share = weight_term.shape[0] // devices
    weight_parts = exchange(weight_term.reshape(devices, share, pair_width))
    grad_out_weight = jnp.sum(weight_parts, axis=0)

    left_back = left_back.reshape(row_count, col_count, local, width, row_block).astype(jnp.float32)
    left_grad = jnp.sum(left_back, axis=1).astype(jnp.bfloat16)
    left_grad = left_grad.transpose(1, 2, 0, 3).reshape(local, width, residues)
    right_back = right_back.reshape(row_count, col_count, local, col_block * width).astype(jnp.float32)
    right_grad = jnp.sum(right_back, axis=0).astype(jnp.bfloat16)
    right_grad = right_grad.transpose(1, 0, 2).reshape(local, residues, width)
    left_wgrad = jnp.einsum("src,shr->ch", normed_low, left_grad, preferred_element_type=jnp.float32)
    right_wgrad = jnp.einsum("src,srh->ch", normed_low, right_grad, preferred_element_type=jnp.float32)
    wgrads = jnp.concatenate([left_wgrad.reshape(devices, 1, -1), right_wgrad.reshape(devices, 1, -1)], axis=1)
    total = jnp.sum(exchange(wgrads), axis=0)
    wgrads = exchange(jnp.broadcast_to(total[None], wgrads.shape))
    grad_left_weight = wgrads[:, 0].reshape(model_width, width)
    grad_right_weight = wgrads[:, 1].reshape(model_width, width)

    upstream = jnp.einsum("shr,ch->src", left_grad, left_weight, preferred_element_type=jnp.float32)
    upstream += jnp.einsum("srh,ch->src", right_grad, right_weight, preferred_element_type=jnp.float32)
    grad_alignment = norm_backward(upstream, normed, inv_sigma).astype(jnp.bfloat16)
    return (pair_update, grad_alignment, grad_out_weight, grad_left_weight, grad_right_weight)


def solution(mesh):
    return jax.shard_map(
        body,
        mesh=mesh,
        in_specs=(P(("row", "col"), None, None), P(), P(), P(), P(), P("row", "col", None)),
        out_specs=(
            P("row", "col", None),
            P(("row", "col"), None, None),
            P(("row", "col"), None),
            P(),
            P(),
        ),
        check_vma=False,
    )
```

```python
import functools

import jax
import jax.numpy as jnp
from jax import lax
from jax.experimental import pallas as pl
from jax.experimental.pallas import tpu as pltpu
from jax.sharding import PartitionSpec as P

BOTH = ("row", "col")
TILE = 16
CORES = 2
VMEM_BYTES = 48 * 1024 * 1024
NT = (((1,), (1,)), ((), ()))


def layer_norm(values):
    centered = values - jnp.mean(values, axis=-1, keepdims=True)
    inv_sigma = lax.rsqrt(jnp.mean(centered * centered, axis=-1, keepdims=True) + 1e-05)
    return (centered * inv_sigma, inv_sigma)


def norm_backward(upstream, normed, inv_sigma):
    first = jnp.mean(upstream, axis=-1, keepdims=True)
    second = jnp.mean(upstream * normed, axis=-1, keepdims=True)
    return inv_sigma * (upstream - first - normed * second)


def outer_grad_tile(weight_ref, cot_ref, grad_ref, width):
    tile, rows, pair_width = cot_ref.shape
    flat = cot_ref[...].reshape(tile * rows, pair_width)
    step = 2
    for j in range(0, tile, step):
        grads = lax.dot_general(
            weight_ref[...], flat[j * rows:(j + step) * rows], NT, preferred_element_type=jnp.float32
        ).astype(jnp.bfloat16)
        for k in range(step):
            for c in range(width):
                grad_ref[(j + k) * width:(j + k + 1) * width, c * rows:(c + 1) * rows] = grads[
                    c * width:(c + 1) * width, k * rows:(k + 1) * rows
                ]


def left_kernel(inverse, width, right_ref, weight_ref, cot_ref, out_ref, grad_ref, acc_ref):
    step = pl.program_id(0)
    outer_grad_tile(weight_ref, cot_ref, grad_ref, width)
    chunk = 1024

    @pl.when(step == 0)
    def _():
        acc_ref[...] = jnp.zeros_like(acc_ref)

    for n in range(0, acc_ref.shape[1], chunk):
        acc_ref[:, n:n + chunk] += jnp.dot(
            right_ref[...], grad_ref[:, n:n + chunk], preferred_element_type=jnp.float32
        )

    @pl.when(step == pl.num_programs(0) - 1)
    def _():
        out_ref[...] = (acc_ref[...] * inverse).astype(out_ref.dtype)


def right_kernel(inverse, width, left_ref, weight_ref, cot_ref, out_ref, grad_ref, left_t_ref):
    @pl.when(pl.program_id(0) == 0)
    def _():
        left_t_ref[...] = left_ref[...].T

    outer_grad_tile(weight_ref, cot_ref, grad_ref, width)
    grads = jnp.dot(grad_ref[...], left_t_ref[...], preferred_element_type=jnp.float32)
    out_ref[...] = (grads * inverse).T.astype(out_ref.dtype)


def forward_kernel(
    inverse, width, left_ref, right_ref, weight_t_ref, bias_ref, cot_ref, update_ref, wgrad_ref, outer_ref
):
    tile, rows, pair_width = cot_ref.shape
    right_t = right_ref[...].T
    step = 2
    for c in range(0, width, step):
        outer = jnp.dot(
            right_t, left_ref[:, c * rows:(c + step) * rows], preferred_element_type=jnp.float32
        ).astype(jnp.bfloat16)
        for k in range(step):
            for j in range(tile):
                outer_ref[(c + k) * width:(c + k + 1) * width, j * rows:(j + 1) * rows] = outer[
                    j * width:(j + 1) * width, k * rows:(k + 1) * rows
                ]
    for j in range(0, tile, step):
        update = jnp.dot(
            weight_t_ref[...], outer_ref[:, j * rows:(j + step) * rows], preferred_element_type=jnp.float32
        )
        for k in range(step):
            one = update[:, k * rows:(k + 1) * rows].T
            update_ref[j + k] = (one * inverse + bias_ref[...]).astype(update_ref.dtype)

    @pl.when(pl.program_id(0) == 0)
    def _():
        wgrad_ref[...] = jnp.zeros_like(wgrad_ref)

    flat = cot_ref[...].reshape(tile * rows, pair_width)
    wgrad_ref[...] += inverse * jnp.dot(outer_ref[...], flat, preferred_element_type=jnp.float32)


def whole(shape):
    return pl.BlockSpec(shape, lambda j: (0,) * len(shape))


def params():
    return pltpu.CompilerParams(dimension_semantics=("arbitrary",), vmem_limit_bytes=VMEM_BYTES)


def left_grads(right, weight, cot, width, interpret=False):
    seqs, cols, rows, pair_width = right.shape[0], cot.shape[0], cot.shape[1], cot.shape[2]
    flops = 2 * cols * rows * width * width * (pair_width + seqs)
    return pl.pallas_call(
        functools.partial(left_kernel, 1.0 / seqs, width),
        grid=(cols // TILE,),
        in_specs=[
            pl.BlockSpec((seqs, TILE * width), lambda j: (0, j)),
            whole(weight.shape),
            pl.BlockSpec((TILE, rows, pair_width), lambda j: (j, 0, 0)),
        ],
        out_specs=whole((seqs, width * rows)),
        out_shape=jax.ShapeDtypeStruct((seqs, width * rows), jnp.bfloat16),
        scratch_shapes=[
            pltpu.VMEM((TILE * width, width * rows), jnp.bfloat16),
            pltpu.VMEM((seqs, width * rows), jnp.float32),
        ],
        compiler_params=params(),
        cost_estimate=pl.CostEstimate(flops=flops, bytes_accessed=5 * 2**20, transcendentals=0),
        interpret=interpret,
        name="left_grads",
    )(right, weight, cot)


def right_grads(left, weight, cot, width, interpret=False):
    seqs, cols, rows, pair_width = left.shape[0], cot.shape[0], cot.shape[1], cot.shape[2]
    flops = 2 * cols * rows * width * width * (pair_width + seqs)
    return pl.pallas_call(
        functools.partial(right_kernel, 1.0 / seqs, width),
        grid=(cols // TILE,),
        in_specs=[
            whole(left.shape),
            whole(weight.shape),
            pl.BlockSpec((TILE, rows, pair_width), lambda j: (j, 0, 0)),
        ],
        out_specs=pl.BlockSpec((seqs, TILE * width), lambda j: (0, j)),
        out_shape=jax.ShapeDtypeStruct((seqs, cols * width), jnp.bfloat16),
        scratch_shapes=[
            pltpu.VMEM((TILE * width, width * rows), jnp.bfloat16),
            pltpu.VMEM((width * rows, seqs), jnp.bfloat16),
        ],
        compiler_params=params(),
        cost_estimate=pl.CostEstimate(flops=flops, bytes_accessed=5 * 2**20, transcendentals=0),
        interpret=interpret,
        name="right_grads",
    )(left, weight, cot)


def forward(left, right, weight_t, bias, cot, width, interpret=False):
    seqs, cols, rows, pair_width = left.shape[0], cot.shape[0], cot.shape[1], cot.shape[2]
    flops = 2 * cols * rows * width * width * (2 * pair_width + seqs)
    return pl.pallas_call(
        functools.partial(forward_kernel, 1.0 / seqs, width),
        grid=(cols // TILE,),
        in_specs=[
            whole(left.shape),
            pl.BlockSpec((seqs, TILE * width), lambda j: (0, j)),
            whole(weight_t.shape),
            whole(bias.shape),
            pl.BlockSpec((TILE, rows, pair_width), lambda j: (j, 0, 0)),
        ],
        out_specs=[
            pl.BlockSpec((TILE, rows, pair_width), lambda j: (j, 0, 0)),
            whole((width * width, pair_width)),
        ],
        out_shape=[
            jax.ShapeDtypeStruct((cols, rows, pair_width), jnp.bfloat16),
            jax.ShapeDtypeStruct((width * width, pair_width), jnp.float32),
        ],
        scratch_shapes=[pltpu.VMEM((width * width, TILE * rows), jnp.bfloat16)],
        compiler_params=params(),
        cost_estimate=pl.CostEstimate(flops=flops, bytes_accessed=8 * 2**20, transcendentals=0),
        interpret=interpret,
        name="forward",
    )(left, right, weight_t, bias, cot)


def exchange(blocks):
    return lax.all_to_all(blocks, BOTH, 0, 0, tiled=True)


def swap_cores(values, col_count):
    return lax.ppermute(values, "col", [(i, i ^ 1) for i in range(col_count)])


def parity_order(blocks):
    return jnp.stack([blocks[:, 0], blocks[:, 1, ::-1]], axis=1)


def body(alignment, left_weight, right_weight, out_weight, out_bias, pair_cotangent):
    row_count = lax.axis_size("row")
    col_count = lax.axis_size("col")
    devices = row_count * col_count
    local, residues, model_width = alignment.shape
    width = left_weight.shape[1]
    row_block, col_block, pair_width = pair_cotangent.shape
    seqs = local * devices

    normed, inv_sigma = layer_norm(alignment.astype(jnp.float32))
    normed_low = normed.astype(jnp.bfloat16)
    left = jnp.einsum("src,ch->shr", normed_low, left_weight, preferred_element_type=jnp.float32).astype(
        jnp.bfloat16
    )
    right = jnp.einsum("src,ch->srh", normed_low, right_weight, preferred_element_type=jnp.float32).astype(
        jnp.bfloat16
    )
    chips = col_count // CORES
    left_out = left.reshape(local, width, row_count, row_block).transpose(2, 0, 1, 3)
    left_out = left_out.reshape(row_count, 1, CORES, width * row_block)
    right_out = right.reshape(local, chips, CORES, col_block * width).transpose(1, 2, 0, 3)
    right_out = parity_order(right_out).reshape(1, chips, CORES, local * col_block * width)
    panel_shape = (row_count, chips, CORES)
    sent = jnp.stack(
        [
            jnp.broadcast_to(left_out, panel_shape + left_out.shape[3:]),
            jnp.broadcast_to(right_out, panel_shape + right_out.shape[3:]),
        ],
        axis=3,
    )
    came = exchange(sent.reshape(devices, 2, width * row_block))
    left_own = came[:, 0]
    left_other = swap_cores(left_own, col_count)
    right_panel = jnp.concatenate([came[:, 1, :col_block * width], came[:, 1, col_block * width:]], axis=0)

    cot = pair_cotangent.transpose(1, 0, 2)
    bias = out_bias.astype(jnp.float32).reshape(1, pair_width)
    left_part = left_grads(right_panel, out_weight, cot, width)
    left_panel = jnp.concatenate([left_own, left_other], axis=0)
    left_panel, left_part = lax.optimization_barrier((left_panel, left_part))
    left_share = swap_cores(left_part[devices:], col_count)
    right_part = right_grads(left_panel, out_weight, cot, width)
    left_pair = (left_part[:devices].astype(jnp.float32) + left_share.astype(jnp.float32)).astype(jnp.bfloat16)
    right_pair = jnp.concatenate([right_part[:devices], right_part[devices:]], axis=1)
    sent = jnp.stack([left_pair, right_pair], axis=1)
    sent, left_panel = lax.optimization_barrier((sent, left_panel))
    back = exchange(sent)
    update, weight_term = forward(left_panel, right_panel, out_weight.T, bias, cot, width)
    pair_update = update.transpose(1, 0, 2)

    back = back.reshape(row_count, chips, CORES, 2, width * row_block).astype(jnp.float32)
    left_grad = jnp.sum(back[:, :, :, 0], axis=1).astype(jnp.bfloat16)
    left_grad = left_grad.reshape(row_count, local, width, row_block)
    left_grad = left_grad.transpose(1, 2, 0, 3).reshape(local, width, residues)
    right_grad = jnp.sum(back[:, :, :, 1], axis=0).astype(jnp.bfloat16)
    right_grad = parity_order(right_grad.reshape(chips, CORES, local, col_block * width))
    right_grad = right_grad.transpose(2, 0, 1, 3).reshape(local, residues, width)
    left_wgrad = jnp.einsum("src,shr->ch", normed_low, left_grad, preferred_element_type=jnp.float32)
    right_wgrad = jnp.einsum("src,srh->ch", normed_low, right_grad, preferred_element_type=jnp.float32)
    share = weight_term.shape[0] // devices
    wgrads = jnp.concatenate(
        [
            left_wgrad.reshape(devices, 1, -1),
            right_wgrad.reshape(devices, 1, -1),
            weight_term.reshape(devices, 1, share * pair_width),
        ],
        axis=2,
    )
    total = jnp.sum(exchange(wgrads), axis=0)
    split = wgrads.shape[2] - share * pair_width
    grad_out_weight = total[:, split:].reshape(share, pair_width)
    wgrads = exchange(jnp.broadcast_to(total[None, :, :split], (devices, 1, split)))
    grad_left_weight = wgrads[:, 0, :split // 2].reshape(model_width, width)
    grad_right_weight = wgrads[:, 0, split // 2:].reshape(model_width, width)

    upstream = jnp.einsum("shr,ch->src", left_grad, left_weight, preferred_element_type=jnp.float32)
    upstream += jnp.einsum("srh,ch->src", right_grad, right_weight, preferred_element_type=jnp.float32)
    grad_alignment = norm_backward(upstream, normed, inv_sigma).astype(jnp.bfloat16)
    return (pair_update, grad_alignment, grad_out_weight, grad_left_weight, grad_right_weight)


def solution(mesh):
    return jax.shard_map(
        body,
        mesh=mesh,
        in_specs=(P(("row", "col"), None, None), P(), P(), P(), P(), P("row", "col", None)),
        out_specs=(
            P("row", "col", None),
            P(("row", "col"), None, None),
            P(("row", "col"), None),
            P(),
            P(),
        ),
        check_vma=False,
    )
```

```python
import functools

import jax
import jax.numpy as jnp
import numpy as np
from jax import lax
from jax.experimental import pallas as pl
from jax.experimental.pallas import tpu as pltpu
from jax.sharding import PartitionSpec as P

BOTH = ("row", "col")
TILE = 16
GRAD_TILE = 8
CORES = 2
VMEM_BYTES = 48 * 1024 * 1024
NT = (((1,), (1,)), ((), ()))


def layer_norm(values):
    centered = values - jnp.mean(values, axis=-1, keepdims=True)
    inv_sigma = lax.rsqrt(jnp.mean(centered * centered, axis=-1, keepdims=True) + 1e-05)
    return (centered * inv_sigma, inv_sigma)


def norm_backward(upstream, normed, inv_sigma):
    first = jnp.mean(upstream, axis=-1, keepdims=True)
    second = jnp.mean(upstream * normed, axis=-1, keepdims=True)
    return inv_sigma * (upstream - first - normed * second)


def outer_grad_kernel(width, weight_ref, cot_ref, grad_ref):
    tile, rows, pair_width = cot_ref.shape
    flat = cot_ref[...].reshape(tile * rows, pair_width)
    step = 2
    for j in range(0, tile, step):
        grads = lax.dot_general(
            weight_ref[...], flat[j * rows:(j + step) * rows], NT, preferred_element_type=jnp.float32
        ).astype(jnp.bfloat16)
        for k in range(step):
            for c in range(width):
                grad_ref[(j + k) * width:(j + k + 1) * width, c * rows:(c + 1) * rows] = grads[
                    c * width:(c + 1) * width, k * rows:(k + 1) * rows
                ]


def left_kernel(inverse, right_ref, grad_ref, out_ref):
    grads = jnp.dot(right_ref[...], grad_ref[...], preferred_element_type=jnp.float32)
    out_ref[...] = (grads * inverse).astype(out_ref.dtype)


def right_kernel(inverse, own_ref, other_ref, grad_ref, out_ref):
    half = own_ref.shape[1]
    grads = lax.dot_general(own_ref[...], grad_ref[:, :half], NT, preferred_element_type=jnp.float32)
    grads += lax.dot_general(other_ref[...], grad_ref[:, half:], NT, preferred_element_type=jnp.float32)
    out_ref[...] = (grads * inverse).astype(out_ref.dtype)


def forward_kernel(
    inverse, width, own_ref, other_ref, right_ref, weight_t_ref, bias_ref, cot_ref, update_ref, wgrad_ref, outer_ref
):
    tile, rows, pair_width = cot_ref.shape
    right_t = right_ref[...].T
    step = 2
    for c in range(0, width, step):
        half_ref, first = (own_ref, c) if c < width // 2 else (other_ref, c - width // 2)
        outer = jnp.dot(
            right_t, half_ref[:, first * rows:(first + step) * rows], preferred_element_type=jnp.float32
        ).astype(jnp.bfloat16)
        for k in range(step):
            for j in range(tile):
                outer_ref[(c + k) * width:(c + k + 1) * width, j * rows:(j + 1) * rows] = outer[
                    j * width:(j + 1) * width, k * rows:(k + 1) * rows
                ]
    for j in range(0, tile, step):
        update = jnp.dot(
            weight_t_ref[...], outer_ref[:, j * rows:(j + step) * rows], preferred_element_type=jnp.float32
        )
        for k in range(step):
            one = update[:, k * rows:(k + 1) * rows].T
            update_ref[j + k] = (one * inverse + bias_ref[...]).astype(update_ref.dtype)

    @pl.when(pl.program_id(0) == 0)
    def _():
        wgrad_ref[...] = jnp.zeros_like(wgrad_ref)

    flat = cot_ref[...].reshape(tile * rows, pair_width)
    wgrad_ref[...] += inverse * jnp.dot(outer_ref[...], flat, preferred_element_type=jnp.float32)


def whole(shape):
    return pl.BlockSpec(shape, lambda j: (0,) * len(shape))


def params():
    return pltpu.CompilerParams(dimension_semantics=("arbitrary",), vmem_limit_bytes=VMEM_BYTES)


def outer_grads(weight, cot, width, interpret=False):
    cols, rows, pair_width = cot.shape
    return pl.pallas_call(
        functools.partial(outer_grad_kernel, width),
        grid=(cols // GRAD_TILE,),
        in_specs=[whole(weight.shape), pl.BlockSpec((GRAD_TILE, rows, pair_width), lambda j: (j, 0, 0))],
        out_specs=pl.BlockSpec((GRAD_TILE * width, width * rows), lambda j: (j, 0)),
        out_shape=jax.ShapeDtypeStruct((cols * width, width * rows), jnp.bfloat16),
        compiler_params=params(),
        cost_estimate=pl.CostEstimate(
            flops=2 * cols * rows * width * width * pair_width, bytes_accessed=18 * 2**20, transcendentals=0
        ),
        interpret=interpret,
        name="outer_grads",
    )(weight, cot)


def left_grads(came, grads, interpret=False):
    seqs, (depth, columns) = came.shape[0], grads.shape
    block = 512
    last = came.shape[1] // depth - 1
    return pl.pallas_call(
        functools.partial(left_kernel, 1.0 / seqs),
        grid=(columns // block,),
        in_specs=[
            pl.BlockSpec((seqs, depth), lambda n: (0, last)),
            pl.BlockSpec((depth, block), lambda n: (0, n)),
        ],
        out_specs=pl.BlockSpec((seqs, block), lambda n: (0, n)),
        out_shape=jax.ShapeDtypeStruct((seqs, columns), jnp.bfloat16),
        compiler_params=params(),
        cost_estimate=pl.CostEstimate(flops=2 * seqs * depth * columns, bytes_accessed=19 * 2**20, transcendentals=0),
        interpret=interpret,
        name="left_grads",
    )(came, grads)


def right_grads(came, other, grads, interpret=False):
    seqs, (rows, depth) = came.shape[0], grads.shape
    block = 256
    return pl.pallas_call(
        functools.partial(right_kernel, 1.0 / seqs),
        grid=(rows // block,),
        in_specs=[
            pl.BlockSpec((seqs, depth // 2), lambda n: (0, 0)),
            whole((seqs, depth // 2)),
            pl.BlockSpec((block, depth), lambda n: (n, 0)),
        ],
        out_specs=pl.BlockSpec((seqs, block), lambda n: (0, n)),
        out_shape=jax.ShapeDtypeStruct((seqs, rows), jnp.bfloat16),
        compiler_params=params(),
        cost_estimate=pl.CostEstimate(flops=2 * seqs * depth * rows, bytes_accessed=19 * 2**20, transcendentals=0),
        interpret=interpret,
        name="right_grads",
    )(came, other, grads)


def forward(came, other, weight_t, bias, cot, width, interpret=False):
    seqs, cols, rows, pair_width = came.shape[0], cot.shape[0], cot.shape[1], cot.shape[2]
    flops = 2 * cols * rows * width * width * (2 * pair_width + seqs)
    first = other.shape[1] // (TILE * width)
    return pl.pallas_call(
        functools.partial(forward_kernel, 1.0 / seqs, width),
        grid=(cols // TILE,),
        in_specs=[
            pl.BlockSpec(other.shape, lambda j: (0, 0)),
            whole(other.shape),
            pl.BlockSpec((seqs, TILE * width), lambda j: (0, first + j)),
            whole(weight_t.shape),
            whole(bias.shape),
            pl.BlockSpec((TILE, rows, pair_width), lambda j: (j, 0, 0)),
        ],
        out_specs=[
            pl.BlockSpec((TILE, rows, pair_width), lambda j: (j, 0, 0)),
            whole((width * width, pair_width)),
        ],
        out_shape=[
            jax.ShapeDtypeStruct((cols, rows, pair_width), jnp.bfloat16),
            jax.ShapeDtypeStruct((width * width, pair_width), jnp.float32),
        ],
        scratch_shapes=[pltpu.VMEM((width * width, TILE * rows), jnp.bfloat16)],
        compiler_params=params(),
        cost_estimate=pl.CostEstimate(flops=flops, bytes_accessed=8 * 2**20, transcendentals=0),
        interpret=interpret,
        name="forward",
    )(came, other, came, weight_t, bias, cot)


def exchange(blocks):
    return lax.all_to_all(blocks, BOTH, 0, 0, tiled=True)


def swap_cores(values):
    return lax.ppermute(values, "col", [(i, i ^ 1) for i in range(lax.axis_size("col"))])


def own_first(values, core):
    half = values.shape[0] // CORES
    return jnp.where(core == 0, values, jnp.concatenate([values[half:], values[:half]], axis=0))


def sum_all(values):
    devices = lax.axis_size(BOTH)

    def partner(part, mask):
        return lax.ppermute(part, BOTH, [(i, i ^ mask) for i in range(devices)])

    core = lax.axis_index("col") % CORES
    half = values.shape[0] // CORES
    halves = own_first(values, core)
    part = halves[:half] + partner(halves[half:], 1)
    mask = CORES
    while mask < devices:
        if 4 * mask <= devices:
            others = [partner(part, mask), partner(part, 2 * mask), partner(part, 3 * mask)]
            part = (part + others[0]) + (others[1] + others[2])
        else:
            part = part + partner(part, mask)
        mask *= 4
    return own_first(jnp.concatenate([part, partner(part, 1)], axis=0), core)


def body(alignment, left_weight, right_weight, out_weight, out_bias, pair_cotangent):
    row_count = lax.axis_size("row")
    col_count = lax.axis_size("col")
    devices = row_count * col_count
    local, residues, model_width = alignment.shape
    width = left_weight.shape[1]
    row_block, col_block, pair_width = pair_cotangent.shape
    seqs = local * devices

    normed, inv_sigma = layer_norm(alignment.astype(jnp.float32))
    normed_low = normed.astype(jnp.bfloat16)
    left = jnp.einsum("src,ch->shr", normed_low, left_weight, preferred_element_type=jnp.float32).astype(
        jnp.bfloat16
    )
    right = jnp.einsum("src,ch->srh", normed_low, right_weight, preferred_element_type=jnp.float32).astype(
        jnp.bfloat16
    )
    chips = col_count // CORES
    core = lax.axis_index("col") % CORES
    panel = row_block * width // CORES
    left_out = left.reshape(local, CORES, width // CORES, row_count, row_block).transpose(3, 1, 0, 2, 4)
    left_out = left_out.reshape(row_count, 1, CORES, local, panel)
    right_out = right.reshape(local, chips, CORES, col_block * width).transpose(1, 2, 0, 3)[None]
    shape = (row_count, chips, CORES, local)
    sent = jnp.concatenate(
        [jnp.broadcast_to(left_out, shape + (panel,)), jnp.broadcast_to(right_out, shape + right_out.shape[4:])], axis=4
    )
    columns = sent.shape[4]
    cot = pair_cotangent.transpose(1, 0, 2)
    bias = out_bias.astype(jnp.float32).reshape(1, pair_width)
    weight = own_first(out_weight, core)
    came = exchange(sent.reshape(devices, local, columns))
    came, outer_grad = lax.optimization_barrier((came, outer_grads(weight, cot, width)))
    came = came.reshape(seqs, columns)
    left_other = swap_cores(came[:, :panel])
    left_part = left_grads(came, outer_grad)
    left_other, left_part = lax.optimization_barrier((left_other, left_part))
    left_share = swap_cores(left_part[:, panel:])
    right_part = right_grads(came, left_other, outer_grad)
    left_pair = (left_part[:, :panel].astype(jnp.float32) + left_share.astype(jnp.float32)).astype(jnp.bfloat16)
    sent = jnp.concatenate([left_pair, right_part], axis=1).reshape(devices, local, columns)
    sent, left_other = lax.optimization_barrier((sent, left_other))
    back = exchange(sent).reshape(seqs, columns)
    update, weight_term = forward(came, left_other, weight.T, bias, cot, width)
    pair_update = update.transpose(1, 0, 2)
    share = weight_term.shape[0] // devices
    weight_parts = exchange(own_first(weight_term, core).reshape(devices, share, pair_width))

    place = np.indices((row_count, chips, CORES, local)).reshape(4, -1)
    left_place = (place[3] * row_count + place[0]) * CORES + place[2]
    right_place = (place[3] * chips + place[1]) * CORES + place[2]
    left_rows, right_rows = local * row_count * CORES, local * chips * CORES
    left_pick = jnp.asarray(np.arange(left_rows)[:, None] == left_place[None], dtype=jnp.bfloat16)
    right_pick = jnp.asarray(np.arange(right_rows)[:, None] == right_place[None], dtype=jnp.bfloat16)
    left_grad = jnp.dot(left_pick, back[:, :panel], preferred_element_type=jnp.float32).astype(jnp.bfloat16)
    right_grad = jnp.dot(right_pick, back[:, panel:], preferred_element_type=jnp.float32).astype(jnp.bfloat16)
    left_grad = left_grad.reshape(local, row_count, width, row_block).transpose(0, 2, 1, 3)
    left_grad = left_grad.reshape(local, width, residues)
    right_grad = right_grad.reshape(local, residues, width)
    left_wgrad = jnp.einsum("src,shr->ch", normed_low, left_grad, preferred_element_type=jnp.float32)
    right_wgrad = jnp.einsum("src,srh->ch", normed_low, right_grad, preferred_element_type=jnp.float32)
    wgrads = sum_all(jnp.concatenate([left_wgrad, right_wgrad], axis=1).reshape(-1, 128))
    wgrads, weight_parts = lax.optimization_barrier((wgrads, weight_parts))
    grad_out_weight = jnp.sum(weight_parts, axis=0)
    wgrads = wgrads.reshape(model_width, 2 * width)

    upstream = jnp.einsum("shr,ch->src", left_grad, left_weight, preferred_element_type=jnp.float32)
    upstream += jnp.einsum("srh,ch->src", right_grad, right_weight, preferred_element_type=jnp.float32)
    grad_alignment = norm_backward(upstream, normed, inv_sigma).astype(jnp.bfloat16)
    return (pair_update, grad_alignment, grad_out_weight, wgrads[:, :width], wgrads[:, width:])


def solution(mesh):
    return jax.shard_map(
        body,
        mesh=mesh,
        in_specs=(P(("row", "col"), None, None), P(), P(), P(), P(), P("row", "col", None)),
        out_specs=(
            P("row", "col", None),
            P(("row", "col"), None, None),
            P(("row", "col"), None),
            P(),
            P(),
        ),
        check_vma=False,
    )
```

```python
import functools

import jax
import jax.numpy as jnp
import numpy as np
from jax import lax
from jax.experimental import pallas as pl
from jax.experimental.pallas import tpu as pltpu
from jax.sharding import PartitionSpec as P

BOTH = ("row", "col")
TILE = 16
GRAD_TILE = 8
STREAMS = 4
CORES = 2
VMEM_BYTES = 48 * 1024 * 1024
NT = (((1,), (1,)), ((), ()))


def layer_norm(values):
    centered = values - jnp.mean(values, axis=-1, keepdims=True)
    inv_sigma = lax.rsqrt(jnp.mean(centered * centered, axis=-1, keepdims=True) + 1e-05)
    return (centered * inv_sigma, inv_sigma)


def norm_backward(upstream, normed, inv_sigma):
    first = jnp.mean(upstream, axis=-1, keepdims=True)
    second = jnp.mean(upstream * normed, axis=-1, keepdims=True)
    return inv_sigma * (upstream - first - normed * second)


def outer_grad_kernel(width, weight_ref, cot_ref, grad_ref):
    tile, rows, pair_width = cot_ref.shape
    flat = cot_ref[...].reshape(tile * rows, pair_width)
    step = 2
    for j in range(0, tile, step):
        grads = lax.dot_general(
            weight_ref[...], flat[j * rows:(j + step) * rows], NT, preferred_element_type=jnp.float32
        ).astype(jnp.bfloat16)
        for k in range(step):
            for c in range(width):
                grad_ref[(j + k) * width:(j + k + 1) * width, c * rows:(c + 1) * rows] = grads[
                    c * width:(c + 1) * width, k * rows:(k + 1) * rows
                ]


def left_kernel(inverse, right_ref, *refs):
    grad_refs, out_ref = refs[:-1], refs[-1]
    depth = grad_refs[0].shape[0]
    grads = 0.0
    for k, grad_ref in enumerate(grad_refs):
        grads += jnp.dot(
            right_ref[:, k * depth:(k + 1) * depth], grad_ref[...], preferred_element_type=jnp.float32
        )
    out_ref[...] = (grads * inverse).astype(out_ref.dtype)


def right_kernel(inverse, own_ref, other_ref, *refs):
    grad_refs, out_ref = refs[:-1], refs[-1]
    depth = grad_refs[0].shape[1]
    each = own_ref.shape[1] // depth
    grads = 0.0
    for k, grad_ref in enumerate(grad_refs):
        half_ref, first = (own_ref, k) if k < each else (other_ref, k - each)
        grads += lax.dot_general(
            half_ref[:, first * depth:(first + 1) * depth], grad_ref[...], NT, preferred_element_type=jnp.float32
        )
    out_ref[...] = (grads * inverse).astype(out_ref.dtype)


def forward_kernel(
    inverse, width, core_ref, own_ref, other_ref, right_ref, weight_t_ref, bias_ref, cot_ref, update_ref, wgrad_ref, outer_ref
):
    tile, rows, pair_width = cot_ref.shape
    right_t = right_ref[...].T
    step = 2
    for c in range(0, width, step):
        half_ref, first = (own_ref, c) if c < width // 2 else (other_ref, c - width // 2)
        outer = jnp.dot(
            right_t, half_ref[:, first * rows:(first + step) * rows], preferred_element_type=jnp.float32
        ).astype(jnp.bfloat16)
        for k in range(step):
            for j in range(tile):
                outer_ref[(c + k) * width:(c + k + 1) * width, j * rows:(j + 1) * rows] = outer[
                    j * width:(j + 1) * width, k * rows:(k + 1) * rows
                ]
    for j in range(0, tile, step):
        update = jnp.dot(
            weight_t_ref[...], outer_ref[:, j * rows:(j + step) * rows], preferred_element_type=jnp.float32
        )
        for k in range(step):
            one = update[:, k * rows:(k + 1) * rows].T
            update_ref[j + k] = (one * inverse + bias_ref[...]).astype(update_ref.dtype)

    @pl.when(pl.program_id(0) == 0)
    def _():
        wgrad_ref[...] = jnp.zeros_like(wgrad_ref)

    flat = cot_ref[...].reshape(tile * rows, pair_width)
    half = wgrad_ref.shape[0] // CORES
    for k in range(CORES):
        place = pl.ds(pl.multiple_of((core_ref[0] ^ k) * half, half), half)
        wgrad_ref[place] += inverse * jnp.dot(
            outer_ref[k * half:(k + 1) * half], flat, preferred_element_type=jnp.float32
        )


def whole(shape):
    return pl.BlockSpec(shape, lambda j: (0,) * len(shape))


def params():
    return pltpu.CompilerParams(dimension_semantics=("arbitrary",), vmem_limit_bytes=VMEM_BYTES)


def outer_grads(weight, cot, width, interpret=False):
    cols, rows, pair_width = cot.shape
    return pl.pallas_call(
        functools.partial(outer_grad_kernel, width),
        grid=(cols // GRAD_TILE,),
        in_specs=[whole(weight.shape), pl.BlockSpec((GRAD_TILE, rows, pair_width), lambda j: (j, 0, 0))],
        out_specs=pl.BlockSpec((GRAD_TILE * width, width * rows), lambda j: (j, 0)),
        out_shape=jax.ShapeDtypeStruct((cols * width, width * rows), jnp.bfloat16),
        compiler_params=params(),
        cost_estimate=pl.CostEstimate(
            flops=2 * cols * rows * width * width * pair_width, bytes_accessed=18 * 2**20, transcendentals=0
        ),
        interpret=interpret,
        name="outer_grads",
    )(weight, cot)


def left_grads(came, grads, interpret=False):
    seqs, (depth, columns) = came.shape[0], grads.shape
    block = 512
    last = came.shape[1] // depth - 1
    return pl.pallas_call(
        functools.partial(left_kernel, 1.0 / seqs),
        grid=(columns // block,),
        in_specs=[
            pl.BlockSpec((seqs, depth), lambda n: (0, last)),
            *[pl.BlockSpec((depth // STREAMS, block), lambda n, k=k: (k, n)) for k in range(STREAMS)],
        ],
        out_specs=pl.BlockSpec((seqs, block), lambda n: (0, n)),
        out_shape=jax.ShapeDtypeStruct((seqs, columns), jnp.bfloat16),
        compiler_params=params(),
        cost_estimate=pl.CostEstimate(flops=2 * seqs * depth * columns, bytes_accessed=19 * 2**20, transcendentals=0),
        interpret=interpret,
        name="left_grads",
    )(came, *[grads] * STREAMS)


def right_grads(came, other, grads, interpret=False):
    seqs, (rows, depth) = came.shape[0], grads.shape
    block = 256
    return pl.pallas_call(
        functools.partial(right_kernel, 1.0 / seqs),
        grid=(rows // block,),
        in_specs=[
            pl.BlockSpec((seqs, depth // 2), lambda n: (0, 0)),
            whole((seqs, depth // 2)),
            *[pl.BlockSpec((block, depth // STREAMS), lambda n, k=k: (n, k)) for k in range(STREAMS)],
        ],
        out_specs=pl.BlockSpec((seqs, block), lambda n: (0, n)),
        out_shape=jax.ShapeDtypeStruct((seqs, rows), jnp.bfloat16),
        compiler_params=params(),
        cost_estimate=pl.CostEstimate(flops=2 * seqs * depth * rows, bytes_accessed=19 * 2**20, transcendentals=0),
        interpret=interpret,
        name="right_grads",
    )(came, other, *[grads] * STREAMS)


def forward(core, came, other, weight_t, bias, cot, width, interpret=False):
    seqs, cols, rows, pair_width = came.shape[0], cot.shape[0], cot.shape[1], cot.shape[2]
    flops = 2 * cols * rows * width * width * (2 * pair_width + seqs)
    first = other.shape[1] // (TILE * width)
    return pl.pallas_call(
        functools.partial(forward_kernel, 1.0 / seqs, width),
        grid=(cols // TILE,),
        in_specs=[
            pl.BlockSpec(memory_space=pltpu.SMEM),
            pl.BlockSpec(other.shape, lambda j: (0, 0)),
            whole(other.shape),
            pl.BlockSpec((seqs, TILE * width), lambda j: (0, first + j)),
            whole(weight_t.shape),
            whole(bias.shape),
            pl.BlockSpec((TILE, rows, pair_width), lambda j: (j, 0, 0)),
        ],
        out_specs=[
            pl.BlockSpec((TILE, rows, pair_width), lambda j: (j, 0, 0)),
            whole((width * width, pair_width)),
        ],
        out_shape=[
            jax.ShapeDtypeStruct((cols, rows, pair_width), jnp.bfloat16),
            jax.ShapeDtypeStruct((width * width, pair_width), jnp.float32),
        ],
        scratch_shapes=[pltpu.VMEM((width * width, TILE * rows), jnp.bfloat16)],
        compiler_params=params(),
        cost_estimate=pl.CostEstimate(flops=flops, bytes_accessed=8 * 2**20, transcendentals=0),
        interpret=interpret,
        name="forward",
    )(core.reshape(1), came, other, came, weight_t, bias, cot)


def exchange(blocks):
    return lax.all_to_all(blocks, BOTH, 0, 0, tiled=True)


def swap_cores(values):
    return lax.ppermute(values, "col", [(i, i ^ 1) for i in range(lax.axis_size("col"))])


def own_first(values, core):
    half = values.shape[0] // CORES
    return jnp.where(core == 0, values, jnp.concatenate([values[half:], values[:half]], axis=0))


def permute_groups():
    devices = lax.axis_size(BOTH)
    groups = [(1, CORES)]
    while groups[-1][0] * groups[-1][1] < devices:
        low = groups[-1][0] * groups[-1][1]
        groups.append((low, min(4, devices // low)))
    return groups


def partner(part, mask):
    return lax.ppermute(part, BOTH, [(i, i ^ mask) for i in range(lax.axis_size(BOTH))])


def add_parts(parts):
    while len(parts) > 1:
        parts = [parts[k] + parts[k + 1] for k in range(0, len(parts), 2)]
    return parts[0]


def scatter_pieces(values, low, size):
    values = values.reshape((-1, size) + values.shape[1:])
    mine = lax.axis_index(BOTH) // low % size
    return [lax.dynamic_index_in_dim(values, mine ^ mask, 1, keepdims=False) for mask in range(size)]


def sum_scatter(values, groups):
    for low, size in groups:
        kept, *pieces = scatter_pieces(values, low, size)
        values = add_parts([kept] + [partner(piece, low * (k + 1)) for k, piece in enumerate(pieces)])
    return values


def sum_all(first, second, values, early):
    core = lax.axis_index(BOTH) % CORES
    own, other = jnp.where(core == 0, first, second), jnp.where(core == 0, second, first)
    part = own + partner(other, 1)
    rows, columns = part.shape
    for step, (low, size) in enumerate(permute_groups()):
        if step == 0:
            continue
        if step < early:
            part = add_parts([part] + [partner(part, low * mask) for mask in range(1, size)])
            continue
        share, lanes = values.shape[1:]
        pieces = [piece.reshape(-1, lanes) for piece in scatter_pieces(values, low, size)]
        used = pieces[0].shape[0]
        pieces = [jnp.pad(piece, ((0, rows - used), (0, 0))) for piece in pieces]
        sent = [jnp.concatenate([part, piece], axis=1) for piece in pieces]
        both = add_parts(sent[:1] + [partner(sent[mask], low * mask) for mask in range(1, size)])
        part, values = both[:, :columns], both[:used, columns:].reshape(-1, share, lanes)
    other = partner(part, 1)
    return jnp.where(core == 0, part, other), jnp.where(core == 0, other, part), values


def body(alignment, left_weight, right_weight, out_weight, out_bias, pair_cotangent):
    row_count = lax.axis_size("row")
    col_count = lax.axis_size("col")
    devices = row_count * col_count
    local, residues, model_width = alignment.shape
    width = left_weight.shape[1]
    row_block, col_block, pair_width = pair_cotangent.shape
    seqs = local * devices

    normed, inv_sigma = layer_norm(alignment.astype(jnp.float32))
    normed_low = normed.astype(jnp.bfloat16)
    left = jnp.einsum("src,ch->shr", normed_low, left_weight, preferred_element_type=jnp.float32).astype(
        jnp.bfloat16
    )
    right = jnp.einsum("src,ch->srh", normed_low, right_weight, preferred_element_type=jnp.float32).astype(
        jnp.bfloat16
    )
    chips = col_count // CORES
    core = lax.axis_index("col") % CORES
    panel = row_block * width // CORES
    left_out = left.reshape(local, CORES, width // CORES, row_count, row_block).transpose(3, 1, 0, 2, 4)
    left_out = left_out.reshape(row_count, 1, CORES, local, panel)
    right_out = right.reshape(local, chips, CORES, col_block * width).transpose(1, 2, 0, 3)[None]
    shape = (row_count, chips, CORES, local)
    sent = jnp.concatenate(
        [jnp.broadcast_to(left_out, shape + (panel,)), jnp.broadcast_to(right_out, shape + right_out.shape[4:])], axis=4
    )
    columns = sent.shape[4]
    cot = pair_cotangent.transpose(1, 0, 2)
    bias = out_bias.astype(jnp.float32).reshape(1, pair_width)
    weight = own_first(out_weight, core)
    came = exchange(sent.reshape(devices, local, columns))
    came, outer_grad = lax.optimization_barrier((came, outer_grads(weight, cot, width)))
    came = came.reshape(seqs, columns)
    left_other = swap_cores(came[:, :panel])
    left_part = left_grads(came, outer_grad)
    left_other, left_part = lax.optimization_barrier((left_other, left_part))
    left_share = swap_cores(left_part[:, panel:])
    right_part = right_grads(came, left_other, outer_grad)
    left_pair = (left_part[:, :panel].astype(jnp.float32) + left_share.astype(jnp.float32)).astype(jnp.bfloat16)
    sent = jnp.concatenate([left_pair, right_part], axis=1).reshape(devices, local, columns)
    sent, left_other = lax.optimization_barrier((sent, left_other))
    back = exchange(sent).reshape(seqs, columns)
    update, weight_term = forward(core, came, left_other, weight.T, bias, cot, width)
    pair_update = update.transpose(1, 0, 2)
    early = 2
    weight_term = weight_term.reshape(devices, -1, pair_width)
    weight_term = sum_scatter(weight_term, permute_groups()[:early])
    back, weight_term = lax.optimization_barrier((back, weight_term))

    place = np.indices((row_count, chips, CORES, local)).reshape(4, -1)
    left_place = (place[3] * row_count + place[0]) * CORES + place[2]
    right_place = (place[3] * chips + place[1]) * CORES + place[2]
    left_rows, right_rows = local * row_count * CORES, local * chips * CORES
    left_pick = jnp.asarray(np.arange(left_rows)[:, None] == left_place[None], dtype=jnp.bfloat16)
    right_pick = jnp.asarray(np.arange(right_rows)[:, None] == right_place[None], dtype=jnp.bfloat16)
    left_grad = jnp.dot(left_pick, back[:, :panel], preferred_element_type=jnp.float32).astype(jnp.bfloat16)
    right_grad = jnp.dot(right_pick, back[:, panel:], preferred_element_type=jnp.float32).astype(jnp.bfloat16)
    left_grad = left_grad.reshape(local, row_count, width, row_block).transpose(0, 2, 1, 3)
    left_grad = left_grad.reshape(local, width, residues)
    right_grad = right_grad.reshape(local, residues, width)
    left_wgrad = jnp.einsum("src,shr->hc", normed_low, left_grad, preferred_element_type=jnp.float32)
    right_wgrad = jnp.einsum("src,srh->hc", normed_low, right_grad, preferred_element_type=jnp.float32)
    left_wgrad, right_wgrad, weight_term = sum_all(left_wgrad, right_wgrad, weight_term, early)
    grad_out_weight = weight_term.reshape(-1, pair_width)

    upstream = jnp.einsum("shr,ch->src", left_grad, left_weight, preferred_element_type=jnp.float32)
    upstream += jnp.einsum("srh,ch->src", right_grad, right_weight, preferred_element_type=jnp.float32)
    grad_alignment = norm_backward(upstream, normed, inv_sigma).astype(jnp.bfloat16)
    return (pair_update, grad_alignment, grad_out_weight, left_wgrad.T, right_wgrad.T)


def solution(mesh):
    return jax.shard_map(
        body,
        mesh=mesh,
        in_specs=(P(("row", "col"), None, None), P(), P(), P(), P(), P("row", "col", None)),
        out_specs=(
            P("row", "col", None),
            P(("row", "col"), None, None),
            P(("row", "col"), None),
            P(),
            P(),
        ),
        check_vma=False,
    )
```

```python
import functools

import jax
import jax.numpy as jnp
import numpy as np
from jax import lax
from jax.experimental import pallas as pl
from jax.experimental.pallas import tpu as pltpu
from jax.sharding import PartitionSpec as P

BOTH = ("row", "col")
TILE = 16
GRAD_TILE = 8
CORES = 2
VMEM_BYTES = 48 * 1024 * 1024
NT = (((1,), (1,)), ((), ()))


def layer_norm(values):
    centered = values - jnp.mean(values, axis=-1, keepdims=True)
    inv_sigma = lax.rsqrt(jnp.mean(centered * centered, axis=-1, keepdims=True) + 1e-05)
    return (centered * inv_sigma, inv_sigma)


def norm_backward(upstream, normed, inv_sigma):
    first = jnp.mean(upstream, axis=-1, keepdims=True)
    second = jnp.mean(upstream * normed, axis=-1, keepdims=True)
    return inv_sigma * (upstream - first - normed * second)


def outer_grad_kernel(width, weight_ref, cot_ref, grad_ref):
    tile, rows, pair_width = cot_ref.shape
    flat = cot_ref[...].reshape(tile * rows, pair_width)
    step = 2
    for j in range(0, tile, step):
        grads = lax.dot_general(
            weight_ref[...], flat[j * rows:(j + step) * rows], NT, preferred_element_type=jnp.float32
        ).astype(jnp.bfloat16)
        for k in range(step):
            for c in range(width):
                grad_ref[(j + k) * width:(j + k + 1) * width, c * rows:(c + 1) * rows] = grads[
                    c * width:(c + 1) * width, k * rows:(k + 1) * rows
                ]


def left_kernel(inverse, right_ref, own_ref, grad_ref, out_ref, partial_ref):
    step = pl.program_id(0)
    grads = jnp.dot(right_ref[...], grad_ref[...], preferred_element_type=jnp.float32)
    out_ref[...] = (grads * inverse).astype(out_ref.dtype)

    @pl.when(step == 0)
    def _():
        partial_ref[...] = lax.dot_general(own_ref[...], grad_ref[...], NT, preferred_element_type=jnp.float32)

    @pl.when((step > 0) & (step < pl.num_programs(0) // CORES))
    def _():
        partial_ref[...] += lax.dot_general(own_ref[...], grad_ref[...], NT, preferred_element_type=jnp.float32)


def right_kernel(inverse, other_ref, partial_ref, grad_ref, out_ref):
    grads = lax.dot_general(other_ref[...], grad_ref[...], NT, preferred_element_type=jnp.float32)
    out_ref[...] = ((partial_ref[...] + grads) * inverse).astype(out_ref.dtype)


def pack_kernel(left_ref, right_ref, out_ref, sems):
    rows, chips = out_ref.shape[:2]
    panel = left_ref.shape[-1]
    copies = [
        pltpu.make_async_copy(right_ref, out_ref.at[k, :, :, :, pl.ds(panel, right_ref.shape[-1])], sems.at[k])
        for k in range(rows)
    ]
    copies += [
        pltpu.make_async_copy(left_ref, out_ref.at[:, k, :, :, pl.ds(0, panel)], sems.at[rows + k])
        for k in range(chips)
    ]
    for copy in copies:
        copy.start()
    for copy in copies:
        copy.wait()


def forward_kernel(
    inverse, width, core_ref, own_ref, other_ref, right_ref, weight_t_ref, bias_ref, cot_ref, update_ref, wgrad_ref, outer_ref
):
    tile, rows, pair_width = cot_ref.shape
    right_t = right_ref[...].T
    step = 2
    for c in range(0, width, step):
        half_ref, first = (own_ref, c) if c < width // 2 else (other_ref, c - width // 2)
        outer = jnp.dot(
            right_t, half_ref[:, first * rows:(first + step) * rows], preferred_element_type=jnp.float32
        ).astype(jnp.bfloat16)
        for k in range(step):
            for j in range(tile):
                outer_ref[(c + k) * width:(c + k + 1) * width, j * rows:(j + 1) * rows] = outer[
                    j * width:(j + 1) * width, k * rows:(k + 1) * rows
                ]
    for j in range(0, tile, step):
        update = jnp.dot(
            weight_t_ref[...], outer_ref[:, j * rows:(j + step) * rows], preferred_element_type=jnp.float32
        )
        for k in range(step):
            one = update[:, k * rows:(k + 1) * rows].T
            update_ref[j + k] = (one * inverse + bias_ref[...]).astype(update_ref.dtype)

    @pl.when(pl.program_id(0) == 0)
    def _():
        wgrad_ref[...] = jnp.zeros_like(wgrad_ref)

    flat = cot_ref[...].reshape(tile * rows, pair_width)
    half = wgrad_ref.shape[0] // CORES
    for k in range(CORES):
        place = pl.ds(pl.multiple_of((core_ref[0] ^ k) * half, half), half)
        wgrad_ref[place] += inverse * jnp.dot(
            outer_ref[k * half:(k + 1) * half], flat, preferred_element_type=jnp.float32
        )


def whole(shape):
    return pl.BlockSpec(shape, lambda j: (0,) * len(shape))


def params():
    return pltpu.CompilerParams(dimension_semantics=("arbitrary",), vmem_limit_bytes=VMEM_BYTES)


def outer_grads(weight, cot, width, interpret=False):
    cols, rows, pair_width = cot.shape
    return pl.pallas_call(
        functools.partial(outer_grad_kernel, width),
        grid=(cols // GRAD_TILE,),
        in_specs=[whole(weight.shape), pl.BlockSpec((GRAD_TILE, rows, pair_width), lambda j: (j, 0, 0))],
        out_specs=pl.BlockSpec((GRAD_TILE * width, width * rows), lambda j: (j, 0)),
        out_shape=jax.ShapeDtypeStruct((cols * width, width * rows), jnp.bfloat16),
        compiler_params=params(),
        cost_estimate=pl.CostEstimate(
            flops=2 * cols * rows * width * width * pair_width, bytes_accessed=18 * 2**20, transcendentals=0
        ),
        interpret=interpret,
        name="outer_grads",
    )(weight, cot)


def left_grads(came, grads, interpret=False):
    seqs, (depth, columns) = came.shape[0], grads.shape
    block = 512
    own = columns // CORES // block
    last = came.shape[1] // depth - 1
    return pl.pallas_call(
        functools.partial(left_kernel, 1.0 / seqs),
        grid=(columns // block,),
        in_specs=[
            pl.BlockSpec((seqs, depth), lambda n: (0, last)),
            pl.BlockSpec((seqs, block), lambda n: (0, jnp.minimum(n, own - 1))),
            pl.BlockSpec((depth, block), lambda n: (0, n)),
        ],
        out_specs=[pl.BlockSpec((seqs, block), lambda n: (0, n)), whole((seqs, depth))],
        out_shape=[
            jax.ShapeDtypeStruct((seqs, columns), jnp.bfloat16),
            jax.ShapeDtypeStruct((seqs, depth), jnp.float32),
        ],
        compiler_params=params(),
        cost_estimate=pl.CostEstimate(flops=3 * seqs * depth * columns, bytes_accessed=21 * 2**20, transcendentals=0),
        interpret=interpret,
        name="left_grads",
    )(came, came, grads)


def right_grads(other, partial, grads, interpret=False):
    seqs, (rows, depth) = other.shape[0], grads.shape
    block = 256
    return pl.pallas_call(
        functools.partial(right_kernel, 1.0 / seqs),
        grid=(rows // block,),
        in_specs=[
            whole(other.shape),
            pl.BlockSpec((seqs, block), lambda n: (0, n)),
            pl.BlockSpec((block, depth // CORES), lambda n: (n, 1)),
        ],
        out_specs=pl.BlockSpec((seqs, block), lambda n: (0, n)),
        out_shape=jax.ShapeDtypeStruct((seqs, rows), jnp.bfloat16),
        compiler_params=params(),
        cost_estimate=pl.CostEstimate(flops=seqs * depth * rows, bytes_accessed=12 * 2**20, transcendentals=0),
        interpret=interpret,
        name="right_grads",
    )(other, partial, grads)


def pack(left, right, interpret=False):
    shape = (left.shape[0],) + right.shape[:-1] + (left.shape[-1] + right.shape[-1],)
    return pl.pallas_call(
        pack_kernel,
        in_specs=[pl.BlockSpec(memory_space=pltpu.VMEM)] * 2,
        out_specs=pl.BlockSpec(memory_space=pl.ANY),
        out_shape=jax.ShapeDtypeStruct(shape, left.dtype),
        scratch_shapes=[pltpu.SemaphoreType.DMA((shape[0] + shape[1],))],
        cost_estimate=pl.CostEstimate(flops=0, bytes_accessed=2 * 2**20, transcendentals=0),
        interpret=interpret,
        name="pack",
    )(left, right)


def forward(core, came, other, weight_t, bias, cot, width, interpret=False):
    seqs, cols, rows, pair_width = came.shape[0], cot.shape[0], cot.shape[1], cot.shape[2]
    flops = 2 * cols * rows * width * width * (2 * pair_width + seqs)
    first = other.shape[1] // (TILE * width)
    return pl.pallas_call(
        functools.partial(forward_kernel, 1.0 / seqs, width),
        grid=(cols // TILE,),
        in_specs=[
            pl.BlockSpec(memory_space=pltpu.SMEM),
            pl.BlockSpec(other.shape, lambda j: (0, 0)),
            whole(other.shape),
            pl.BlockSpec((seqs, TILE * width), lambda j: (0, first + j)),
            whole(weight_t.shape),
            whole(bias.shape),
            pl.BlockSpec((TILE, rows, pair_width), lambda j: (j, 0, 0)),
        ],
        out_specs=[
            pl.BlockSpec((TILE, rows, pair_width), lambda j: (j, 0, 0)),
            whole((width * width, pair_width)),
        ],
        out_shape=[
            jax.ShapeDtypeStruct((cols, rows, pair_width), jnp.bfloat16),
            jax.ShapeDtypeStruct((width * width, pair_width), jnp.float32),
        ],
        scratch_shapes=[pltpu.VMEM((width * width, TILE * rows), jnp.bfloat16)],
        compiler_params=params(),
        cost_estimate=pl.CostEstimate(flops=flops, bytes_accessed=8 * 2**20, transcendentals=0),
        interpret=interpret,
        name="forward",
    )(core.reshape(1), came, other, came, weight_t, bias, cot)


def exchange(blocks):
    return lax.all_to_all(blocks, BOTH, 0, 0, tiled=True)


def swap_cores(values):
    return lax.ppermute(values, "col", [(i, i ^ 1) for i in range(lax.axis_size("col"))])


def own_first(values, core):
    half = values.shape[0] // CORES
    return jnp.where(core == 0, values, jnp.concatenate([values[half:], values[:half]], axis=0))


def permute_groups():
    devices = lax.axis_size(BOTH)
    groups = [(1, CORES)]
    while groups[-1][0] * groups[-1][1] < devices:
        low = groups[-1][0] * groups[-1][1]
        groups.append((low, min(4, devices // low)))
    return groups


def partner(part, mask):
    return lax.ppermute(part, BOTH, [(i, i ^ mask) for i in range(lax.axis_size(BOTH))])


def add_parts(parts):
    while len(parts) > 1:
        parts = [parts[k] + parts[k + 1] for k in range(0, len(parts), 2)]
    return parts[0]


def scatter_pieces(values, low, size):
    values = values.reshape((-1, size) + values.shape[1:])
    mine = lax.axis_index(BOTH) // low % size
    return [lax.dynamic_index_in_dim(values, mine ^ mask, 1, keepdims=False) for mask in range(size)]


def sum_scatter(values, groups):
    for low, size in groups:
        kept, *pieces = scatter_pieces(values, low, size)
        values = add_parts([kept] + [partner(piece, low * (k + 1)) for k, piece in enumerate(pieces)])
    return values


def sum_all(first, second, values, early):
    core = lax.axis_index(BOTH) % CORES
    own, other = jnp.where(core == 0, first, second), jnp.where(core == 0, second, first)
    part = own + partner(other, 1)
    rows, columns = part.shape
    for step, (low, size) in enumerate(permute_groups()):
        if step == 0:
            continue
        if step < early:
            part = add_parts([part] + [partner(part, low * mask) for mask in range(1, size)])
            continue
        share, lanes = values.shape[1:]
        pieces = [piece.reshape(-1, lanes) for piece in scatter_pieces(values, low, size)]
        used = pieces[0].shape[0]
        pieces = [jnp.pad(piece, ((0, rows - used), (0, 0))) for piece in pieces]
        sent = [jnp.concatenate([part, piece], axis=1) for piece in pieces]
        both = add_parts(sent[:1] + [partner(sent[mask], low * mask) for mask in range(1, size)])
        part, values = both[:, :columns], both[:used, columns:].reshape(-1, share, lanes)
    other = partner(part, 1)
    return jnp.where(core == 0, part, other), jnp.where(core == 0, other, part), values


def body(alignment, left_weight, right_weight, out_weight, out_bias, pair_cotangent):
    row_count = lax.axis_size("row")
    col_count = lax.axis_size("col")
    devices = row_count * col_count
    local, residues, model_width = alignment.shape
    width = left_weight.shape[1]
    row_block, col_block, pair_width = pair_cotangent.shape
    seqs = local * devices

    normed, inv_sigma = layer_norm(alignment.astype(jnp.float32))
    normed_low = normed.astype(jnp.bfloat16)
    left = jnp.einsum("src,ch->shr", normed_low, left_weight, preferred_element_type=jnp.float32).astype(
        jnp.bfloat16
    )
    right = jnp.einsum("src,ch->srh", normed_low, right_weight, preferred_element_type=jnp.float32).astype(
        jnp.bfloat16
    )
    chips = col_count // CORES
    core = lax.axis_index("col") % CORES
    panel = row_block * width // CORES
    left_out = left.reshape(local, CORES, width // CORES, row_count, row_block).transpose(3, 1, 0, 2, 4)
    left_out = left_out.reshape(row_count, CORES, local, panel)
    right_out = right.reshape(local, chips, CORES, col_block * width).transpose(1, 2, 0, 3)
    sent = pack(left_out, right_out)
    columns = sent.shape[4]
    cot = pair_cotangent.transpose(1, 0, 2)
    bias = out_bias.astype(jnp.float32).reshape(1, pair_width)
    weight = own_first(out_weight, core)
    came = exchange(sent.reshape(devices, local, columns))
    came, outer_grad = lax.optimization_barrier((came, outer_grads(weight, cot, width)))
    came = came.reshape(seqs, columns)
    left_other = swap_cores(came[:, :panel])
    left_part, right_partial = left_grads(came, outer_grad)
    left_other, left_part = lax.optimization_barrier((left_other, left_part))
    left_share = swap_cores(left_part[:, panel:])
    right_part = right_grads(left_other, right_partial, outer_grad)
    left_pair = (left_part[:, :panel].astype(jnp.float32) + left_share.astype(jnp.float32)).astype(jnp.bfloat16)
    sent = jnp.concatenate([left_pair, right_part], axis=1).reshape(devices, local, columns)
    sent, left_other = lax.optimization_barrier((sent, left_other))
    back = exchange(sent).reshape(seqs, columns)
    update, weight_term = forward(core, came, left_other, weight.T, bias, cot, width)
    pair_update = update.transpose(1, 0, 2)
    early = 2
    weight_term = weight_term.reshape(devices, -1, pair_width)
    weight_term = sum_scatter(weight_term, permute_groups()[:early])
    back, weight_term = lax.optimization_barrier((back, weight_term))

    place = np.indices((row_count, chips, CORES, local)).reshape(4, -1)
    left_place = (place[3] * row_count + place[0]) * CORES + place[2]
    right_place = (place[3] * chips + place[1]) * CORES + place[2]
    left_rows, right_rows = local * row_count * CORES, local * chips * CORES
    left_pick = jnp.asarray(np.arange(left_rows)[:, None] == left_place[None], dtype=jnp.bfloat16)
    right_pick = jnp.asarray(np.arange(right_rows)[:, None] == right_place[None], dtype=jnp.bfloat16)
    left_grad = jnp.dot(left_pick, back[:, :panel], preferred_element_type=jnp.float32).astype(jnp.bfloat16)
    right_grad = jnp.dot(right_pick, back[:, panel:], preferred_element_type=jnp.float32).astype(jnp.bfloat16)
    left_grad = left_grad.reshape(local, row_count, width, row_block).transpose(0, 2, 1, 3)
    left_grad = left_grad.reshape(local, width, residues)
    right_grad = right_grad.reshape(local, residues, width)
    left_wgrad = jnp.einsum("src,shr->hc", normed_low, left_grad, preferred_element_type=jnp.float32)
    right_wgrad = jnp.einsum("src,srh->hc", normed_low, right_grad, preferred_element_type=jnp.float32)
    left_wgrad, right_wgrad, weight_term = sum_all(left_wgrad, right_wgrad, weight_term, early)
    grad_out_weight = weight_term.reshape(-1, pair_width)

    upstream = jnp.einsum("shr,ch->src", left_grad, left_weight, preferred_element_type=jnp.float32)
    upstream += jnp.einsum("srh,ch->src", right_grad, right_weight, preferred_element_type=jnp.float32)
    grad_alignment = norm_backward(upstream, normed, inv_sigma).astype(jnp.bfloat16)
    return (pair_update, grad_alignment, grad_out_weight, left_wgrad.T, right_wgrad.T)


def solution(mesh):
    return jax.shard_map(
        body,
        mesh=mesh,
        in_specs=(P(("row", "col"), None, None), P(), P(), P(), P(), P("row", "col", None)),
        out_specs=(
            P("row", "col", None),
            P(("row", "col"), None, None),
            P(("row", "col"), None),
            P(),
            P(),
        ),
        check_vma=False,
    )
```

```python
import functools

import jax
import jax.numpy as jnp
import numpy as np
from jax import lax
from jax.experimental import pallas as pl
from jax.experimental.pallas import tpu as pltpu
from jax.sharding import PartitionSpec as P

BOTH = ("row", "col")
TILE = 16
GRAD_TILE = 8
BLOCKS = 4
CORES = 2
VMEM_BYTES = 48 * 1024 * 1024
NT = (((1,), (1,)), ((), ()))


def layer_norm(values):
    centered = values - jnp.mean(values, axis=-1, keepdims=True)
    inv_sigma = lax.rsqrt(jnp.mean(centered * centered, axis=-1, keepdims=True) + 1e-05)
    return (centered * inv_sigma, inv_sigma)


def norm_backward(upstream, normed, inv_sigma):
    first = jnp.mean(upstream, axis=-1, keepdims=True)
    second = jnp.mean(upstream * normed, axis=-1, keepdims=True)
    return inv_sigma * (upstream - first - normed * second)


def outer_grad_kernel(width, weight_ref, cot_ref, grad_ref):
    tile, rows, pair_width = cot_ref.shape
    flat = cot_ref[...].reshape(tile * rows, pair_width)
    step = 2
    for j in range(0, tile, step):
        grads = lax.dot_general(
            weight_ref[...], flat[j * rows:(j + step) * rows], NT, preferred_element_type=jnp.float32
        ).astype(jnp.bfloat16)
        for k in range(step):
            for c in range(width):
                grad_ref[(j + k) * width:(j + k + 1) * width, c * rows:(c + 1) * rows] = grads[
                    c * width:(c + 1) * width, k * rows:(k + 1) * rows
                ]


def left_kernel(inverse, came_ref, grad_ref, out_ref, partial_ref, panel_ref, held_ref, sems):
    blocks = sems.shape[0] - 1
    depth, columns = held_ref.shape
    block, half = columns // blocks, columns // CORES
    panel = pltpu.make_async_copy(came_ref, panel_ref, sems.at[blocks])
    panel.start()
    parts = [pl.ds(n * block, block) for n in range(blocks)]
    copies = [
        pltpu.make_async_copy(grad_ref.at[:, part], held_ref.at[:, part], sems.at[n]) for n, part in enumerate(parts)
    ]
    for copy in copies:
        copy.start()
    panel.wait()
    for n, part in enumerate(parts):
        if n == blocks // CORES:
            partial_ref[...] = lax.dot_general(
                panel_ref[:, :half], held_ref[:, :half], NT, preferred_element_type=jnp.float32
            )
        copies[n].wait()
        grads = jnp.dot(panel_ref[:, -depth:], held_ref[:, part], preferred_element_type=jnp.float32)
        out_ref[:, part] = (grads * inverse).astype(out_ref.dtype)


def right_kernel(inverse, other_ref, partial_ref, grad_ref, out_ref, held_ref, sems):
    blocks = sems.shape[0]
    rows, depth = held_ref.shape
    block = rows // blocks
    parts = [pl.ds(n * block, block) for n in range(blocks)]
    copies = [
        pltpu.make_async_copy(grad_ref.at[part, pl.ds(depth, depth)], held_ref.at[part], sems.at[n])
        for n, part in enumerate(parts)
    ]
    for copy in copies:
        copy.start()
    for n, part in enumerate(parts):
        copies[n].wait()
        grads = lax.dot_general(other_ref[...], held_ref[part], NT, preferred_element_type=jnp.float32)
        out_ref[:, part] = ((partial_ref[:, part] + grads) * inverse).astype(out_ref.dtype)


def pack_kernel(left_ref, right_ref, out_ref, sems):
    rows, chips = out_ref.shape[:2]
    panel = left_ref.shape[-1]
    copies = [
        pltpu.make_async_copy(right_ref, out_ref.at[k, :, :, :, pl.ds(panel, right_ref.shape[-1])], sems.at[k])
        for k in range(rows)
    ]
    copies += [
        pltpu.make_async_copy(left_ref, out_ref.at[:, k, :, :, pl.ds(0, panel)], sems.at[rows + k])
        for k in range(chips)
    ]
    for copy in copies:
        copy.start()
    for copy in copies:
        copy.wait()


def forward_kernel(
    inverse, width, core_ref, own_ref, other_ref, right_ref, weight_t_ref, bias_ref, cot_ref, update_ref, wgrad_ref, outer_ref
):
    tile, rows, pair_width = cot_ref.shape
    right_t = right_ref[...].T
    step = 2
    for c in range(0, width, step):
        half_ref, first = (own_ref, c) if c < width // 2 else (other_ref, c - width // 2)
        outer = jnp.dot(
            right_t, half_ref[:, first * rows:(first + step) * rows], preferred_element_type=jnp.float32
        ).astype(jnp.bfloat16)
        for k in range(step):
            for j in range(tile):
                outer_ref[(c + k) * width:(c + k + 1) * width, j * rows:(j + 1) * rows] = outer[
                    j * width:(j + 1) * width, k * rows:(k + 1) * rows
                ]
    for j in range(0, tile, step):
        update = jnp.dot(
            weight_t_ref[...], outer_ref[:, j * rows:(j + step) * rows], preferred_element_type=jnp.float32
        )
        for k in range(step):
            one = update[:, k * rows:(k + 1) * rows].T
            update_ref[j + k] = (one * inverse + bias_ref[...]).astype(update_ref.dtype)

    @pl.when(pl.program_id(0) == 0)
    def _():
        wgrad_ref[...] = jnp.zeros_like(wgrad_ref)

    flat = cot_ref[...].reshape(tile * rows, pair_width)
    half = wgrad_ref.shape[0] // CORES
    for k in range(CORES):
        place = pl.ds(pl.multiple_of((core_ref[0] ^ k) * half, half), half)
        wgrad_ref[place] += inverse * jnp.dot(
            outer_ref[k * half:(k + 1) * half], flat, preferred_element_type=jnp.float32
        )


def whole(shape):
    return pl.BlockSpec(shape, lambda j: (0,) * len(shape))


def params():
    return pltpu.CompilerParams(dimension_semantics=("arbitrary",), vmem_limit_bytes=VMEM_BYTES)


def outer_grads(weight, cot, width, interpret=False):
    cols, rows, pair_width = cot.shape
    return pl.pallas_call(
        functools.partial(outer_grad_kernel, width),
        grid=(cols // GRAD_TILE,),
        in_specs=[whole(weight.shape), pl.BlockSpec((GRAD_TILE, rows, pair_width), lambda j: (j, 0, 0))],
        out_specs=pl.BlockSpec((GRAD_TILE * width, width * rows), lambda j: (j, 0)),
        out_shape=jax.ShapeDtypeStruct((cols * width, width * rows), jnp.bfloat16),
        compiler_params=params(),
        cost_estimate=pl.CostEstimate(
            flops=2 * cols * rows * width * width * pair_width, bytes_accessed=18 * 2**20, transcendentals=0
        ),
        interpret=interpret,
        name="outer_grads",
    )(weight, cot)


def left_grads(came, grads, interpret=False):
    seqs, (depth, columns) = came.shape[0], grads.shape
    return pl.pallas_call(
        functools.partial(left_kernel, 1.0 / seqs),
        in_specs=[pl.BlockSpec(memory_space=pl.ANY)] * 2,
        out_specs=[pl.BlockSpec(memory_space=pltpu.VMEM)] * 2,
        out_shape=[
            jax.ShapeDtypeStruct((seqs, columns), jnp.bfloat16),
            jax.ShapeDtypeStruct((seqs, depth), jnp.float32),
        ],
        scratch_shapes=[
            pltpu.VMEM(came.shape, jnp.bfloat16),
            pltpu.VMEM(grads.shape, jnp.bfloat16),
            pltpu.SemaphoreType.DMA((BLOCKS + 1,)),
        ],
        compiler_params=pltpu.CompilerParams(vmem_limit_bytes=VMEM_BYTES),
        cost_estimate=pl.CostEstimate(flops=3 * seqs * depth * columns, bytes_accessed=21 * 2**20, transcendentals=0),
        interpret=interpret,
        name="left_grads",
    )(came, grads)


def right_grads(other, partial, grads, interpret=False):
    seqs, (rows, depth) = other.shape[0], grads.shape
    return pl.pallas_call(
        functools.partial(right_kernel, 1.0 / seqs),
        in_specs=[pl.BlockSpec(memory_space=pltpu.VMEM)] * 2 + [pl.BlockSpec(memory_space=pl.ANY)],
        out_specs=pl.BlockSpec(memory_space=pltpu.VMEM),
        out_shape=jax.ShapeDtypeStruct((seqs, rows), jnp.bfloat16),
        scratch_shapes=[pltpu.VMEM((rows, depth // CORES), jnp.bfloat16), pltpu.SemaphoreType.DMA((BLOCKS,))],
        compiler_params=pltpu.CompilerParams(vmem_limit_bytes=VMEM_BYTES),
        cost_estimate=pl.CostEstimate(flops=seqs * depth * rows, bytes_accessed=12 * 2**20, transcendentals=0),
        interpret=interpret,
        name="right_grads",
    )(other, partial, grads)


def pack(left, right, interpret=False):
    shape = (left.shape[0],) + right.shape[:-1] + (left.shape[-1] + right.shape[-1],)
    return pl.pallas_call(
        pack_kernel,
        in_specs=[pl.BlockSpec(memory_space=pltpu.VMEM)] * 2,
        out_specs=pl.BlockSpec(memory_space=pl.ANY),
        out_shape=jax.ShapeDtypeStruct(shape, left.dtype),
        scratch_shapes=[pltpu.SemaphoreType.DMA((shape[0] + shape[1],))],
        cost_estimate=pl.CostEstimate(flops=0, bytes_accessed=2 * 2**20, transcendentals=0),
        interpret=interpret,
        name="pack",
    )(left, right)


def forward(core, came, other, weight_t, bias, cot, width, interpret=False):
    seqs, cols, rows, pair_width = came.shape[0], cot.shape[0], cot.shape[1], cot.shape[2]
    flops = 2 * cols * rows * width * width * (2 * pair_width + seqs)
    first = other.shape[1] // (TILE * width)
    return pl.pallas_call(
        functools.partial(forward_kernel, 1.0 / seqs, width),
        grid=(cols // TILE,),
        in_specs=[
            pl.BlockSpec(memory_space=pltpu.SMEM),
            pl.BlockSpec(other.shape, lambda j: (0, 0)),
            whole(other.shape),
            pl.BlockSpec((seqs, TILE * width), lambda j: (0, first + j)),
            whole(weight_t.shape),
            whole(bias.shape),
            pl.BlockSpec((TILE, rows, pair_width), lambda j: (j, 0, 0)),
        ],
        out_specs=[
            pl.BlockSpec((TILE, rows, pair_width), lambda j: (j, 0, 0)),
            whole((width * width, pair_width)),
        ],
        out_shape=[
            jax.ShapeDtypeStruct((cols, rows, pair_width), jnp.bfloat16),
            jax.ShapeDtypeStruct((width * width, pair_width), jnp.float32),
        ],
        scratch_shapes=[pltpu.VMEM((width * width, TILE * rows), jnp.bfloat16)],
        compiler_params=params(),
        cost_estimate=pl.CostEstimate(flops=flops, bytes_accessed=8 * 2**20, transcendentals=0),
        interpret=interpret,
        name="forward",
    )(core.reshape(1), came, other, came, weight_t, bias, cot)


def exchange(blocks):
    return lax.all_to_all(blocks, BOTH, 0, 0, tiled=True)


def swap_cores(values):
    return lax.ppermute(values, "col", [(i, i ^ 1) for i in range(lax.axis_size("col"))])


def own_first(values, core):
    half = values.shape[0] // CORES
    return jnp.where(core == 0, values, jnp.concatenate([values[half:], values[:half]], axis=0))


def permute_groups():
    devices = lax.axis_size(BOTH)
    groups = [(1, CORES)]
    while groups[-1][0] * groups[-1][1] < devices:
        low = groups[-1][0] * groups[-1][1]
        groups.append((low, min(4, devices // low)))
    return groups


def partner(part, mask):
    return lax.ppermute(part, BOTH, [(i, i ^ mask) for i in range(lax.axis_size(BOTH))])


def add_parts(parts):
    while len(parts) > 1:
        parts = [parts[k] + parts[k + 1] for k in range(0, len(parts), 2)]
    return parts[0]


def scatter_pieces(values, low, size):
    values = values.reshape((-1, size) + values.shape[1:])
    mine = lax.axis_index(BOTH) // low % size
    return [lax.dynamic_index_in_dim(values, mine ^ mask, 1, keepdims=False) for mask in range(size)]


def sum_scatter(values, groups):
    for low, size in groups:
        kept, *pieces = scatter_pieces(values, low, size)
        values = add_parts([kept] + [partner(piece, low * (k + 1)) for k, piece in enumerate(pieces)])
    return values


def sum_all(first, second, values, early):
    core = lax.axis_index(BOTH) % CORES
    own, other = jnp.where(core == 0, first, second), jnp.where(core == 0, second, first)
    part = own + partner(other, 1)
    rows, columns = part.shape
    for step, (low, size) in enumerate(permute_groups()):
        if step == 0:
            continue
        if step < early:
            part = add_parts([part] + [partner(part, low * mask) for mask in range(1, size)])
            continue
        share, lanes = values.shape[1:]
        pieces = [piece.reshape(-1, lanes) for piece in scatter_pieces(values, low, size)]
        used = pieces[0].shape[0]
        pieces = [jnp.pad(piece, ((0, rows - used), (0, 0))) for piece in pieces]
        sent = [jnp.concatenate([part, piece], axis=1) for piece in pieces]
        both = add_parts(sent[:1] + [partner(sent[mask], low * mask) for mask in range(1, size)])
        part, values = both[:, :columns], both[:used, columns:].reshape(-1, share, lanes)
    other = partner(part, 1)
    return jnp.where(core == 0, part, other), jnp.where(core == 0, other, part), values


def body(alignment, left_weight, right_weight, out_weight, out_bias, pair_cotangent):
    row_count = lax.axis_size("row")
    col_count = lax.axis_size("col")
    devices = row_count * col_count
    local, residues, model_width = alignment.shape
    width = left_weight.shape[1]
    row_block, col_block, pair_width = pair_cotangent.shape
    seqs = local * devices

    normed, inv_sigma = layer_norm(alignment.astype(jnp.float32))
    normed_low = normed.astype(jnp.bfloat16)
    left = jnp.einsum("src,ch->shr", normed_low, left_weight, preferred_element_type=jnp.float32).astype(
        jnp.bfloat16
    )
    right = jnp.einsum("src,ch->srh", normed_low, right_weight, preferred_element_type=jnp.float32).astype(
        jnp.bfloat16
    )
    chips = col_count // CORES
    core = lax.axis_index("col") % CORES
    panel = row_block * width // CORES
    left_out = left.reshape(local, CORES, width // CORES, row_count, row_block).transpose(3, 1, 0, 2, 4)
    left_out = left_out.reshape(row_count, CORES, local, panel)
    right_out = right.reshape(local, chips, CORES, col_block * width).transpose(1, 2, 0, 3)
    sent = pack(left_out, right_out)
    columns = sent.shape[4]
    cot = pair_cotangent.transpose(1, 0, 2)
    bias = out_bias.astype(jnp.float32).reshape(1, pair_width)
    weight = own_first(out_weight, core)
    came = exchange(sent.reshape(devices, local, columns))
    came, outer_grad = lax.optimization_barrier((came, outer_grads(weight, cot, width)))
    came = came.reshape(seqs, columns)
    left_other = swap_cores(came[:, :panel])
    left_part, right_partial = left_grads(came, outer_grad)
    left_other, left_part = lax.optimization_barrier((left_other, left_part))
    left_share = swap_cores(left_part[:, panel:])
    right_part = right_grads(left_other, right_partial, outer_grad)
    left_pair = (left_part[:, :panel].astype(jnp.float32) + left_share.astype(jnp.float32)).astype(jnp.bfloat16)
    sent = jnp.concatenate([left_pair, right_part], axis=1).reshape(devices, local, columns)
    sent, left_other = lax.optimization_barrier((sent, left_other))
    back = exchange(sent).reshape(seqs, columns)
    update, weight_term = forward(core, came, left_other, weight.T, bias, cot, width)
    pair_update = update.transpose(1, 0, 2)
    early = 2
    weight_term = weight_term.reshape(devices, -1, pair_width)
    weight_term = sum_scatter(weight_term, permute_groups()[:early])
    back, weight_term = lax.optimization_barrier((back, weight_term))

    place = np.indices((row_count, chips, CORES, local)).reshape(4, -1)
    left_place = (place[3] * row_count + place[0]) * CORES + place[2]
    right_place = (place[3] * chips + place[1]) * CORES + place[2]
    left_rows, right_rows = local * row_count * CORES, local * chips * CORES
    left_pick = jnp.asarray(np.arange(left_rows)[:, None] == left_place[None], dtype=jnp.bfloat16)
    right_pick = jnp.asarray(np.arange(right_rows)[:, None] == right_place[None], dtype=jnp.bfloat16)
    left_grad = jnp.dot(left_pick, back[:, :panel], preferred_element_type=jnp.float32).astype(jnp.bfloat16)
    right_grad = jnp.dot(right_pick, back[:, panel:], preferred_element_type=jnp.float32).astype(jnp.bfloat16)
    left_grad = left_grad.reshape(local, row_count, width, row_block).transpose(0, 2, 1, 3)
    left_grad = left_grad.reshape(local, width, residues)
    right_grad = right_grad.reshape(local, residues, width)
    left_wgrad = jnp.einsum("src,shr->hc", normed_low, left_grad, preferred_element_type=jnp.float32)
    right_wgrad = jnp.einsum("src,srh->hc", normed_low, right_grad, preferred_element_type=jnp.float32)
    left_wgrad, right_wgrad, weight_term = sum_all(left_wgrad, right_wgrad, weight_term, early)
    grad_out_weight = weight_term.reshape(-1, pair_width)

    upstream = jnp.einsum("shr,ch->src", left_grad, left_weight, preferred_element_type=jnp.float32)
    upstream += jnp.einsum("srh,ch->src", right_grad, right_weight, preferred_element_type=jnp.float32)
    grad_alignment = norm_backward(upstream, normed, inv_sigma).astype(jnp.bfloat16)
    return (pair_update, grad_alignment, grad_out_weight, left_wgrad.T, right_wgrad.T)


def solution(mesh):
    return jax.shard_map(
        body,
        mesh=mesh,
        in_specs=(P(("row", "col"), None, None), P(), P(), P(), P(), P("row", "col", None)),
        out_specs=(
            P("row", "col", None),
            P(("row", "col"), None, None),
            P(("row", "col"), None),
            P(),
            P(),
        ),
        check_vma=False,
    )
```

```python
import functools

import jax
import jax.numpy as jnp
import numpy as np
from jax import lax
from jax.experimental import layout
from jax.experimental import pallas as pl
from jax.experimental.pallas import tpu as pltpu
from jax.sharding import PartitionSpec as P

BOTH = ("row", "col")
TILE = 16
GRAD_TILE = 8
BLOCKS = 4
CORES = 2
VMEM_BYTES = 48 * 1024 * 1024
NT = (((1,), (1,)), ((), ()))


def layer_norm(values):
    centered = values - jnp.mean(values, axis=-1, keepdims=True)
    inv_sigma = lax.rsqrt(jnp.mean(centered * centered, axis=-1, keepdims=True) + 1e-05)
    return (centered * inv_sigma, inv_sigma)


def norm_backward(upstream, normed, inv_sigma):
    first = jnp.mean(upstream, axis=-1, keepdims=True)
    second = jnp.mean(upstream * normed, axis=-1, keepdims=True)
    return inv_sigma * (upstream - first - normed * second)


def outer_grad_kernel(width, weight_ref, cot_ref, grad_ref):
    tile, rows, pair_width = cot_ref.shape
    flat = cot_ref[...].reshape(tile * rows, pair_width)
    step = 2
    for j in range(0, tile, step):
        grads = lax.dot_general(
            weight_ref[...], flat[j * rows:(j + step) * rows], NT, preferred_element_type=jnp.float32
        ).astype(jnp.bfloat16)
        for k in range(step):
            for c in range(width):
                grad_ref[(j + k) * width:(j + k + 1) * width, c * rows:(c + 1) * rows] = grads[
                    c * width:(c + 1) * width, k * rows:(k + 1) * rows
                ]


def left_kernel(inverse, came_ref, grad_ref, out_ref, partial_ref, panel_ref, held_ref, sems):
    blocks = sems.shape[0] - 1
    depth, columns = held_ref.shape
    block, half = columns // blocks, columns // CORES
    panel = pltpu.make_async_copy(came_ref, panel_ref, sems.at[blocks])
    panel.start()
    parts = [pl.ds(n * block, block) for n in range(blocks)]
    copies = [
        pltpu.make_async_copy(grad_ref.at[:, part], held_ref.at[:, part], sems.at[n]) for n, part in enumerate(parts)
    ]
    for copy in copies:
        copy.start()
    panel.wait()
    for n, part in enumerate(parts):
        if n == blocks // CORES:
            partial_ref[...] = lax.dot_general(
                panel_ref[:, :half], held_ref[:, :half], NT, preferred_element_type=jnp.float32
            )
        copies[n].wait()
        grads = jnp.dot(panel_ref[:, -depth:], held_ref[:, part], preferred_element_type=jnp.float32)
        out_ref[:, part] = (grads * inverse).astype(out_ref.dtype)


def right_kernel(inverse, other_ref, partial_ref, grad_ref, out_ref, held_ref, sems):
    blocks = sems.shape[0]
    rows, depth = held_ref.shape
    block = rows // blocks
    parts = [pl.ds(n * block, block) for n in range(blocks)]
    copies = [
        pltpu.make_async_copy(grad_ref.at[part, pl.ds(depth, depth)], held_ref.at[part], sems.at[n])
        for n, part in enumerate(parts)
    ]
    for copy in copies:
        copy.start()
    for n, part in enumerate(parts):
        copies[n].wait()
        grads = lax.dot_general(other_ref[...], held_ref[part], NT, preferred_element_type=jnp.float32)
        out_ref[:, part] = ((partial_ref[:, part] + grads) * inverse).astype(out_ref.dtype)


def pack_kernel(left_ref, right_ref, out_ref, sems):
    rows, chips = out_ref.shape[:2]
    panel = left_ref.shape[-1]
    copies = [
        pltpu.make_async_copy(right_ref, out_ref.at[k, :, :, :, pl.ds(panel, right_ref.shape[-1])], sems.at[k])
        for k in range(rows)
    ]
    copies += [
        pltpu.make_async_copy(left_ref, out_ref.at[:, k, :, :, pl.ds(0, panel)], sems.at[rows + k])
        for k in range(chips)
    ]
    for copy in copies:
        copy.start()
    for copy in copies:
        copy.wait()


def forward_kernel(
    inverse, width, core_ref, own_ref, other_ref, right_ref, weight_t_ref, bias_ref, cot_ref, update_ref, wgrad_ref, outer_ref
):
    tile, rows, pair_width = cot_ref.shape
    right_t = right_ref[...].T
    step = 2
    for c in range(0, width, step):
        half_ref, first = (own_ref, c) if c < width // 2 else (other_ref, c - width // 2)
        outer = jnp.dot(
            right_t, half_ref[:, first * rows:(first + step) * rows], preferred_element_type=jnp.float32
        ).astype(jnp.bfloat16)
        for k in range(step):
            for j in range(tile):
                outer_ref[(c + k) * width:(c + k + 1) * width, j * rows:(j + 1) * rows] = outer[
                    j * width:(j + 1) * width, k * rows:(k + 1) * rows
                ]
    for j in range(0, tile, step):
        update = jnp.dot(
            weight_t_ref[...], outer_ref[:, j * rows:(j + step) * rows], preferred_element_type=jnp.float32
        )
        for k in range(step):
            one = update[:, k * rows:(k + 1) * rows].T
            update_ref[j + k] = (one * inverse + bias_ref[...]).astype(update_ref.dtype)

    @pl.when(pl.program_id(0) == 0)
    def _():
        wgrad_ref[...] = jnp.zeros_like(wgrad_ref)

    flat = cot_ref[...].reshape(tile * rows, pair_width)
    half = wgrad_ref.shape[0] // CORES
    for k in range(CORES):
        place = pl.ds(pl.multiple_of((core_ref[0] ^ k) * half, half), half)
        wgrad_ref[place] += inverse * jnp.dot(
            outer_ref[k * half:(k + 1) * half], flat, preferred_element_type=jnp.float32
        )


def whole(shape):
    return pl.BlockSpec(shape, lambda j: (0,) * len(shape))


def params():
    return pltpu.CompilerParams(dimension_semantics=("arbitrary",), vmem_limit_bytes=VMEM_BYTES)


def outer_grads(weight, cot, width, interpret=False):
    cols, rows, pair_width = cot.shape
    return pl.pallas_call(
        functools.partial(outer_grad_kernel, width),
        grid=(cols // GRAD_TILE,),
        in_specs=[whole(weight.shape), pl.BlockSpec((GRAD_TILE, rows, pair_width), lambda j: (j, 0, 0))],
        out_specs=pl.BlockSpec((GRAD_TILE * width, width * rows), lambda j: (j, 0)),
        out_shape=jax.ShapeDtypeStruct((cols * width, width * rows), jnp.bfloat16),
        compiler_params=params(),
        cost_estimate=pl.CostEstimate(
            flops=2 * cols * rows * width * width * pair_width, bytes_accessed=18 * 2**20, transcendentals=0
        ),
        interpret=interpret,
        name="outer_grads",
    )(weight, cot)


def left_grads(came, grads, interpret=False):
    seqs, (depth, columns) = came.shape[0], grads.shape
    return pl.pallas_call(
        functools.partial(left_kernel, 1.0 / seqs),
        in_specs=[pl.BlockSpec(memory_space=pl.ANY)] * 2,
        out_specs=[pl.BlockSpec(memory_space=pltpu.VMEM)] * 2,
        out_shape=[
            jax.ShapeDtypeStruct((seqs, columns), jnp.bfloat16),
            jax.ShapeDtypeStruct((seqs, depth), jnp.float32),
        ],
        scratch_shapes=[
            pltpu.VMEM(came.shape, jnp.bfloat16),
            pltpu.VMEM(grads.shape, jnp.bfloat16),
            pltpu.SemaphoreType.DMA((BLOCKS + 1,)),
        ],
        compiler_params=pltpu.CompilerParams(vmem_limit_bytes=VMEM_BYTES),
        cost_estimate=pl.CostEstimate(flops=3 * seqs * depth * columns, bytes_accessed=21 * 2**20, transcendentals=0),
        interpret=interpret,
        name="left_grads",
    )(came, grads)


def right_grads(other, partial, grads, interpret=False):
    seqs, (rows, depth) = other.shape[0], grads.shape
    return pl.pallas_call(
        functools.partial(right_kernel, 1.0 / seqs),
        in_specs=[pl.BlockSpec(memory_space=pltpu.VMEM)] * 2 + [pl.BlockSpec(memory_space=pl.ANY)],
        out_specs=pl.BlockSpec(memory_space=pltpu.VMEM),
        out_shape=jax.ShapeDtypeStruct((seqs, rows), jnp.bfloat16),
        scratch_shapes=[pltpu.VMEM((rows, depth // CORES), jnp.bfloat16), pltpu.SemaphoreType.DMA((BLOCKS,))],
        compiler_params=pltpu.CompilerParams(vmem_limit_bytes=VMEM_BYTES),
        cost_estimate=pl.CostEstimate(flops=seqs * depth * rows, bytes_accessed=12 * 2**20, transcendentals=0),
        interpret=interpret,
        name="right_grads",
    )(other, partial, grads)


def pack(left, right, interpret=False):
    shape = (left.shape[0],) + right.shape[:-1] + (left.shape[-1] + right.shape[-1],)
    return pl.pallas_call(
        pack_kernel,
        in_specs=[pl.BlockSpec(memory_space=pltpu.VMEM)] * 2,
        out_specs=pl.BlockSpec(memory_space=pl.ANY),
        out_shape=jax.ShapeDtypeStruct(shape, left.dtype),
        scratch_shapes=[pltpu.SemaphoreType.DMA((shape[0] + shape[1],))],
        cost_estimate=pl.CostEstimate(flops=0, bytes_accessed=2 * 2**20, transcendentals=0),
        interpret=interpret,
        name="pack",
    )(left, right)


def forward(core, came, other, weight_t, bias, cot, width, interpret=False):
    seqs, cols, rows, pair_width = came.shape[0], cot.shape[0], cot.shape[1], cot.shape[2]
    flops = 2 * cols * rows * width * width * (2 * pair_width + seqs)
    first = other.shape[1] // (TILE * width)
    return pl.pallas_call(
        functools.partial(forward_kernel, 1.0 / seqs, width),
        grid=(cols // TILE,),
        in_specs=[
            pl.BlockSpec(memory_space=pltpu.SMEM),
            pl.BlockSpec(other.shape, lambda j: (0, 0)),
            whole(other.shape),
            pl.BlockSpec((seqs, TILE * width), lambda j: (0, first + j)),
            whole(weight_t.shape),
            whole(bias.shape),
            pl.BlockSpec((TILE, rows, pair_width), lambda j: (j, 0, 0)),
        ],
        out_specs=[
            pl.BlockSpec((TILE, rows, pair_width), lambda j: (j, 0, 0)),
            whole((width * width, pair_width)),
        ],
        out_shape=[
            jax.ShapeDtypeStruct((cols, rows, pair_width), jnp.bfloat16),
            jax.ShapeDtypeStruct((width * width, pair_width), jnp.float32),
        ],
        scratch_shapes=[pltpu.VMEM((width * width, TILE * rows), jnp.bfloat16)],
        compiler_params=params(),
        cost_estimate=pl.CostEstimate(flops=flops, bytes_accessed=8 * 2**20, transcendentals=0),
        interpret=interpret,
        name="forward",
    )(core.reshape(1), came, other, came, weight_t, bias, cot)


def exchange(blocks):
    return lax.all_to_all(blocks, BOTH, 0, 0, tiled=True)


def swap_cores(values):
    return lax.ppermute(values, "col", [(i, i ^ 1) for i in range(lax.axis_size("col"))])


def own_first(values, core):
    half = values.shape[0] // CORES
    return jnp.where(core == 0, values, jnp.concatenate([values[half:], values[:half]], axis=0))


def row_major(values):
    return layout.with_layout_constraint(values, layout.Layout(major_to_minor=tuple(range(values.ndim))))


def permute_groups():
    devices = lax.axis_size(BOTH)
    groups = [(1, CORES)]
    while groups[-1][0] * groups[-1][1] < devices:
        low = groups[-1][0] * groups[-1][1]
        groups.append((low, min(4, devices // low)))
    return groups


def partner(part, mask):
    return lax.ppermute(part, BOTH, [(i, i ^ mask) for i in range(lax.axis_size(BOTH))])


def add_parts(parts):
    while len(parts) > 1:
        parts = [parts[k] + parts[k + 1] for k in range(0, len(parts), 2)]
    return parts[0]


def scatter_pieces(values, low, size):
    values = values.reshape((-1, size) + values.shape[1:])
    mine = lax.axis_index(BOTH) // low % size
    return [lax.dynamic_index_in_dim(values, mine ^ mask, 1, keepdims=False) for mask in range(size)]


def sum_scatter(values, groups):
    for low, size in groups:
        kept, *pieces = scatter_pieces(values, low, size)
        values = add_parts([kept] + [partner(piece, low * (k + 1)) for k, piece in enumerate(pieces)])
    return values


def sum_all(first, second, values, early, beside):
    core = lax.axis_index(BOTH) % CORES
    own, other = jnp.where(core == 0, first, second), jnp.where(core == 0, second, first)
    part = own + partner(other, 1)
    rows, columns = part.shape
    for step, (low, size) in enumerate(permute_groups()):
        if step == 0:
            continue
        if step < early:
            part = add_parts([part] + [partner(part, low * mask) for mask in range(1, size)])
            continue
        if step == len(permute_groups()) - 1:
            part, beside = lax.optimization_barrier((part, beside))
        share, lanes = values.shape[1:]
        pieces = [piece.reshape(-1, lanes) for piece in scatter_pieces(values, low, size)]
        used = pieces[0].shape[0]
        pieces = [jnp.pad(piece, ((0, rows - used), (0, 0))) for piece in pieces]
        sent = [jnp.concatenate([part, piece], axis=1) for piece in pieces]
        both = add_parts(sent[:1] + [partner(sent[mask], low * mask) for mask in range(1, size)])
        part, values = both[:, :columns], both[:used, columns:].reshape(-1, share, lanes)
    other = partner(part, 1)
    return jnp.where(core == 0, part, other), jnp.where(core == 0, other, part), values, beside


def body(alignment, left_weight, right_weight, out_weight, out_bias, pair_cotangent):
    row_count = lax.axis_size("row")
    col_count = lax.axis_size("col")
    devices = row_count * col_count
    local, residues, model_width = alignment.shape
    width = left_weight.shape[1]
    row_block, col_block, pair_width = pair_cotangent.shape
    seqs = local * devices

    normed, inv_sigma = layer_norm(alignment.astype(jnp.float32))
    normed_low = normed.astype(jnp.bfloat16)
    left = jnp.einsum("src,ch->shr", normed_low, left_weight, preferred_element_type=jnp.float32).astype(
        jnp.bfloat16
    )
    right = jnp.einsum("src,ch->srh", normed_low, right_weight, preferred_element_type=jnp.float32).astype(
        jnp.bfloat16
    )
    chips = col_count // CORES
    core = lax.axis_index("col") % CORES
    panel = row_block * width // CORES
    left_out = left.reshape(local, CORES, width // CORES, row_count, row_block).transpose(3, 1, 0, 2, 4)
    left_out = left_out.reshape(row_count, CORES, local, panel)
    right_out = right.reshape(local, chips, CORES, col_block * width).transpose(1, 2, 0, 3)
    sent = pack(left_out, right_out)
    columns = sent.shape[4]
    cot = pair_cotangent.transpose(1, 0, 2)
    bias = out_bias.astype(jnp.float32).reshape(1, pair_width)
    weight = own_first(out_weight, core)
    came = exchange(sent.reshape(devices, local, columns))
    came, outer_grad = lax.optimization_barrier((came, outer_grads(weight, cot, width)))
    came = came.reshape(seqs, columns)
    left_other = swap_cores(came[:, :panel])
    left_part, right_partial = left_grads(came, outer_grad)
    left_other, left_part = lax.optimization_barrier((left_other, left_part))
    left_share = swap_cores(left_part[:, panel:])
    right_part = right_grads(left_other, right_partial, outer_grad)
    left_pair = (left_part[:, :panel].astype(jnp.float32) + left_share.astype(jnp.float32)).astype(jnp.bfloat16)
    sent = jnp.concatenate([left_pair, right_part], axis=1).reshape(devices, local, columns)
    sent, left_other = lax.optimization_barrier((sent, left_other))
    back = exchange(sent).reshape(seqs, columns)
    update, weight_term = forward(core, came, left_other, weight.T, bias, cot, width)
    pair_update = row_major(update.transpose(1, 0, 2))
    early = 2
    weight_term = weight_term.reshape(devices, -1, pair_width)
    weight_term = sum_scatter(weight_term, permute_groups()[:early])
    back, weight_term, pair_update = lax.optimization_barrier((back, weight_term, pair_update))

    place = np.indices((row_count, chips, CORES, local)).reshape(4, -1)
    left_place = (place[3] * row_count + place[0]) * CORES + place[2]
    right_place = (place[3] * chips + place[1]) * CORES + place[2]
    left_rows, right_rows = local * row_count * CORES, local * chips * CORES
    left_pick = jnp.asarray(np.arange(left_rows)[:, None] == left_place[None], dtype=jnp.bfloat16)
    right_pick = jnp.asarray(np.arange(right_rows)[:, None] == right_place[None], dtype=jnp.bfloat16)
    left_grad = jnp.dot(left_pick, back[:, :panel], preferred_element_type=jnp.float32).astype(jnp.bfloat16)
    right_grad = jnp.dot(right_pick, back[:, panel:], preferred_element_type=jnp.float32).astype(jnp.bfloat16)
    left_grad = left_grad.reshape(local, row_count, width, row_block).transpose(0, 2, 1, 3)
    left_grad = left_grad.reshape(local, width, residues)
    right_grad = right_grad.reshape(local, residues, width)
    left_wgrad = jnp.einsum("src,shr->hc", normed_low, left_grad, preferred_element_type=jnp.float32)
    right_wgrad = jnp.einsum("src,srh->hc", normed_low, right_grad, preferred_element_type=jnp.float32)
    upstream = jnp.einsum("shr,ch->src", left_grad, left_weight, preferred_element_type=jnp.float32)
    upstream += jnp.einsum("srh,ch->src", right_grad, right_weight, preferred_element_type=jnp.float32)
    grad_alignment = norm_backward(upstream, normed, inv_sigma).astype(jnp.bfloat16)
    grad_alignment = row_major(grad_alignment)
    left_wgrad, right_wgrad, weight_term, grad_alignment = sum_all(
        left_wgrad, right_wgrad, weight_term, early, grad_alignment
    )
    grad_out_weight = weight_term.reshape(-1, pair_width)
    return (pair_update, grad_alignment, grad_out_weight, left_wgrad.T, right_wgrad.T)


def solution(mesh):
    return jax.shard_map(
        body,
        mesh=mesh,
        in_specs=(P(("row", "col"), None, None), P(), P(), P(), P(), P("row", "col", None)),
        out_specs=(
            P("row", "col", None),
            P(("row", "col"), None, None),
            P(("row", "col"), None),
            P(),
            P(),
        ),
        check_vma=False,
    )
```

```python
import functools

import jax
import jax.numpy as jnp
import numpy as np
from jax import lax
from jax.experimental import layout
from jax.experimental import pallas as pl
from jax.experimental.pallas import tpu as pltpu
from jax.sharding import PartitionSpec as P

BOTH = ("row", "col")
TILE = 16
GRAD_TILE = 8
BLOCKS = 4
CORES = 2
VMEM_BYTES = 48 * 1024 * 1024
NT = (((1,), (1,)), ((), ()))


def layer_norm(values):
    centered = values - jnp.mean(values, axis=-1, keepdims=True)
    inv_sigma = lax.rsqrt(jnp.mean(centered * centered, axis=-1, keepdims=True) + 1e-05)
    return (centered * inv_sigma, inv_sigma)


def norm_backward(upstream, normed, inv_sigma):
    first = jnp.mean(upstream, axis=-1, keepdims=True)
    second = jnp.mean(upstream * normed, axis=-1, keepdims=True)
    return inv_sigma * (upstream - first - normed * second)


def outer_grad_kernel(width, weight_ref, cot_ref, grad_ref):
    tile, rows, pair_width = cot_ref.shape
    flat = cot_ref[...].reshape(tile * rows, pair_width)
    step = 2
    for j in range(0, tile, step):
        grads = lax.dot_general(
            weight_ref[...], flat[j * rows:(j + step) * rows], NT, preferred_element_type=jnp.float32
        ).astype(jnp.bfloat16)
        for k in range(step):
            for c in range(width):
                grad_ref[(j + k) * width:(j + k + 1) * width, c * rows:(c + 1) * rows] = grads[
                    c * width:(c + 1) * width, k * rows:(k + 1) * rows
                ]


def left_kernel(inverse, came_ref, grad_ref, out_ref, partial_ref, panel_ref, held_ref, sems):
    blocks = sems.shape[0] - 1
    depth, columns = held_ref.shape
    block, half = columns // blocks, columns // CORES
    panel = pltpu.make_async_copy(came_ref, panel_ref, sems.at[blocks])
    panel.start()
    parts = [pl.ds(n * block, block) for n in range(blocks)]
    copies = [
        pltpu.make_async_copy(grad_ref.at[:, part], held_ref.at[:, part], sems.at[n]) for n, part in enumerate(parts)
    ]
    for copy in copies:
        copy.start()
    panel.wait()
    for n, part in enumerate(parts):
        if n == blocks // CORES:
            partial_ref[...] = lax.dot_general(
                panel_ref[:, :half], held_ref[:, :half], NT, preferred_element_type=jnp.float32
            )
        copies[n].wait()
        grads = jnp.dot(panel_ref[:, -depth:], held_ref[:, part], preferred_element_type=jnp.float32)
        out_ref[:, part] = (grads * inverse).astype(out_ref.dtype)


def right_kernel(inverse, other_ref, partial_ref, grad_ref, out_ref, held_ref, sems):
    blocks = sems.shape[0]
    rows, depth = held_ref.shape
    block = rows // blocks
    parts = [pl.ds(n * block, block) for n in range(blocks)]
    copies = [
        pltpu.make_async_copy(grad_ref.at[part, pl.ds(depth, depth)], held_ref.at[part], sems.at[n])
        for n, part in enumerate(parts)
    ]
    for copy in copies:
        copy.start()
    for n, part in enumerate(parts):
        copies[n].wait()
        grads = lax.dot_general(other_ref[...], held_ref[part], NT, preferred_element_type=jnp.float32)
        out_ref[:, part] = ((partial_ref[:, part] + grads) * inverse).astype(out_ref.dtype)


def pack_kernel(left_ref, right_ref, out_ref, sems):
    rows, chips = out_ref.shape[:2]
    panel = left_ref.shape[-1]
    copies = [
        pltpu.make_async_copy(right_ref, out_ref.at[k, :, :, :, pl.ds(panel, right_ref.shape[-1])], sems.at[k])
        for k in range(rows)
    ]
    copies += [
        pltpu.make_async_copy(left_ref, out_ref.at[:, k, :, :, pl.ds(0, panel)], sems.at[rows + k])
        for k in range(chips)
    ]
    for copy in copies:
        copy.start()
    for copy in copies:
        copy.wait()


def forward_kernel(
    inverse, width, core_ref, own_ref, other_ref, right_ref, weight_t_ref, bias_ref, cot_ref, update_ref, wgrad_ref, outer_ref
):
    tile, rows, pair_width = cot_ref.shape
    right_t = right_ref[...].T
    step = 2
    for c in range(0, width, step):
        half_ref, first = (own_ref, c) if c < width // 2 else (other_ref, c - width // 2)
        outer = jnp.dot(
            right_t, half_ref[:, first * rows:(first + step) * rows], preferred_element_type=jnp.float32
        ).astype(jnp.bfloat16)
        for k in range(step):
            for j in range(tile):
                outer_ref[(c + k) * width:(c + k + 1) * width, j * rows:(j + 1) * rows] = outer[
                    j * width:(j + 1) * width, k * rows:(k + 1) * rows
                ]
    for j in range(0, tile, step):
        update = jnp.dot(
            weight_t_ref[...], outer_ref[:, j * rows:(j + step) * rows], preferred_element_type=jnp.float32
        )
        for k in range(step):
            one = update[:, k * rows:(k + 1) * rows].T
            update_ref[j + k] = (one * inverse + bias_ref[...]).astype(update_ref.dtype)

    @pl.when(pl.program_id(0) == 0)
    def _():
        wgrad_ref[...] = jnp.zeros_like(wgrad_ref)

    flat = cot_ref[...].reshape(tile * rows, pair_width)
    half = wgrad_ref.shape[0] // CORES
    for k in range(CORES):
        place = pl.ds(pl.multiple_of((core_ref[0] ^ k) * half, half), half)
        wgrad_ref[place] += inverse * jnp.dot(
            outer_ref[k * half:(k + 1) * half], flat, preferred_element_type=jnp.float32
        )


def whole(shape):
    return pl.BlockSpec(shape, lambda j: (0,) * len(shape))


def params():
    return pltpu.CompilerParams(dimension_semantics=("arbitrary",), vmem_limit_bytes=VMEM_BYTES)


def outer_grads(weight, cot, width, interpret=False):
    cols, rows, pair_width = cot.shape
    return pl.pallas_call(
        functools.partial(outer_grad_kernel, width),
        grid=(cols // GRAD_TILE,),
        in_specs=[whole(weight.shape), pl.BlockSpec((GRAD_TILE, rows, pair_width), lambda j: (j, 0, 0))],
        out_specs=pl.BlockSpec((GRAD_TILE * width, width * rows), lambda j: (j, 0)),
        out_shape=jax.ShapeDtypeStruct((cols * width, width * rows), jnp.bfloat16),
        compiler_params=params(),
        cost_estimate=pl.CostEstimate(
            flops=2 * cols * rows * width * width * pair_width, bytes_accessed=18 * 2**20, transcendentals=0
        ),
        interpret=interpret,
        name="outer_grads",
    )(weight, cot)


def left_grads(came, grads, interpret=False):
    seqs, (depth, columns) = came.shape[0], grads.shape
    return pl.pallas_call(
        functools.partial(left_kernel, 1.0 / seqs),
        in_specs=[pl.BlockSpec(memory_space=pl.ANY)] * 2,
        out_specs=[pl.BlockSpec(memory_space=pltpu.VMEM)] * 2,
        out_shape=[
            jax.ShapeDtypeStruct((seqs, columns), jnp.bfloat16),
            jax.ShapeDtypeStruct((seqs, depth), jnp.float32),
        ],
        scratch_shapes=[
            pltpu.VMEM(came.shape, jnp.bfloat16),
            pltpu.VMEM(grads.shape, jnp.bfloat16),
            pltpu.SemaphoreType.DMA((BLOCKS + 1,)),
        ],
        compiler_params=pltpu.CompilerParams(vmem_limit_bytes=VMEM_BYTES),
        cost_estimate=pl.CostEstimate(flops=3 * seqs * depth * columns, bytes_accessed=21 * 2**20, transcendentals=0),
        interpret=interpret,
        name="left_grads",
    )(came, grads)


def right_grads(other, partial, grads, interpret=False):
    seqs, (rows, depth) = other.shape[0], grads.shape
    return pl.pallas_call(
        functools.partial(right_kernel, 1.0 / seqs),
        in_specs=[pl.BlockSpec(memory_space=pltpu.VMEM)] * 2 + [pl.BlockSpec(memory_space=pl.ANY)],
        out_specs=pl.BlockSpec(memory_space=pltpu.VMEM),
        out_shape=jax.ShapeDtypeStruct((seqs, rows), jnp.bfloat16),
        scratch_shapes=[pltpu.VMEM((rows, depth // CORES), jnp.bfloat16), pltpu.SemaphoreType.DMA((BLOCKS,))],
        compiler_params=pltpu.CompilerParams(vmem_limit_bytes=VMEM_BYTES),
        cost_estimate=pl.CostEstimate(flops=seqs * depth * rows, bytes_accessed=12 * 2**20, transcendentals=0),
        interpret=interpret,
        name="right_grads",
    )(other, partial, grads)


def pack(left, right, interpret=False):
    shape = (left.shape[0],) + right.shape[:-1] + (left.shape[-1] + right.shape[-1],)
    return pl.pallas_call(
        pack_kernel,
        in_specs=[pl.BlockSpec(memory_space=pltpu.VMEM)] * 2,
        out_specs=pl.BlockSpec(memory_space=pl.ANY),
        out_shape=jax.ShapeDtypeStruct(shape, left.dtype),
        scratch_shapes=[pltpu.SemaphoreType.DMA((shape[0] + shape[1],))],
        cost_estimate=pl.CostEstimate(flops=0, bytes_accessed=2 * 2**20, transcendentals=0),
        interpret=interpret,
        name="pack",
    )(left, right)


def forward(core, came, other, weight_t, bias, cot, width, interpret=False):
    seqs, cols, rows, pair_width = came.shape[0], cot.shape[0], cot.shape[1], cot.shape[2]
    flops = 2 * cols * rows * width * width * (2 * pair_width + seqs)
    first = other.shape[1] // (TILE * width)
    return pl.pallas_call(
        functools.partial(forward_kernel, 1.0 / seqs, width),
        grid=(cols // TILE,),
        in_specs=[
            pl.BlockSpec(memory_space=pltpu.SMEM),
            pl.BlockSpec(other.shape, lambda j: (0, 0)),
            whole(other.shape),
            pl.BlockSpec((seqs, TILE * width), lambda j: (0, first + j)),
            whole(weight_t.shape),
            whole(bias.shape),
            pl.BlockSpec((TILE, rows, pair_width), lambda j: (j, 0, 0)),
        ],
        out_specs=[
            pl.BlockSpec((TILE, rows, pair_width), lambda j: (j, 0, 0)),
            whole((width * width, pair_width)),
        ],
        out_shape=[
            jax.ShapeDtypeStruct((cols, rows, pair_width), jnp.bfloat16),
            jax.ShapeDtypeStruct((width * width, pair_width), jnp.float32),
        ],
        scratch_shapes=[pltpu.VMEM((width * width, TILE * rows), jnp.bfloat16)],
        compiler_params=params(),
        cost_estimate=pl.CostEstimate(flops=flops, bytes_accessed=8 * 2**20, transcendentals=0),
        interpret=interpret,
        name="forward",
    )(core.reshape(1), came, other, came, weight_t, bias, cot)


def exchange(blocks):
    return lax.all_to_all(blocks, BOTH, 0, 0, tiled=True)


def swap_cores(values):
    return lax.ppermute(values, "col", [(i, i ^ 1) for i in range(lax.axis_size("col"))])


def own_first(values, core):
    half = values.shape[0] // CORES
    return jnp.where(core == 0, values, jnp.concatenate([values[half:], values[:half]], axis=0))


def row_major(values):
    return layout.with_layout_constraint(values, layout.Layout(major_to_minor=tuple(range(values.ndim))))


def permute_groups():
    devices = lax.axis_size(BOTH)
    groups = [(1, CORES)]
    while groups[-1][0] * groups[-1][1] < devices:
        low = groups[-1][0] * groups[-1][1]
        groups.append((low, min(4, devices // low)))
    return groups


def partner(part, mask):
    return lax.ppermute(part, BOTH, [(i, i ^ mask) for i in range(lax.axis_size(BOTH))])


def add_parts(parts):
    while len(parts) > 1:
        parts = [parts[k] + parts[k + 1] for k in range(0, len(parts), 2)]
    return parts[0]


def scatter_pieces(values, low, size):
    values = values.reshape((-1, size) + values.shape[1:])
    mine = lax.axis_index(BOTH) // low % size
    return [lax.dynamic_index_in_dim(values, mine ^ mask, 1, keepdims=False) for mask in range(size)]


def sum_scatter(values, groups):
    for low, size in groups:
        kept, *pieces = scatter_pieces(values, low, size)
        values = add_parts([kept] + [partner(piece, low * (k + 1)) for k, piece in enumerate(pieces)])
    return values


def sum_all(first, second, values, early, beside):
    core = lax.axis_index(BOTH) % CORES
    own, other = jnp.where(core == 0, first, second), jnp.where(core == 0, second, first)
    part = own + partner(other, 1)
    rows, columns = part.shape
    for step, (low, size) in enumerate(permute_groups()):
        if step == 0:
            continue
        if step < early:
            part = add_parts([part] + [partner(part, low * mask) for mask in range(1, size)])
            continue
        if step == len(permute_groups()) - 1:
            part, beside = lax.optimization_barrier((part, beside))
        share, lanes = values.shape[1:]
        pieces = [piece.reshape(-1, lanes) for piece in scatter_pieces(values, low, size)]
        used = pieces[0].shape[0]
        pieces = [jnp.pad(piece, ((0, rows - used), (0, 0))) for piece in pieces]
        sent = [jnp.concatenate([part, piece], axis=1) for piece in pieces]
        both = add_parts(sent[:1] + [partner(sent[mask], low * mask) for mask in range(1, size)])
        part, values = both[:, :columns], both[:used, columns:].reshape(-1, share, lanes)
    other = partner(part, 1)
    return jnp.where(core == 0, part, other), jnp.where(core == 0, other, part), values, beside


def body(alignment, left_weight, right_weight, out_weight, out_bias, pair_cotangent):
    row_count = lax.axis_size("row")
    col_count = lax.axis_size("col")
    devices = row_count * col_count
    local, residues, model_width = alignment.shape
    width = left_weight.shape[1]
    row_block, col_block, pair_width = pair_cotangent.shape
    seqs = local * devices

    normed, inv_sigma = layer_norm(alignment.astype(jnp.float32))
    normed_low = normed.astype(jnp.bfloat16)
    left = jnp.einsum("src,ch->shr", normed_low, left_weight, preferred_element_type=jnp.float32).astype(
        jnp.bfloat16
    )
    right = jnp.einsum("src,ch->srh", normed_low, right_weight, preferred_element_type=jnp.float32).astype(
        jnp.bfloat16
    )
    chips = col_count // CORES
    core = lax.axis_index("col") % CORES
    panel = row_block * width // CORES
    left_out = left.reshape(local, CORES, width // CORES, row_count, row_block).transpose(3, 1, 0, 2, 4)
    left_out = left_out.reshape(row_count, CORES, local, panel)
    right_out = right.reshape(local, chips, CORES, col_block * width).transpose(1, 2, 0, 3)
    sent = pack(left_out, right_out)
    columns = sent.shape[4]
    cot = pair_cotangent.transpose(1, 0, 2)
    bias = out_bias.astype(jnp.float32).reshape(1, pair_width)
    weight = own_first(out_weight, core)
    came = exchange(sent.reshape(devices, local, columns))
    came, outer_grad = lax.optimization_barrier((came, outer_grads(weight, cot, width)))
    came = came.reshape(seqs, columns)
    left_other = swap_cores(came[:, :panel])
    left_part, right_partial = left_grads(came, outer_grad)
    left_other, left_part = lax.optimization_barrier((left_other, left_part))
    left_share = swap_cores(left_part[:, panel:])
    right_part = right_grads(left_other, right_partial, outer_grad)
    left_pair = (left_part[:, :panel].astype(jnp.float32) + left_share.astype(jnp.float32)).astype(jnp.bfloat16)
    sent = jnp.concatenate([left_pair, right_part], axis=1).reshape(devices, local, columns)
    sent, left_other = lax.optimization_barrier((sent, left_other))
    back = exchange(sent).reshape(seqs, columns)
    update, weight_term = forward(core, came, left_other, weight.T, bias, cot, width)
    pair_update = row_major(update.transpose(1, 0, 2))
    early = 2
    weight_term = weight_term.reshape(devices, -1, pair_width)
    weight_term = sum_scatter(weight_term, permute_groups()[:early])
    back, weight_term = lax.optimization_barrier((back, weight_term))

    place = np.indices((row_count, chips, CORES, local)).reshape(4, -1)
    left_place = (place[3] * row_count + place[0]) * CORES + place[2]
    right_place = (place[3] * chips + place[1]) * CORES + place[2]
    left_rows, right_rows = local * row_count * CORES, local * chips * CORES
    left_pick = jnp.asarray(np.arange(left_rows)[:, None] == left_place[None], dtype=jnp.bfloat16)
    right_pick = jnp.asarray(np.arange(right_rows)[:, None] == right_place[None], dtype=jnp.bfloat16)
    left_grad = jnp.dot(left_pick, back[:, :panel], preferred_element_type=jnp.float32).astype(jnp.bfloat16)
    right_grad = jnp.dot(right_pick, back[:, panel:], preferred_element_type=jnp.float32).astype(jnp.bfloat16)
    left_grad = left_grad.reshape(local, row_count, width, row_block).transpose(0, 2, 1, 3)
    left_grad = left_grad.reshape(local, width, residues)
    right_grad = right_grad.reshape(local, residues, width)
    left_wgrad = jnp.einsum("src,shr->hc", normed_low, left_grad, preferred_element_type=jnp.float32)
    right_wgrad = jnp.einsum("src,srh->hc", normed_low, right_grad, preferred_element_type=jnp.float32)
    upstream = jnp.einsum("shr,ch->src", left_grad, left_weight, preferred_element_type=jnp.float32)
    upstream += jnp.einsum("srh,ch->src", right_grad, right_weight, preferred_element_type=jnp.float32)
    grad_alignment = norm_backward(upstream, normed, inv_sigma).astype(jnp.bfloat16)
    left_wgrad, right_wgrad, weight_term, pair_update = sum_all(
        left_wgrad, right_wgrad, weight_term, early, pair_update
    )
    grad_out_weight = weight_term.reshape(-1, pair_width)
    return (pair_update, grad_alignment, grad_out_weight, left_wgrad.T, right_wgrad.T)


def solution(mesh):
    return jax.shard_map(
        body,
        mesh=mesh,
        in_specs=(P(("row", "col"), None, None), P(), P(), P(), P(), P("row", "col", None)),
        out_specs=(
            P("row", "col", None),
            P(("row", "col"), None, None),
            P(("row", "col"), None),
            P(),
            P(),
        ),
        check_vma=False,
    )
```

```python
import functools

import jax
import jax.numpy as jnp
import numpy as np
from jax import lax
from jax.experimental import layout
from jax.experimental import pallas as pl
from jax.experimental.pallas import tpu as pltpu
from jax.sharding import PartitionSpec as P

BOTH = ("row", "col")
TILE = 16
GRAD_TILE = 8
BLOCKS = 4
CORES = 2
VMEM_BYTES = 48 * 1024 * 1024
NT = (((1,), (1,)), ((), ()))


def layer_norm(values):
    centered = values - jnp.mean(values, axis=-1, keepdims=True)
    inv_sigma = lax.rsqrt(jnp.mean(centered * centered, axis=-1, keepdims=True) + 1e-05)
    return (centered * inv_sigma, inv_sigma)


def norm_backward(upstream, normed, inv_sigma):
    first = jnp.mean(upstream, axis=-1, keepdims=True)
    second = jnp.mean(upstream * normed, axis=-1, keepdims=True)
    return inv_sigma * (upstream - first - normed * second)


def outer_grad_kernel(width, weight_ref, cot_ref, grad_ref):
    tile, rows, pair_width = cot_ref.shape
    flat = cot_ref[...].reshape(tile * rows, pair_width)
    step = 2
    for j in range(0, tile, step):
        grads = lax.dot_general(
            weight_ref[...], flat[j * rows:(j + step) * rows], NT, preferred_element_type=jnp.float32
        ).astype(jnp.bfloat16)
        for k in range(step):
            for c in range(width):
                grad_ref[(j + k) * width:(j + k + 1) * width, c * rows:(c + 1) * rows] = grads[
                    c * width:(c + 1) * width, k * rows:(k + 1) * rows
                ]


def left_kernel(inverse, came_ref, grad_ref, out_ref, partial_ref, panel_ref, held_ref, sems):
    blocks = sems.shape[0] - 1
    depth, columns = held_ref.shape
    block, half = columns // blocks, columns // CORES
    panel = pltpu.make_async_copy(came_ref, panel_ref, sems.at[blocks])
    panel.start()
    parts = [pl.ds(n * block, block) for n in range(blocks)]
    copies = [
        pltpu.make_async_copy(grad_ref.at[:, part], held_ref.at[:, part], sems.at[n]) for n, part in enumerate(parts)
    ]
    for copy in copies:
        copy.start()
    panel.wait()
    for n, part in enumerate(parts):
        if n == blocks // CORES:
            partial_ref[...] = lax.dot_general(
                panel_ref[:, :half], held_ref[:, :half], NT, preferred_element_type=jnp.float32
            )
        copies[n].wait()
        grads = jnp.dot(panel_ref[:, -depth:], held_ref[:, part], preferred_element_type=jnp.float32)
        out_ref[:, part] = (grads * inverse).astype(out_ref.dtype)


def right_kernel(inverse, other_ref, partial_ref, grad_ref, out_ref, held_ref, sems):
    blocks = sems.shape[0]
    rows, depth = held_ref.shape
    block = rows // blocks
    parts = [pl.ds(n * block, block) for n in range(blocks)]
    copies = [
        pltpu.make_async_copy(grad_ref.at[part, pl.ds(depth, depth)], held_ref.at[part], sems.at[n])
        for n, part in enumerate(parts)
    ]
    for copy in copies:
        copy.start()
    for n, part in enumerate(parts):
        copies[n].wait()
        grads = lax.dot_general(other_ref[...], held_ref[part], NT, preferred_element_type=jnp.float32)
        out_ref[:, part] = ((partial_ref[:, part] + grads) * inverse).astype(out_ref.dtype)


def pack_kernel(left_ref, right_ref, out_ref, sems):
    rows, chips = out_ref.shape[:2]
    panel = left_ref.shape[-1]
    copies = [
        pltpu.make_async_copy(right_ref, out_ref.at[k, :, :, :, pl.ds(panel, right_ref.shape[-1])], sems.at[k])
        for k in range(rows)
    ]
    copies += [
        pltpu.make_async_copy(left_ref, out_ref.at[:, k, :, :, pl.ds(0, panel)], sems.at[rows + k])
        for k in range(chips)
    ]
    for copy in copies:
        copy.start()
    for copy in copies:
        copy.wait()


def forward_kernel(
    inverse, width, core_ref, own_ref, other_ref, right_ref, weight_t_ref, bias_ref, cot_ref, update_ref, wgrad_ref, outer_ref
):
    tile, rows, pair_width = cot_ref.shape
    right_t = right_ref[...].T
    step = 2
    for c in range(0, width, step):
        half_ref, first = (own_ref, c) if c < width // 2 else (other_ref, c - width // 2)
        outer = jnp.dot(
            right_t, half_ref[:, first * rows:(first + step) * rows], preferred_element_type=jnp.float32
        ).astype(jnp.bfloat16)
        for k in range(step):
            for j in range(tile):
                outer_ref[(c + k) * width:(c + k + 1) * width, j * rows:(j + 1) * rows] = outer[
                    j * width:(j + 1) * width, k * rows:(k + 1) * rows
                ]
    for j in range(0, tile, step):
        update = jnp.dot(
            weight_t_ref[...], outer_ref[:, j * rows:(j + step) * rows], preferred_element_type=jnp.float32
        )
        for k in range(step):
            one = update[:, k * rows:(k + 1) * rows].T
            update_ref[j + k] = (one * inverse + bias_ref[...]).astype(update_ref.dtype)

    @pl.when(pl.program_id(0) == 0)
    def _():
        wgrad_ref[...] = jnp.zeros_like(wgrad_ref)

    flat = cot_ref[...].reshape(tile * rows, pair_width)
    half = wgrad_ref.shape[0] // CORES
    for k in range(CORES):
        place = pl.ds(pl.multiple_of((core_ref[0] ^ k) * half, half), half)
        wgrad_ref[place] += inverse * jnp.dot(
            outer_ref[k * half:(k + 1) * half], flat, preferred_element_type=jnp.float32
        )


def whole(shape):
    return pl.BlockSpec(shape, lambda j: (0,) * len(shape))


def params():
    return pltpu.CompilerParams(dimension_semantics=("arbitrary",), vmem_limit_bytes=VMEM_BYTES)


def outer_grads(weight, cot, width, interpret=False):
    cols, rows, pair_width = cot.shape
    return pl.pallas_call(
        functools.partial(outer_grad_kernel, width),
        grid=(cols // GRAD_TILE,),
        in_specs=[whole(weight.shape), pl.BlockSpec((GRAD_TILE, rows, pair_width), lambda j: (j, 0, 0))],
        out_specs=pl.BlockSpec((GRAD_TILE * width, width * rows), lambda j: (j, 0)),
        out_shape=jax.ShapeDtypeStruct((cols * width, width * rows), jnp.bfloat16),
        compiler_params=params(),
        cost_estimate=pl.CostEstimate(
            flops=2 * cols * rows * width * width * pair_width, bytes_accessed=18 * 2**20, transcendentals=0
        ),
        interpret=interpret,
        name="outer_grads",
    )(weight, cot)


def left_grads(came, grads, interpret=False):
    seqs, (depth, columns) = came.shape[0], grads.shape
    return pl.pallas_call(
        functools.partial(left_kernel, 1.0 / seqs),
        in_specs=[pl.BlockSpec(memory_space=pl.ANY)] * 2,
        out_specs=[pl.BlockSpec(memory_space=pltpu.VMEM)] * 2,
        out_shape=[
            jax.ShapeDtypeStruct((seqs, columns), jnp.bfloat16),
            jax.ShapeDtypeStruct((seqs, depth), jnp.float32),
        ],
        scratch_shapes=[
            pltpu.VMEM(came.shape, jnp.bfloat16),
            pltpu.VMEM(grads.shape, jnp.bfloat16),
            pltpu.SemaphoreType.DMA((BLOCKS + 1,)),
        ],
        compiler_params=pltpu.CompilerParams(vmem_limit_bytes=VMEM_BYTES),
        cost_estimate=pl.CostEstimate(flops=3 * seqs * depth * columns, bytes_accessed=21 * 2**20, transcendentals=0),
        interpret=interpret,
        name="left_grads",
    )(came, grads)


def right_grads(other, partial, grads, interpret=False):
    seqs, (rows, depth) = other.shape[0], grads.shape
    return pl.pallas_call(
        functools.partial(right_kernel, 1.0 / seqs),
        in_specs=[pl.BlockSpec(memory_space=pltpu.VMEM)] * 2 + [pl.BlockSpec(memory_space=pl.ANY)],
        out_specs=pl.BlockSpec(memory_space=pltpu.VMEM),
        out_shape=jax.ShapeDtypeStruct((seqs, rows), jnp.bfloat16),
        scratch_shapes=[pltpu.VMEM((rows, depth // CORES), jnp.bfloat16), pltpu.SemaphoreType.DMA((BLOCKS,))],
        compiler_params=pltpu.CompilerParams(vmem_limit_bytes=VMEM_BYTES),
        cost_estimate=pl.CostEstimate(flops=seqs * depth * rows, bytes_accessed=12 * 2**20, transcendentals=0),
        interpret=interpret,
        name="right_grads",
    )(other, partial, grads)


def pack(left, right, interpret=False):
    shape = (left.shape[0],) + right.shape[:-1] + (left.shape[-1] + right.shape[-1],)
    return pl.pallas_call(
        pack_kernel,
        in_specs=[pl.BlockSpec(memory_space=pltpu.VMEM)] * 2,
        out_specs=pl.BlockSpec(memory_space=pl.ANY),
        out_shape=jax.ShapeDtypeStruct(shape, left.dtype),
        scratch_shapes=[pltpu.SemaphoreType.DMA((shape[0] + shape[1],))],
        cost_estimate=pl.CostEstimate(flops=0, bytes_accessed=2 * 2**20, transcendentals=0),
        interpret=interpret,
        name="pack",
    )(left, right)


def forward(core, came, other, weight_t, bias, cot, width, interpret=False):
    seqs, cols, rows, pair_width = came.shape[0], cot.shape[0], cot.shape[1], cot.shape[2]
    flops = 2 * cols * rows * width * width * (2 * pair_width + seqs)
    first = other.shape[1] // (TILE * width)
    return pl.pallas_call(
        functools.partial(forward_kernel, 1.0 / seqs, width),
        grid=(cols // TILE,),
        in_specs=[
            pl.BlockSpec(memory_space=pltpu.SMEM),
            pl.BlockSpec(other.shape, lambda j: (0, 0)),
            whole(other.shape),
            pl.BlockSpec((seqs, TILE * width), lambda j: (0, first + j)),
            whole(weight_t.shape),
            whole(bias.shape),
            pl.BlockSpec((TILE, rows, pair_width), lambda j: (j, 0, 0)),
        ],
        out_specs=[
            pl.BlockSpec((TILE, rows, pair_width), lambda j: (j, 0, 0)),
            whole((width * width, pair_width)),
        ],
        out_shape=[
            jax.ShapeDtypeStruct((cols, rows, pair_width), jnp.bfloat16),
            jax.ShapeDtypeStruct((width * width, pair_width), jnp.float32),
        ],
        scratch_shapes=[pltpu.VMEM((width * width, TILE * rows), jnp.bfloat16)],
        compiler_params=params(),
        cost_estimate=pl.CostEstimate(flops=flops, bytes_accessed=8 * 2**20, transcendentals=0),
        interpret=interpret,
        name="forward",
    )(core.reshape(1), came, other, came, weight_t, bias, cot)


def flip_kernel(in_ref, out_ref):
    for k in range(in_ref.shape[0]):
        out_ref[k] = in_ref[k].T


def flip(values, interpret=False):
    shape = (values.shape[0], values.shape[2], values.shape[1])
    return pl.pallas_call(
        flip_kernel,
        in_specs=[pl.BlockSpec(memory_space=pltpu.VMEM)],
        out_specs=pl.BlockSpec(memory_space=pltpu.VMEM),
        out_shape=jax.ShapeDtypeStruct(shape, values.dtype),
        compiler_params=pltpu.CompilerParams(vmem_limit_bytes=VMEM_BYTES),
        cost_estimate=pl.CostEstimate(flops=0, bytes_accessed=2 * 2**20, transcendentals=0),
        interpret=interpret,
        name="flip",
    )(values)


def exchange(blocks):
    return lax.all_to_all(blocks, BOTH, 0, 0, tiled=True)


def swap_cores(values):
    return lax.ppermute(values, "col", [(i, i ^ 1) for i in range(lax.axis_size("col"))])


def own_first(values, core):
    half = values.shape[0] // CORES
    return jnp.where(core == 0, values, jnp.concatenate([values[half:], values[:half]], axis=0))


def row_major(values):
    return layout.with_layout_constraint(values, layout.Layout(major_to_minor=tuple(range(values.ndim))))


def permute_groups():
    devices = lax.axis_size(BOTH)
    groups = [(1, CORES)]
    while groups[-1][0] * groups[-1][1] < devices:
        low = groups[-1][0] * groups[-1][1]
        groups.append((low, min(4, devices // low)))
    return groups


def partner(part, mask):
    return lax.ppermute(part, BOTH, [(i, i ^ mask) for i in range(lax.axis_size(BOTH))])


def add_parts(parts):
    while len(parts) > 1:
        parts = [parts[k] + parts[k + 1] for k in range(0, len(parts), 2)]
    return parts[0]


def scatter_pieces(values, low, size):
    values = values.reshape((-1, size) + values.shape[1:])
    mine = lax.axis_index(BOTH) // low % size
    return [lax.dynamic_index_in_dim(values, mine ^ mask, 1, keepdims=False) for mask in range(size)]


def sum_scatter(values, groups):
    for low, size in groups:
        kept, *pieces = scatter_pieces(values, low, size)
        values = add_parts([kept] + [partner(piece, low * (k + 1)) for k, piece in enumerate(pieces)])
    return values


def sum_all(first, second, values, early, beside):
    core = lax.axis_index(BOTH) % CORES
    own, other = jnp.where(core == 0, first, second), jnp.where(core == 0, second, first)
    part = own + partner(other, 1)
    rows, columns = part.shape
    for step, (low, size) in enumerate(permute_groups()):
        if step == 0:
            continue
        if step < early:
            part = add_parts([part] + [partner(part, low * mask) for mask in range(1, size)])
            continue
        if step == len(permute_groups()) - 1:
            part, beside[0] = lax.optimization_barrier((part, beside[0]))
        share, lanes = values.shape[1:]
        pieces = [piece.reshape(-1, lanes) for piece in scatter_pieces(values, low, size)]
        used = pieces[0].shape[0]
        pieces = [jnp.pad(piece, ((0, rows - used), (0, 0))) for piece in pieces]
        sent = [jnp.concatenate([part, piece], axis=1) for piece in pieces]
        both = add_parts(sent[:1] + [partner(sent[mask], low * mask) for mask in range(1, size)])
        part, values = both[:, :columns], both[:used, columns:].reshape(-1, share, lanes)
    part, beside[1] = lax.optimization_barrier((part, beside[1]))
    other = partner(part, 1)
    return jnp.where(core == 0, part, other), jnp.where(core == 0, other, part), values, beside


def body(alignment, left_weight, right_weight, out_weight, out_bias, pair_cotangent):
    row_count = lax.axis_size("row")
    col_count = lax.axis_size("col")
    devices = row_count * col_count
    local, residues, model_width = alignment.shape
    width = left_weight.shape[1]
    row_block, col_block, pair_width = pair_cotangent.shape
    seqs = local * devices

    normed, inv_sigma = layer_norm(alignment.astype(jnp.float32))
    normed_low = normed.astype(jnp.bfloat16)
    left = jnp.einsum("src,ch->shr", normed_low, left_weight, preferred_element_type=jnp.float32).astype(
        jnp.bfloat16
    )
    right = jnp.einsum("src,ch->srh", normed_low, right_weight, preferred_element_type=jnp.float32).astype(
        jnp.bfloat16
    )
    chips = col_count // CORES
    core = lax.axis_index("col") % CORES
    panel = row_block * width // CORES
    left_out = left.reshape(local, CORES, width // CORES, row_count, row_block).transpose(3, 1, 0, 2, 4)
    left_out = left_out.reshape(row_count, CORES, local, panel)
    right_out = right.reshape(local, chips, CORES, col_block * width).transpose(1, 2, 0, 3)
    sent = pack(left_out, right_out)
    columns = sent.shape[4]
    cot = pair_cotangent.transpose(1, 0, 2)
    bias = out_bias.astype(jnp.float32).reshape(1, pair_width)
    weight = own_first(out_weight, core)
    came = exchange(sent.reshape(devices, local, columns))
    came, outer_grad = lax.optimization_barrier((came, outer_grads(weight, cot, width)))
    came = came.reshape(seqs, columns)
    left_other = swap_cores(came[:, :panel])
    left_part, right_partial = left_grads(came, outer_grad)
    left_other, left_part = lax.optimization_barrier((left_other, left_part))
    left_share = swap_cores(left_part[:, panel:])
    right_part = right_grads(left_other, right_partial, outer_grad)
    left_pair = (left_part[:, :panel].astype(jnp.float32) + left_share.astype(jnp.float32)).astype(jnp.bfloat16)
    sent = jnp.concatenate([left_pair, right_part], axis=1).reshape(devices, local, columns)
    sent, left_other = lax.optimization_barrier((sent, left_other))
    back = exchange(sent).reshape(seqs, columns)
    update, weight_term = forward(core, came, left_other, weight.T, bias, cot, width)
    early = 2
    weight_term = weight_term.reshape(devices, -1, pair_width)
    weight_term = sum_scatter(weight_term, permute_groups()[:early])
    back, weight_term, update = lax.optimization_barrier((back, weight_term, update))
    pair_update = row_major(update.transpose(1, 0, 2))

    place = np.indices((row_count, chips, CORES, local)).reshape(4, -1)
    left_place = (place[3] * row_count + place[0]) * CORES + place[2]
    right_place = (place[3] * chips + place[1]) * CORES + place[2]
    left_rows, right_rows = local * row_count * CORES, local * chips * CORES
    left_pick = jnp.asarray(np.arange(left_rows)[:, None] == left_place[None], dtype=jnp.bfloat16)
    right_pick = jnp.asarray(np.arange(right_rows)[:, None] == right_place[None], dtype=jnp.bfloat16)
    left_grad = jnp.dot(left_pick, back[:, :panel], preferred_element_type=jnp.float32).astype(jnp.bfloat16)
    right_grad = jnp.dot(right_pick, back[:, panel:], preferred_element_type=jnp.float32).astype(jnp.bfloat16)
    left_grad = left_grad.reshape(local, row_count, width, row_block).transpose(0, 2, 1, 3)
    left_grad = left_grad.reshape(local, width, residues)
    right_grad = right_grad.reshape(local, residues, width)
    left_wgrad = jnp.einsum("src,shr->hc", normed_low, left_grad, preferred_element_type=jnp.float32)
    right_wgrad = jnp.einsum("src,srh->hc", normed_low, right_grad, preferred_element_type=jnp.float32)
    upstream = jnp.einsum("shr,ch->src", left_grad, left_weight, preferred_element_type=jnp.float32)
    upstream += jnp.einsum("srh,ch->src", right_grad, right_weight, preferred_element_type=jnp.float32)
    grad_alignment = norm_backward(upstream, normed, inv_sigma).astype(jnp.bfloat16)
    grad_alignment = flip(grad_alignment.transpose(0, 2, 1))
    left_wgrad, right_wgrad, weight_term, (grad_alignment, pair_update) = sum_all(
        left_wgrad, right_wgrad, weight_term, early, [grad_alignment, pair_update]
    )
    grad_out_weight = weight_term.reshape(-1, pair_width)
    return (pair_update, grad_alignment, grad_out_weight, left_wgrad.T, right_wgrad.T)


def solution(mesh):
    return jax.shard_map(
        body,
        mesh=mesh,
        in_specs=(P(("row", "col"), None, None), P(), P(), P(), P(), P("row", "col", None)),
        out_specs=(
            P("row", "col", None),
            P(("row", "col"), None, None),
            P(("row", "col"), None),
            P(),
            P(),
        ),
        check_vma=False,
    )
```

```python
import functools

import jax
import jax.numpy as jnp
import numpy as np
from jax import lax
from jax.experimental import layout
from jax.experimental import pallas as pl
from jax.experimental.pallas import tpu as pltpu
from jax.sharding import PartitionSpec as P

BOTH = ("row", "col")
TILE = 16
GRAD_TILE = 8
BLOCKS = 4
CORES = 2
VMEM_BYTES = 48 * 1024 * 1024
NT = (((1,), (1,)), ((), ()))


def layer_norm(values):
    centered = values - jnp.mean(values, axis=-1, keepdims=True)
    inv_sigma = lax.rsqrt(jnp.mean(centered * centered, axis=-1, keepdims=True) + 1e-05)
    return (centered * inv_sigma, inv_sigma)


def norm_backward(upstream, normed, inv_sigma):
    first = jnp.mean(upstream, axis=-1, keepdims=True)
    second = jnp.mean(upstream * normed, axis=-1, keepdims=True)
    return inv_sigma * (upstream - first - normed * second)


def outer_grad_kernel(width, weight_ref, cot_ref, grad_ref):
    tile, rows, pair_width = cot_ref.shape
    flat = cot_ref[...].reshape(tile * rows, pair_width)
    step = 2
    for j in range(0, tile, step):
        grads = lax.dot_general(
            weight_ref[...], flat[j * rows:(j + step) * rows], NT, preferred_element_type=jnp.float32
        ).astype(jnp.bfloat16)
        for k in range(step):
            for c in range(width):
                grad_ref[(j + k) * width:(j + k + 1) * width, c * rows:(c + 1) * rows] = grads[
                    c * width:(c + 1) * width, k * rows:(k + 1) * rows
                ]


def left_kernel(inverse, came_ref, grad_ref, out_ref, partial_ref, panel_ref, held_ref, sems):
    blocks = sems.shape[0] - 1
    depth, columns = held_ref.shape
    block, half = columns // blocks, columns // CORES
    panel = pltpu.make_async_copy(came_ref, panel_ref, sems.at[blocks])
    panel.start()
    parts = [pl.ds(n * block, block) for n in range(blocks)]
    copies = [
        pltpu.make_async_copy(grad_ref.at[:, part], held_ref.at[:, part], sems.at[n]) for n, part in enumerate(parts)
    ]
    for copy in copies:
        copy.start()
    panel.wait()
    for n, part in enumerate(parts):
        if n == blocks // CORES:
            partial_ref[...] = lax.dot_general(
                panel_ref[:, :half], held_ref[:, :half], NT, preferred_element_type=jnp.float32
            )
        copies[n].wait()
        grads = jnp.dot(panel_ref[:, -depth:], held_ref[:, part], preferred_element_type=jnp.float32)
        out_ref[:, part] = (grads * inverse).astype(out_ref.dtype)


def right_kernel(inverse, other_ref, partial_ref, grad_ref, out_ref, held_ref, sems):
    blocks = sems.shape[0]
    rows, depth = held_ref.shape
    block = rows // blocks
    parts = [pl.ds(n * block, block) for n in range(blocks)]
    copies = [
        pltpu.make_async_copy(grad_ref.at[part, pl.ds(depth, depth)], held_ref.at[part], sems.at[n])
        for n, part in enumerate(parts)
    ]
    for copy in copies:
        copy.start()
    for n, part in enumerate(parts):
        copies[n].wait()
        grads = lax.dot_general(other_ref[...], held_ref[part], NT, preferred_element_type=jnp.float32)
        out_ref[:, part] = ((partial_ref[:, part] + grads) * inverse).astype(out_ref.dtype)


def pack_kernel(left_ref, right_ref, out_ref, sems):
    rows, chips = out_ref.shape[:2]
    panel = left_ref.shape[-1]
    copies = [
        pltpu.make_async_copy(right_ref, out_ref.at[k, :, :, :, pl.ds(panel, right_ref.shape[-1])], sems.at[k])
        for k in range(rows)
    ]
    copies += [
        pltpu.make_async_copy(left_ref, out_ref.at[:, k, :, :, pl.ds(0, panel)], sems.at[rows + k])
        for k in range(chips)
    ]
    for copy in copies:
        copy.start()
    for copy in copies:
        copy.wait()


def forward_kernel(
    inverse, width, core_ref, own_ref, other_ref, right_ref, weight_t_ref, bias_ref, cot_ref, update_ref, wgrad_ref, outer_ref
):
    tile, rows, pair_width = cot_ref.shape
    right_t = right_ref[...].T
    step = 2
    for c in range(0, width, step):
        half_ref, first = (own_ref, c) if c < width // 2 else (other_ref, c - width // 2)
        outer = jnp.dot(
            right_t, half_ref[:, first * rows:(first + step) * rows], preferred_element_type=jnp.float32
        ).astype(jnp.bfloat16)
        for k in range(step):
            for j in range(tile):
                outer_ref[(c + k) * width:(c + k + 1) * width, j * rows:(j + 1) * rows] = outer[
                    j * width:(j + 1) * width, k * rows:(k + 1) * rows
                ]
    for j in range(0, tile, step):
        update = jnp.dot(
            weight_t_ref[...], outer_ref[:, j * rows:(j + step) * rows], preferred_element_type=jnp.float32
        )
        for k in range(step):
            one = update[:, k * rows:(k + 1) * rows].T
            update_ref[j + k] = (one * inverse + bias_ref[...]).astype(update_ref.dtype)

    @pl.when(pl.program_id(0) == 0)
    def _():
        wgrad_ref[...] = jnp.zeros_like(wgrad_ref)

    flat = cot_ref[...].reshape(tile * rows, pair_width)
    half = wgrad_ref.shape[0] // CORES
    for k in range(CORES):
        place = pl.ds(pl.multiple_of((core_ref[0] ^ k) * half, half), half)
        wgrad_ref[place] += inverse * jnp.dot(
            outer_ref[k * half:(k + 1) * half], flat, preferred_element_type=jnp.float32
        )


def whole(shape):
    return pl.BlockSpec(shape, lambda j: (0,) * len(shape))


def params():
    return pltpu.CompilerParams(dimension_semantics=("arbitrary",), vmem_limit_bytes=VMEM_BYTES)


def outer_grads(weight, cot, width, interpret=False):
    cols, rows, pair_width = cot.shape
    return pl.pallas_call(
        functools.partial(outer_grad_kernel, width),
        grid=(cols // GRAD_TILE,),
        in_specs=[whole(weight.shape), pl.BlockSpec((GRAD_TILE, rows, pair_width), lambda j: (j, 0, 0))],
        out_specs=pl.BlockSpec((GRAD_TILE * width, width * rows), lambda j: (j, 0)),
        out_shape=jax.ShapeDtypeStruct((cols * width, width * rows), jnp.bfloat16),
        compiler_params=params(),
        cost_estimate=pl.CostEstimate(
            flops=2 * cols * rows * width * width * pair_width, bytes_accessed=18 * 2**20, transcendentals=0
        ),
        interpret=interpret,
        name="outer_grads",
    )(weight, cot)


def left_grads(came, grads, interpret=False):
    seqs, (depth, columns) = came.shape[0], grads.shape
    return pl.pallas_call(
        functools.partial(left_kernel, 1.0 / seqs),
        in_specs=[pl.BlockSpec(memory_space=pl.ANY)] * 2,
        out_specs=[pl.BlockSpec(memory_space=pltpu.VMEM)] * 2,
        out_shape=[
            jax.ShapeDtypeStruct((seqs, columns), jnp.bfloat16),
            jax.ShapeDtypeStruct((seqs, depth), jnp.float32),
        ],
        scratch_shapes=[
            pltpu.VMEM(came.shape, jnp.bfloat16),
            pltpu.VMEM(grads.shape, jnp.bfloat16),
            pltpu.SemaphoreType.DMA((BLOCKS + 1,)),
        ],
        compiler_params=pltpu.CompilerParams(vmem_limit_bytes=VMEM_BYTES),
        cost_estimate=pl.CostEstimate(flops=3 * seqs * depth * columns, bytes_accessed=21 * 2**20, transcendentals=0),
        interpret=interpret,
        name="left_grads",
    )(came, grads)


def right_grads(other, partial, grads, interpret=False):
    seqs, (rows, depth) = other.shape[0], grads.shape
    return pl.pallas_call(
        functools.partial(right_kernel, 1.0 / seqs),
        in_specs=[pl.BlockSpec(memory_space=pltpu.VMEM)] * 2 + [pl.BlockSpec(memory_space=pl.ANY)],
        out_specs=pl.BlockSpec(memory_space=pltpu.VMEM),
        out_shape=jax.ShapeDtypeStruct((seqs, rows), jnp.bfloat16),
        scratch_shapes=[pltpu.VMEM((rows, depth // CORES), jnp.bfloat16), pltpu.SemaphoreType.DMA((BLOCKS,))],
        compiler_params=pltpu.CompilerParams(vmem_limit_bytes=VMEM_BYTES),
        cost_estimate=pl.CostEstimate(flops=seqs * depth * rows, bytes_accessed=12 * 2**20, transcendentals=0),
        interpret=interpret,
        name="right_grads",
    )(other, partial, grads)


def pack(left, right, interpret=False):
    shape = (left.shape[0],) + right.shape[:-1] + (left.shape[-1] + right.shape[-1],)
    return pl.pallas_call(
        pack_kernel,
        in_specs=[pl.BlockSpec(memory_space=pltpu.VMEM)] * 2,
        out_specs=pl.BlockSpec(memory_space=pl.ANY),
        out_shape=jax.ShapeDtypeStruct(shape, left.dtype),
        scratch_shapes=[pltpu.SemaphoreType.DMA((shape[0] + shape[1],))],
        cost_estimate=pl.CostEstimate(flops=0, bytes_accessed=2 * 2**20, transcendentals=0),
        interpret=interpret,
        name="pack",
    )(left, right)


def forward(core, came, other, weight_t, bias, cot, width, interpret=False):
    seqs, cols, rows, pair_width = came.shape[0], cot.shape[0], cot.shape[1], cot.shape[2]
    flops = 2 * cols * rows * width * width * (2 * pair_width + seqs)
    first = other.shape[1] // (TILE * width)
    return pl.pallas_call(
        functools.partial(forward_kernel, 1.0 / seqs, width),
        grid=(cols // TILE,),
        in_specs=[
            pl.BlockSpec(memory_space=pltpu.SMEM),
            pl.BlockSpec(other.shape, lambda j: (0, 0)),
            whole(other.shape),
            pl.BlockSpec((seqs, TILE * width), lambda j: (0, first + j)),
            whole(weight_t.shape),
            whole(bias.shape),
            pl.BlockSpec((TILE, rows, pair_width), lambda j: (j, 0, 0)),
        ],
        out_specs=[
            pl.BlockSpec((TILE, rows, pair_width), lambda j: (j, 0, 0)),
            whole((width * width, pair_width)),
        ],
        out_shape=[
            jax.ShapeDtypeStruct((cols, rows, pair_width), jnp.bfloat16),
            jax.ShapeDtypeStruct((width * width, pair_width), jnp.float32),
        ],
        scratch_shapes=[pltpu.VMEM((width * width, TILE * rows), jnp.bfloat16)],
        compiler_params=params(),
        cost_estimate=pl.CostEstimate(flops=flops, bytes_accessed=8 * 2**20, transcendentals=0),
        interpret=interpret,
        name="forward",
    )(core.reshape(1), came, other, came, weight_t, bias, cot)


def flip_kernel(in_ref, out_ref):
    for k in range(in_ref.shape[0]):
        out_ref[k] = in_ref[k].T


def flip(values, interpret=False):
    shape = (values.shape[0], values.shape[2], values.shape[1])
    return pl.pallas_call(
        flip_kernel,
        in_specs=[pl.BlockSpec(memory_space=pltpu.VMEM)],
        out_specs=pl.BlockSpec(memory_space=pltpu.VMEM),
        out_shape=jax.ShapeDtypeStruct(shape, values.dtype),
        compiler_params=pltpu.CompilerParams(vmem_limit_bytes=VMEM_BYTES),
        cost_estimate=pl.CostEstimate(flops=0, bytes_accessed=2 * 2**20, transcendentals=0),
        interpret=interpret,
        name="flip",
    )(values)


def exchange(blocks):
    return lax.all_to_all(blocks, BOTH, 0, 0, tiled=True)


def swap_cores(values):
    return lax.ppermute(values, "col", [(i, i ^ 1) for i in range(lax.axis_size("col"))])


def own_first(values, core):
    half = values.shape[0] // CORES
    return jnp.where(core == 0, values, jnp.concatenate([values[half:], values[:half]], axis=0))


def row_major(values):
    return layout.with_layout_constraint(values, layout.Layout(major_to_minor=tuple(range(values.ndim))))


def permute_groups():
    devices = lax.axis_size(BOTH)
    groups = [(1, CORES)]
    while groups[-1][0] * groups[-1][1] < devices:
        low = groups[-1][0] * groups[-1][1]
        groups.append((low, min(4, devices // low)))
    return groups


def partner(part, mask):
    return lax.ppermute(part, BOTH, [(i, i ^ mask) for i in range(lax.axis_size(BOTH))])


def add_parts(parts):
    while len(parts) > 1:
        parts = [parts[k] + parts[k + 1] for k in range(0, len(parts), 2)]
    return parts[0]


def scatter_pieces(values, low, size):
    values = values.reshape((-1, size) + values.shape[1:])
    mine = lax.axis_index(BOTH) // low % size
    return [lax.dynamic_index_in_dim(values, mine ^ mask, 1, keepdims=False) for mask in range(size)]


def sum_scatter(values, groups):
    for low, size in groups:
        kept, *pieces = scatter_pieces(values, low, size)
        values = add_parts([kept] + [partner(piece, low * (k + 1)) for k, piece in enumerate(pieces)])
    return values


def sum_all(first, second, values, early, beside):
    core = lax.axis_index(BOTH) % CORES
    own, other = jnp.where(core == 0, first, second), jnp.where(core == 0, second, first)
    part = own + partner(other, 1)
    rows, columns = part.shape
    for step, (low, size) in enumerate(permute_groups()):
        if step == 0:
            continue
        if step < early:
            part = add_parts([part] + [partner(part, low * mask) for mask in range(1, size)])
            continue
        if step == early:
            part, values = lax.optimization_barrier((part, values))
            values = add_parts(values)
        if step == len(permute_groups()) - 1:
            part, beside[0] = lax.optimization_barrier((part, beside[0]))
        share, lanes = values.shape[1:]
        pieces = [piece.reshape(-1, lanes) for piece in scatter_pieces(values, low, size)]
        used = pieces[0].shape[0]
        pieces = [jnp.pad(piece, ((0, rows - used), (0, 0))) for piece in pieces]
        sent = [jnp.concatenate([part, piece], axis=1) for piece in pieces]
        both = add_parts(sent[:1] + [partner(sent[mask], low * mask) for mask in range(1, size)])
        part, values = both[:, :columns], both[:used, columns:].reshape(-1, share, lanes)
    part, beside[1] = lax.optimization_barrier((part, beside[1]))
    other = partner(part, 1)
    return jnp.where(core == 0, part, other), jnp.where(core == 0, other, part), values, beside


def body(alignment, left_weight, right_weight, out_weight, out_bias, pair_cotangent):
    row_count = lax.axis_size("row")
    col_count = lax.axis_size("col")
    devices = row_count * col_count
    local, residues, model_width = alignment.shape
    width = left_weight.shape[1]
    row_block, col_block, pair_width = pair_cotangent.shape
    seqs = local * devices

    normed, inv_sigma = layer_norm(alignment.astype(jnp.float32))
    normed_low = normed.astype(jnp.bfloat16)
    left = jnp.einsum("src,ch->shr", normed_low, left_weight, preferred_element_type=jnp.float32).astype(
        jnp.bfloat16
    )
    right = jnp.einsum("src,ch->srh", normed_low, right_weight, preferred_element_type=jnp.float32).astype(
        jnp.bfloat16
    )
    chips = col_count // CORES
    core = lax.axis_index("col") % CORES
    panel = row_block * width // CORES
    left_out = left.reshape(local, CORES, width // CORES, row_count, row_block).transpose(3, 1, 0, 2, 4)
    left_out = left_out.reshape(row_count, CORES, local, panel)
    right_out = right.reshape(local, chips, CORES, col_block * width).transpose(1, 2, 0, 3)
    sent = pack(left_out, right_out)
    columns = sent.shape[4]
    cot = pair_cotangent.transpose(1, 0, 2)
    bias = out_bias.astype(jnp.float32).reshape(1, pair_width)
    weight = own_first(out_weight, core)
    came = exchange(sent.reshape(devices, local, columns))
    came, outer_grad = lax.optimization_barrier((came, outer_grads(weight, cot, width)))
    came = came.reshape(seqs, columns)
    left_other = swap_cores(came[:, :panel])
    left_part, right_partial = left_grads(came, outer_grad)
    left_other, left_part = lax.optimization_barrier((left_other, left_part))
    left_share = swap_cores(left_part[:, panel:])
    right_part = right_grads(left_other, right_partial, outer_grad)
    left_pair = (left_part[:, :panel].astype(jnp.float32) + left_share.astype(jnp.float32)).astype(jnp.bfloat16)
    sent = jnp.concatenate([left_pair, right_part], axis=1).reshape(devices, local, columns)
    sent, left_other = lax.optimization_barrier((sent, left_other))
    back = exchange(sent).reshape(seqs, columns)
    update, weight_term = forward(core, came, left_other, weight.T, bias, cot, width)
    early = 2
    weight_term = weight_term.reshape(devices, -1, pair_width)
    weight_term = sum_scatter(weight_term, permute_groups()[:early - 1])
    low, size = permute_groups()[early - 1]
    kept, *pieces = scatter_pieces(weight_term, low, size)
    weight_parts = [kept] + [partner(piece, low * (k + 1)) for k, piece in enumerate(pieces)]
    back, update = lax.optimization_barrier((back, update))
    pair_update = row_major(update.transpose(1, 0, 2))

    place = np.indices((row_count, chips, CORES, local)).reshape(4, -1)
    left_place = (place[3] * row_count + place[0]) * CORES + place[2]
    right_place = (place[3] * chips + place[1]) * CORES + place[2]
    left_rows, right_rows = local * row_count * CORES, local * chips * CORES
    left_pick = jnp.asarray(np.arange(left_rows)[:, None] == left_place[None], dtype=jnp.bfloat16)
    right_pick = jnp.asarray(np.arange(right_rows)[:, None] == right_place[None], dtype=jnp.bfloat16)
    left_grad = jnp.dot(left_pick, back[:, :panel], preferred_element_type=jnp.float32).astype(jnp.bfloat16)
    right_grad = jnp.dot(right_pick, back[:, panel:], preferred_element_type=jnp.float32).astype(jnp.bfloat16)
    left_grad = left_grad.reshape(local, row_count, width, row_block).transpose(0, 2, 1, 3)
    left_grad = left_grad.reshape(local, width, residues)
    right_grad = right_grad.reshape(local, residues, width)
    left_wgrad = jnp.einsum("src,shr->hc", normed_low, left_grad, preferred_element_type=jnp.float32)
    right_wgrad = jnp.einsum("src,srh->hc", normed_low, right_grad, preferred_element_type=jnp.float32)
    upstream = jnp.einsum("shr,ch->src", left_grad, left_weight, preferred_element_type=jnp.float32)
    upstream += jnp.einsum("srh,ch->src", right_grad, right_weight, preferred_element_type=jnp.float32)
    grad_alignment = norm_backward(upstream, normed, inv_sigma).astype(jnp.bfloat16)
    grad_alignment = flip(grad_alignment.transpose(0, 2, 1))
    left_wgrad, right_wgrad, weight_term, (grad_alignment, pair_update) = sum_all(
        left_wgrad, right_wgrad, weight_parts, early, [grad_alignment, pair_update]
    )
    grad_out_weight = weight_term.reshape(-1, pair_width)
    return (pair_update, grad_alignment, grad_out_weight, left_wgrad.T, right_wgrad.T)


def solution(mesh):
    return jax.shard_map(
        body,
        mesh=mesh,
        in_specs=(P(("row", "col"), None, None), P(), P(), P(), P(), P("row", "col", None)),
        out_specs=(
            P("row", "col", None),
            P(("row", "col"), None, None),
            P(("row", "col"), None),
            P(),
            P(),
        ),
        check_vma=False,
    )
```

```python
import functools

import jax
import jax.numpy as jnp
import numpy as np
from jax import lax
from jax.experimental import layout
from jax.experimental import pallas as pl
from jax.experimental.pallas import tpu as pltpu
from jax.sharding import PartitionSpec as P

BOTH = ("row", "col")
TILE = 16
GRAD_TILE = 8
BLOCKS = 4
CORES = 2
VMEM_BYTES = 48 * 1024 * 1024
NT = (((1,), (1,)), ((), ()))


def layer_norm(values):
    centered = values - jnp.mean(values, axis=-1, keepdims=True)
    inv_sigma = lax.rsqrt(jnp.mean(centered * centered, axis=-1, keepdims=True) + 1e-05)
    return (centered * inv_sigma, inv_sigma)


def norm_backward(upstream, normed, inv_sigma):
    first = jnp.mean(upstream, axis=-1, keepdims=True)
    second = jnp.mean(upstream * normed, axis=-1, keepdims=True)
    return inv_sigma * (upstream - first - normed * second)


def outer_grad_kernel(width, weight_ref, cot_ref, grad_ref):
    tile, rows, pair_width = cot_ref.shape
    flat = cot_ref[...].reshape(tile * rows, pair_width)
    step = 2
    for j in range(0, tile, step):
        grads = lax.dot_general(
            weight_ref[...], flat[j * rows:(j + step) * rows], NT, preferred_element_type=jnp.float32
        ).astype(jnp.bfloat16)
        for k in range(step):
            for c in range(width):
                grad_ref[(j + k) * width:(j + k + 1) * width, c * rows:(c + 1) * rows] = grads[
                    c * width:(c + 1) * width, k * rows:(k + 1) * rows
                ]


def left_kernel(inverse, came_ref, grad_ref, out_ref, partial_ref, panel_ref, held_ref, sems):
    blocks = sems.shape[0] - 2
    depth, columns = held_ref.shape
    block, half = columns // blocks, columns // CORES
    panel = pltpu.make_async_copy(came_ref, panel_ref, sems.at[blocks + 1])
    panel.start()
    parts = [pl.ds(0, block // 2), pl.ds(block // 2, block // 2)]
    parts += [pl.ds(n * block, block) for n in range(1, blocks)]
    copies = [
        pltpu.make_async_copy(grad_ref.at[:, part], held_ref.at[:, part], sems.at[n]) for n, part in enumerate(parts)
    ]
    for copy in copies:
        copy.start()
    panel.wait()
    for n, part in enumerate(parts):
        if n == blocks // CORES + 1:
            partial_ref[...] = lax.dot_general(
                panel_ref[:, :half], held_ref[:, :half], NT, preferred_element_type=jnp.float32
            )
        copies[n].wait()
        grads = jnp.dot(panel_ref[:, -depth:], held_ref[:, part], preferred_element_type=jnp.float32)
        out_ref[:, part] = (grads * inverse).astype(out_ref.dtype)


def right_kernel(inverse, other_ref, partial_ref, grad_ref, out_ref, held_ref, sems):
    blocks = sems.shape[0]
    rows, depth = held_ref.shape
    block = rows // blocks
    parts = [pl.ds(n * block, block) for n in range(blocks)]
    copies = [
        pltpu.make_async_copy(grad_ref.at[part, pl.ds(depth, depth)], held_ref.at[part], sems.at[n])
        for n, part in enumerate(parts)
    ]
    for copy in copies:
        copy.start()
    for n, part in enumerate(parts):
        copies[n].wait()
        grads = lax.dot_general(other_ref[...], held_ref[part], NT, preferred_element_type=jnp.float32)
        out_ref[:, part] = ((partial_ref[:, part] + grads) * inverse).astype(out_ref.dtype)


def pack_kernel(left_ref, right_ref, out_ref, sems):
    rows, chips = out_ref.shape[:2]
    panel = left_ref.shape[-1]
    copies = [
        pltpu.make_async_copy(right_ref, out_ref.at[k, :, :, :, pl.ds(panel, right_ref.shape[-1])], sems.at[k])
        for k in range(rows)
    ]
    copies += [
        pltpu.make_async_copy(left_ref, out_ref.at[:, k, :, :, pl.ds(0, panel)], sems.at[rows + k])
        for k in range(chips)
    ]
    for copy in copies:
        copy.start()
    for copy in copies:
        copy.wait()


def forward_kernel(
    inverse, width, core_ref, own_ref, other_ref, right_ref, weight_t_ref, bias_ref, cot_ref, update_ref, wgrad_ref, outer_ref
):
    tile, rows, pair_width = cot_ref.shape
    right_t = right_ref[...].T
    step = 2
    for c in range(0, width, step):
        half_ref, first = (own_ref, c) if c < width // 2 else (other_ref, c - width // 2)
        outer = jnp.dot(
            right_t, half_ref[:, first * rows:(first + step) * rows], preferred_element_type=jnp.float32
        ).astype(jnp.bfloat16)
        for k in range(step):
            for j in range(tile):
                outer_ref[(c + k) * width:(c + k + 1) * width, j * rows:(j + 1) * rows] = outer[
                    j * width:(j + 1) * width, k * rows:(k + 1) * rows
                ]
    for j in range(0, tile, step):
        update = jnp.dot(
            weight_t_ref[...], outer_ref[:, j * rows:(j + step) * rows], preferred_element_type=jnp.float32
        )
        for k in range(step):
            one = update[:, k * rows:(k + 1) * rows].T
            update_ref[j + k] = (one * inverse + bias_ref[...]).astype(update_ref.dtype)

    @pl.when(pl.program_id(0) == 0)
    def _():
        wgrad_ref[...] = jnp.zeros_like(wgrad_ref)

    flat = cot_ref[...].reshape(tile * rows, pair_width)
    half = wgrad_ref.shape[0] // CORES
    for k in range(CORES):
        place = pl.ds(pl.multiple_of((core_ref[0] ^ k) * half, half), half)
        wgrad_ref[place] += inverse * jnp.dot(
            outer_ref[k * half:(k + 1) * half], flat, preferred_element_type=jnp.float32
        )


def whole(shape):
    return pl.BlockSpec(shape, lambda j: (0,) * len(shape))


def params():
    return pltpu.CompilerParams(dimension_semantics=("arbitrary",), vmem_limit_bytes=VMEM_BYTES)


def outer_grads(weight, cot, width, interpret=False):
    cols, rows, pair_width = cot.shape
    return pl.pallas_call(
        functools.partial(outer_grad_kernel, width),
        grid=(cols // GRAD_TILE,),
        in_specs=[whole(weight.shape), pl.BlockSpec((GRAD_TILE, rows, pair_width), lambda j: (j, 0, 0))],
        out_specs=pl.BlockSpec((GRAD_TILE * width, width * rows), lambda j: (j, 0)),
        out_shape=jax.ShapeDtypeStruct((cols * width, width * rows), jnp.bfloat16),
        compiler_params=params(),
        cost_estimate=pl.CostEstimate(
            flops=2 * cols * rows * width * width * pair_width, bytes_accessed=18 * 2**20, transcendentals=0
        ),
        interpret=interpret,
        name="outer_grads",
    )(weight, cot)


def left_grads(came, grads, interpret=False):
    seqs, (depth, columns) = came.shape[0], grads.shape
    return pl.pallas_call(
        functools.partial(left_kernel, 1.0 / seqs),
        in_specs=[pl.BlockSpec(memory_space=pl.ANY)] * 2,
        out_specs=[pl.BlockSpec(memory_space=pltpu.VMEM)] * 2,
        out_shape=[
            jax.ShapeDtypeStruct((seqs, columns), jnp.bfloat16),
            jax.ShapeDtypeStruct((seqs, depth), jnp.float32),
        ],
        scratch_shapes=[
            pltpu.VMEM(came.shape, jnp.bfloat16),
            pltpu.VMEM(grads.shape, jnp.bfloat16),
            pltpu.SemaphoreType.DMA((BLOCKS + 2,)),
        ],
        compiler_params=pltpu.CompilerParams(vmem_limit_bytes=VMEM_BYTES),
        cost_estimate=pl.CostEstimate(flops=3 * seqs * depth * columns, bytes_accessed=21 * 2**20, transcendentals=0),
        interpret=interpret,
        name="left_grads",
    )(came, grads)


def right_grads(other, partial, grads, interpret=False):
    seqs, (rows, depth) = other.shape[0], grads.shape
    return pl.pallas_call(
        functools.partial(right_kernel, 1.0 / seqs),
        in_specs=[pl.BlockSpec(memory_space=pltpu.VMEM)] * 2 + [pl.BlockSpec(memory_space=pl.ANY)],
        out_specs=pl.BlockSpec(memory_space=pltpu.VMEM),
        out_shape=jax.ShapeDtypeStruct((seqs, rows), jnp.bfloat16),
        scratch_shapes=[pltpu.VMEM((rows, depth // CORES), jnp.bfloat16), pltpu.SemaphoreType.DMA((BLOCKS,))],
        compiler_params=pltpu.CompilerParams(vmem_limit_bytes=VMEM_BYTES),
        cost_estimate=pl.CostEstimate(flops=seqs * depth * rows, bytes_accessed=12 * 2**20, transcendentals=0),
        interpret=interpret,
        name="right_grads",
    )(other, partial, grads)


def pack(left, right, interpret=False):
    shape = (left.shape[0],) + right.shape[:-1] + (left.shape[-1] + right.shape[-1],)
    return pl.pallas_call(
        pack_kernel,
        in_specs=[pl.BlockSpec(memory_space=pltpu.VMEM)] * 2,
        out_specs=pl.BlockSpec(memory_space=pl.ANY),
        out_shape=jax.ShapeDtypeStruct(shape, left.dtype),
        scratch_shapes=[pltpu.SemaphoreType.DMA((shape[0] + shape[1],))],
        cost_estimate=pl.CostEstimate(flops=0, bytes_accessed=2 * 2**20, transcendentals=0),
        interpret=interpret,
        name="pack",
    )(left, right)


def forward(core, came, other, weight_t, bias, cot, width, interpret=False):
    seqs, cols, rows, pair_width = came.shape[0], cot.shape[0], cot.shape[1], cot.shape[2]
    flops = 2 * cols * rows * width * width * (2 * pair_width + seqs)
    first = other.shape[1] // (TILE * width)
    return pl.pallas_call(
        functools.partial(forward_kernel, 1.0 / seqs, width),
        grid=(cols // TILE,),
        in_specs=[
            pl.BlockSpec(memory_space=pltpu.SMEM),
            pl.BlockSpec(other.shape, lambda j: (0, 0)),
            whole(other.shape),
            pl.BlockSpec((seqs, TILE * width), lambda j: (0, first + j)),
            whole(weight_t.shape),
            whole(bias.shape),
            pl.BlockSpec((TILE, rows, pair_width), lambda j: (j, 0, 0)),
        ],
        out_specs=[
            pl.BlockSpec((TILE, rows, pair_width), lambda j: (j, 0, 0)),
            whole((width * width, pair_width)),
        ],
        out_shape=[
            jax.ShapeDtypeStruct((cols, rows, pair_width), jnp.bfloat16),
            jax.ShapeDtypeStruct((width * width, pair_width), jnp.float32),
        ],
        scratch_shapes=[pltpu.VMEM((width * width, TILE * rows), jnp.bfloat16)],
        compiler_params=params(),
        cost_estimate=pl.CostEstimate(flops=flops, bytes_accessed=8 * 2**20, transcendentals=0),
        interpret=interpret,
        name="forward",
    )(core.reshape(1), came, other, came, weight_t, bias, cot)


def flip_kernel(in_ref, out_ref):
    for k in range(in_ref.shape[0]):
        out_ref[k] = in_ref[k].T


def flip(values, interpret=False):
    shape = (values.shape[0], values.shape[2], values.shape[1])
    return pl.pallas_call(
        flip_kernel,
        in_specs=[pl.BlockSpec(memory_space=pltpu.VMEM)],
        out_specs=pl.BlockSpec(memory_space=pltpu.VMEM),
        out_shape=jax.ShapeDtypeStruct(shape, values.dtype),
        compiler_params=pltpu.CompilerParams(vmem_limit_bytes=VMEM_BYTES),
        cost_estimate=pl.CostEstimate(flops=0, bytes_accessed=2 * 2**20, transcendentals=0),
        interpret=interpret,
        name="flip",
    )(values)


def exchange(blocks):
    return lax.all_to_all(blocks, BOTH, 0, 0, tiled=True)


def swap_cores(values):
    return lax.ppermute(values, "col", [(i, i ^ 1) for i in range(lax.axis_size("col"))])


def own_first(values, core):
    half = values.shape[0] // CORES
    return jnp.where(core == 0, values, jnp.concatenate([values[half:], values[:half]], axis=0))


def row_major(values):
    return layout.with_layout_constraint(values, layout.Layout(major_to_minor=tuple(range(values.ndim))))


def permute_groups():
    devices = lax.axis_size(BOTH)
    groups = [(1, CORES)]
    while groups[-1][0] * groups[-1][1] < devices:
        low = groups[-1][0] * groups[-1][1]
        groups.append((low, min(4, devices // low)))
    return groups


def partner(part, mask):
    return lax.ppermute(part, BOTH, [(i, i ^ mask) for i in range(lax.axis_size(BOTH))])


def add_parts(parts):
    while len(parts) > 1:
        parts = [parts[k] + parts[k + 1] for k in range(0, len(parts), 2)]
    return parts[0]


def scatter_pieces(values, low, size):
    values = values.reshape((-1, size) + values.shape[1:])
    mine = lax.axis_index(BOTH) // low % size
    return [lax.dynamic_index_in_dim(values, mine ^ mask, 1, keepdims=False) for mask in range(size)]


def sum_scatter(values, groups):
    for low, size in groups:
        kept, *pieces = scatter_pieces(values, low, size)
        values = add_parts([kept] + [partner(piece, low * (k + 1)) for k, piece in enumerate(pieces)])
    return values


def sum_all(first, second, values, early, beside):
    core = lax.axis_index(BOTH) % CORES
    own, other = jnp.where(core == 0, first, second), jnp.where(core == 0, second, first)
    part = own + partner(other, 1)
    rows, columns = part.shape
    for step, (low, size) in enumerate(permute_groups()):
        if step == 0:
            continue
        if step < early:
            part = add_parts([part] + [partner(part, low * mask) for mask in range(1, size)])
            continue
        if step == len(permute_groups()) - 1:
            part, beside[0] = lax.optimization_barrier((part, beside[0]))
        share, lanes = values.shape[1:]
        pieces = [piece.reshape(-1, lanes) for piece in scatter_pieces(values, low, size)]
        used = pieces[0].shape[0]
        pieces = [jnp.pad(piece, ((0, rows - used), (0, 0))) for piece in pieces]
        sent = [jnp.concatenate([part, piece], axis=1) for piece in pieces]
        both = add_parts(sent[:1] + [partner(sent[mask], low * mask) for mask in range(1, size)])
        part, values = both[:, :columns], both[:used, columns:].reshape(-1, share, lanes)
    part, beside[1] = lax.optimization_barrier((part, beside[1]))
    other = partner(part, 1)
    return jnp.where(core == 0, part, other), jnp.where(core == 0, other, part), values, beside


def body(alignment, left_weight, right_weight, out_weight, out_bias, pair_cotangent):
    row_count = lax.axis_size("row")
    col_count = lax.axis_size("col")
    devices = row_count * col_count
    local, residues, model_width = alignment.shape
    width = left_weight.shape[1]
    row_block, col_block, pair_width = pair_cotangent.shape
    seqs = local * devices

    normed, inv_sigma = layer_norm(alignment.astype(jnp.float32))
    normed_low = normed.astype(jnp.bfloat16)
    left = jnp.einsum("src,ch->shr", normed_low, left_weight, preferred_element_type=jnp.float32).astype(
        jnp.bfloat16
    )
    right = jnp.einsum("src,ch->srh", normed_low, right_weight, preferred_element_type=jnp.float32).astype(
        jnp.bfloat16
    )
    chips = col_count // CORES
    core = lax.axis_index("col") % CORES
    panel = row_block * width // CORES
    left_out = left.reshape(local, CORES, width // CORES, row_count, row_block).transpose(3, 1, 0, 2, 4)
    left_out = left_out.reshape(row_count, CORES, local, panel)
    right_out = right.reshape(local, chips, CORES, col_block * width).transpose(1, 2, 0, 3)
    sent = pack(left_out, right_out)
    columns = sent.shape[4]
    cot = pair_cotangent.transpose(1, 0, 2)
    bias = out_bias.astype(jnp.float32).reshape(1, pair_width)
    weight = own_first(out_weight, core)
    came = exchange(sent.reshape(devices, local, columns))
    came, outer_grad = lax.optimization_barrier((came, outer_grads(weight, cot, width)))
    came = came.reshape(seqs, columns)
    left_other = swap_cores(came[:, :panel])
    left_part, right_partial = left_grads(came, outer_grad)
    left_other, left_part = lax.optimization_barrier((left_other, left_part))
    left_share = swap_cores(left_part[:, panel:])
    right_part = right_grads(left_other, right_partial, outer_grad)
    left_pair = (left_part[:, :panel].astype(jnp.float32) + left_share.astype(jnp.float32)).astype(jnp.bfloat16)
    sent = jnp.concatenate([left_pair, right_part], axis=1).reshape(devices, local, columns)
    sent, left_other = lax.optimization_barrier((sent, left_other))
    back = exchange(sent).reshape(seqs, columns)
    update, weight_term = forward(core, came, left_other, weight.T, bias, cot, width)
    early = 2
    weight_term = weight_term.reshape(devices, -1, pair_width)
    weight_term = sum_scatter(weight_term, permute_groups()[:early])
    back, weight_term, update = lax.optimization_barrier((back, weight_term, update))
    pair_update = row_major(update.transpose(1, 0, 2))

    place = np.indices((row_count, chips, CORES, local)).reshape(4, -1)
    left_place = (place[3] * row_count + place[0]) * CORES + place[2]
    right_place = (place[3] * chips + place[1]) * CORES + place[2]
    left_rows, right_rows = local * row_count * CORES, local * chips * CORES
    left_pick = jnp.asarray(np.arange(left_rows)[:, None] == left_place[None], dtype=jnp.bfloat16)
    right_pick = jnp.asarray(np.arange(right_rows)[:, None] == right_place[None], dtype=jnp.bfloat16)
    left_grad = jnp.dot(left_pick, back[:, :panel], preferred_element_type=jnp.float32).astype(jnp.bfloat16)
    right_grad = jnp.dot(right_pick, back[:, panel:], preferred_element_type=jnp.float32).astype(jnp.bfloat16)
    left_grad = left_grad.reshape(local, row_count, width, row_block).transpose(0, 2, 1, 3)
    left_grad = left_grad.reshape(local, width, residues)
    right_grad = right_grad.reshape(local, residues, width)
    left_wgrad = jnp.einsum("src,shr->hc", normed_low, left_grad, preferred_element_type=jnp.float32)
    right_wgrad = jnp.einsum("src,srh->hc", normed_low, right_grad, preferred_element_type=jnp.float32)
    upstream = jnp.einsum("shr,ch->src", left_grad, left_weight, preferred_element_type=jnp.float32)
    upstream += jnp.einsum("srh,ch->src", right_grad, right_weight, preferred_element_type=jnp.float32)
    grad_alignment = norm_backward(upstream, normed, inv_sigma).astype(jnp.bfloat16)
    grad_alignment = flip(grad_alignment.transpose(0, 2, 1))
    left_wgrad, right_wgrad, weight_term, (grad_alignment, pair_update) = sum_all(
        left_wgrad, right_wgrad, weight_term, early, [grad_alignment, pair_update]
    )
    grad_out_weight = weight_term.reshape(-1, pair_width)
    return (pair_update, grad_alignment, grad_out_weight, left_wgrad.T, right_wgrad.T)


def solution(mesh):
    return jax.shard_map(
        body,
        mesh=mesh,
        in_specs=(P(("row", "col"), None, None), P(), P(), P(), P(), P("row", "col", None)),
        out_specs=(
            P("row", "col", None),
            P(("row", "col"), None, None),
            P(("row", "col"), None),
            P(),
            P(),
        ),
        check_vma=False,
    )
```

```python
import functools

import jax
import jax.numpy as jnp
import numpy as np
from jax import lax
from jax.experimental import layout
from jax.experimental import pallas as pl
from jax.experimental.pallas import tpu as pltpu
from jax.sharding import PartitionSpec as P

BOTH = ("row", "col")
TILE = 32
GRAD_TILE = 8
BLOCKS = 4
CORES = 2
VMEM_BYTES = 48 * 1024 * 1024
NT = (((1,), (1,)), ((), ()))


def layer_norm(values):
    centered = values - jnp.mean(values, axis=-1, keepdims=True)
    inv_sigma = lax.rsqrt(jnp.mean(centered * centered, axis=-1, keepdims=True) + 1e-05)
    return (centered * inv_sigma, inv_sigma)


def norm_backward(upstream, normed, inv_sigma):
    first = jnp.mean(upstream, axis=-1, keepdims=True)
    second = jnp.mean(upstream * normed, axis=-1, keepdims=True)
    return inv_sigma * (upstream - first - normed * second)


def outer_grad_kernel(width, weight_ref, cot_ref, grad_ref):
    tile, rows, pair_width = cot_ref.shape
    flat = cot_ref[...].reshape(tile * rows, pair_width)
    step = 2
    for j in range(0, tile, step):
        grads = lax.dot_general(
            weight_ref[...], flat[j * rows:(j + step) * rows], NT, preferred_element_type=jnp.float32
        ).astype(jnp.bfloat16)
        for k in range(step):
            for c in range(width):
                grad_ref[(j + k) * width:(j + k + 1) * width, c * rows:(c + 1) * rows] = grads[
                    c * width:(c + 1) * width, k * rows:(k + 1) * rows
                ]


def left_kernel(inverse, came_ref, grad_ref, out_ref, partial_ref, panel_ref, held_ref, sems):
    blocks = sems.shape[0] - 1
    depth, columns = held_ref.shape
    block, half = columns // blocks, columns // CORES
    panel = pltpu.make_async_copy(came_ref, panel_ref, sems.at[blocks])
    panel.start()
    parts = [pl.ds(n * block, block) for n in range(blocks)]
    copies = [
        pltpu.make_async_copy(grad_ref.at[:, part], held_ref.at[:, part], sems.at[n]) for n, part in enumerate(parts)
    ]
    for copy in copies:
        copy.start()
    panel.wait()
    for n, part in enumerate(parts):
        if n == blocks // CORES:
            partial_ref[...] = lax.dot_general(
                panel_ref[:, :half], held_ref[:, :half], NT, preferred_element_type=jnp.float32
            )
        copies[n].wait()
        grads = jnp.dot(panel_ref[:, -depth:], held_ref[:, part], preferred_element_type=jnp.float32)
        out_ref[:, part] = (grads * inverse).astype(out_ref.dtype)


def right_kernel(inverse, other_ref, partial_ref, grad_ref, out_ref, held_ref, sems):
    blocks = sems.shape[0]
    rows, depth = held_ref.shape
    block = rows // blocks
    parts = [pl.ds(n * block, block) for n in range(blocks)]
    copies = [
        pltpu.make_async_copy(grad_ref.at[part, pl.ds(depth, depth)], held_ref.at[part], sems.at[n])
        for n, part in enumerate(parts)
    ]
    for copy in copies:
        copy.start()
    for n, part in enumerate(parts):
        copies[n].wait()
        grads = lax.dot_general(other_ref[...], held_ref[part], NT, preferred_element_type=jnp.float32)
        out_ref[:, part] = ((partial_ref[:, part] + grads) * inverse).astype(out_ref.dtype)


def pack_kernel(left_ref, right_ref, out_ref, sems):
    rows, chips = out_ref.shape[:2]
    panel = left_ref.shape[-1]
    copies = [
        pltpu.make_async_copy(right_ref, out_ref.at[k, :, :, :, pl.ds(panel, right_ref.shape[-1])], sems.at[k])
        for k in range(rows)
    ]
    copies += [
        pltpu.make_async_copy(left_ref, out_ref.at[:, k, :, :, pl.ds(0, panel)], sems.at[rows + k])
        for k in range(chips)
    ]
    for copy in copies:
        copy.start()
    for copy in copies:
        copy.wait()


def forward_kernel(
    inverse, width, core_ref, own_ref, other_ref, right_ref, weight_t_ref, bias_ref, cot_ref, update_ref, wgrad_ref, outer_ref
):
    tile, rows, pair_width = cot_ref.shape
    right_t = right_ref[...].T
    step = 2
    for c in range(0, width, step):
        half_ref, first = (own_ref, c) if c < width // 2 else (other_ref, c - width // 2)
        outer = jnp.dot(
            right_t, half_ref[:, first * rows:(first + step) * rows], preferred_element_type=jnp.float32
        ).astype(jnp.bfloat16)
        for k in range(step):
            for j in range(tile):
                outer_ref[(c + k) * width:(c + k + 1) * width, j * rows:(j + 1) * rows] = outer[
                    j * width:(j + 1) * width, k * rows:(k + 1) * rows
                ]
    for j in range(0, tile, step):
        update = jnp.dot(
            weight_t_ref[...], outer_ref[:, j * rows:(j + step) * rows], preferred_element_type=jnp.float32
        )
        for k in range(step):
            one = update[:, k * rows:(k + 1) * rows].T
            update_ref[j + k] = (one * inverse + bias_ref[...]).astype(update_ref.dtype)

    @pl.when(pl.program_id(0) == 0)
    def _():
        wgrad_ref[...] = jnp.zeros_like(wgrad_ref)

    flat = cot_ref[...].reshape(tile * rows, pair_width)
    half = wgrad_ref.shape[0] // CORES
    for k in range(CORES):
        place = pl.ds(pl.multiple_of((core_ref[0] ^ k) * half, half), half)
        wgrad_ref[place] += inverse * jnp.dot(
            outer_ref[k * half:(k + 1) * half], flat, preferred_element_type=jnp.float32
        )


def whole(shape):
    return pl.BlockSpec(shape, lambda j: (0,) * len(shape))


def params():
    return pltpu.CompilerParams(dimension_semantics=("arbitrary",), vmem_limit_bytes=VMEM_BYTES)


def outer_grads(weight, cot, width, interpret=False):
    cols, rows, pair_width = cot.shape
    return pl.pallas_call(
        functools.partial(outer_grad_kernel, width),
        grid=(cols // GRAD_TILE,),
        in_specs=[whole(weight.shape), pl.BlockSpec((GRAD_TILE, rows, pair_width), lambda j: (j, 0, 0))],
        out_specs=pl.BlockSpec((GRAD_TILE * width, width * rows), lambda j: (j, 0)),
        out_shape=jax.ShapeDtypeStruct((cols * width, width * rows), jnp.bfloat16),
        compiler_params=params(),
        cost_estimate=pl.CostEstimate(
            flops=2 * cols * rows * width * width * pair_width, bytes_accessed=18 * 2**20, transcendentals=0
        ),
        interpret=interpret,
        name="outer_grads",
    )(weight, cot)


def left_grads(came, grads, interpret=False):
    seqs, (depth, columns) = came.shape[0], grads.shape
    return pl.pallas_call(
        functools.partial(left_kernel, 1.0 / seqs),
        in_specs=[pl.BlockSpec(memory_space=pl.ANY)] * 2,
        out_specs=[pl.BlockSpec(memory_space=pltpu.VMEM)] * 2,
        out_shape=[
            jax.ShapeDtypeStruct((seqs, columns), jnp.bfloat16),
            jax.ShapeDtypeStruct((seqs, depth), jnp.float32),
        ],
        scratch_shapes=[
            pltpu.VMEM(came.shape, jnp.bfloat16),
            pltpu.VMEM(grads.shape, jnp.bfloat16),
            pltpu.SemaphoreType.DMA((BLOCKS + 1,)),
        ],
        compiler_params=pltpu.CompilerParams(vmem_limit_bytes=VMEM_BYTES),
        cost_estimate=pl.CostEstimate(flops=3 * seqs * depth * columns, bytes_accessed=21 * 2**20, transcendentals=0),
        interpret=interpret,
        name="left_grads",
    )(came, grads)


def right_grads(other, partial, grads, interpret=False):
    seqs, (rows, depth) = other.shape[0], grads.shape
    return pl.pallas_call(
        functools.partial(right_kernel, 1.0 / seqs),
        in_specs=[pl.BlockSpec(memory_space=pltpu.VMEM)] * 2 + [pl.BlockSpec(memory_space=pl.ANY)],
        out_specs=pl.BlockSpec(memory_space=pltpu.VMEM),
        out_shape=jax.ShapeDtypeStruct((seqs, rows), jnp.bfloat16),
        scratch_shapes=[pltpu.VMEM((rows, depth // CORES), jnp.bfloat16), pltpu.SemaphoreType.DMA((BLOCKS,))],
        compiler_params=pltpu.CompilerParams(vmem_limit_bytes=VMEM_BYTES),
        cost_estimate=pl.CostEstimate(flops=seqs * depth * rows, bytes_accessed=12 * 2**20, transcendentals=0),
        interpret=interpret,
        name="right_grads",
    )(other, partial, grads)


def pack(left, right, interpret=False):
    shape = (left.shape[0],) + right.shape[:-1] + (left.shape[-1] + right.shape[-1],)
    return pl.pallas_call(
        pack_kernel,
        in_specs=[pl.BlockSpec(memory_space=pltpu.VMEM)] * 2,
        out_specs=pl.BlockSpec(memory_space=pl.ANY),
        out_shape=jax.ShapeDtypeStruct(shape, left.dtype),
        scratch_shapes=[pltpu.SemaphoreType.DMA((shape[0] + shape[1],))],
        cost_estimate=pl.CostEstimate(flops=0, bytes_accessed=2 * 2**20, transcendentals=0),
        interpret=interpret,
        name="pack",
    )(left, right)


def forward(core, came, other, weight_t, bias, cot, width, interpret=False):
    seqs, cols, rows, pair_width = came.shape[0], cot.shape[0], cot.shape[1], cot.shape[2]
    flops = 2 * cols * rows * width * width * (2 * pair_width + seqs)
    first = other.shape[1] // (TILE * width)
    return pl.pallas_call(
        functools.partial(forward_kernel, 1.0 / seqs, width),
        grid=(cols // TILE,),
        in_specs=[
            pl.BlockSpec(memory_space=pltpu.SMEM),
            pl.BlockSpec(other.shape, lambda j: (0, 0)),
            whole(other.shape),
            pl.BlockSpec((seqs, TILE * width), lambda j: (0, first + j)),
            whole(weight_t.shape),
            whole(bias.shape),
            pl.BlockSpec((TILE, rows, pair_width), lambda j: (j, 0, 0)),
        ],
        out_specs=[
            pl.BlockSpec((TILE, rows, pair_width), lambda j: (j, 0, 0)),
            whole((width * width, pair_width)),
        ],
        out_shape=[
            jax.ShapeDtypeStruct((cols, rows, pair_width), jnp.bfloat16),
            jax.ShapeDtypeStruct((width * width, pair_width), jnp.float32),
        ],
        scratch_shapes=[pltpu.VMEM((width * width, TILE * rows), jnp.bfloat16)],
        compiler_params=params(),
        cost_estimate=pl.CostEstimate(flops=flops, bytes_accessed=8 * 2**20, transcendentals=0),
        interpret=interpret,
        name="forward",
    )(core.reshape(1), came, other, came, weight_t, bias, cot)


def flip_kernel(in_ref, out_ref):
    for k in range(in_ref.shape[0]):
        out_ref[k] = in_ref[k].T


def flip(values, interpret=False):
    shape = (values.shape[0], values.shape[2], values.shape[1])
    return pl.pallas_call(
        flip_kernel,
        in_specs=[pl.BlockSpec(memory_space=pltpu.VMEM)],
        out_specs=pl.BlockSpec(memory_space=pltpu.VMEM),
        out_shape=jax.ShapeDtypeStruct(shape, values.dtype),
        compiler_params=pltpu.CompilerParams(vmem_limit_bytes=VMEM_BYTES),
        cost_estimate=pl.CostEstimate(flops=0, bytes_accessed=2 * 2**20, transcendentals=0),
        interpret=interpret,
        name="flip",
    )(values)


def exchange(blocks):
    return lax.all_to_all(blocks, BOTH, 0, 0, tiled=True)


def swap_cores(values):
    return lax.ppermute(values, "col", [(i, i ^ 1) for i in range(lax.axis_size("col"))])


def own_first(values, core):
    half = values.shape[0] // CORES
    return jnp.where(core == 0, values, jnp.concatenate([values[half:], values[:half]], axis=0))


def row_major(values):
    return layout.with_layout_constraint(values, layout.Layout(major_to_minor=tuple(range(values.ndim))))


def permute_groups():
    devices = lax.axis_size(BOTH)
    groups = [(1, CORES)]
    while groups[-1][0] * groups[-1][1] < devices:
        low = groups[-1][0] * groups[-1][1]
        groups.append((low, min(4, devices // low)))
    return groups


def partner(part, mask):
    return lax.ppermute(part, BOTH, [(i, i ^ mask) for i in range(lax.axis_size(BOTH))])


def add_parts(parts):
    while len(parts) > 1:
        parts = [parts[k] + parts[k + 1] for k in range(0, len(parts), 2)]
    return parts[0]


def scatter_pieces(values, low, size):
    values = values.reshape((-1, size) + values.shape[1:])
    mine = lax.axis_index(BOTH) // low % size
    return [lax.dynamic_index_in_dim(values, mine ^ mask, 1, keepdims=False) for mask in range(size)]


def sum_scatter(values, groups):
    for low, size in groups:
        kept, *pieces = scatter_pieces(values, low, size)
        values = add_parts([kept] + [partner(piece, low * (k + 1)) for k, piece in enumerate(pieces)])
    return values


def sum_all(first, second, values, early, beside):
    core = lax.axis_index(BOTH) % CORES
    own, other = jnp.where(core == 0, first, second), jnp.where(core == 0, second, first)
    part = own + partner(other, 1)
    rows, columns = part.shape
    for step, (low, size) in enumerate(permute_groups()):
        if step == 0:
            continue
        if step < early:
            part = add_parts([part] + [partner(part, low * mask) for mask in range(1, size)])
            continue
        if step == len(permute_groups()) - 1:
            part, beside[0] = lax.optimization_barrier((part, beside[0]))
        share, lanes = values.shape[1:]
        pieces = [piece.reshape(-1, lanes) for piece in scatter_pieces(values, low, size)]
        used = pieces[0].shape[0]
        pieces = [jnp.pad(piece, ((0, rows - used), (0, 0))) for piece in pieces]
        sent = [jnp.concatenate([part, piece], axis=1) for piece in pieces]
        both = add_parts(sent[:1] + [partner(sent[mask], low * mask) for mask in range(1, size)])
        part, values = both[:, :columns], both[:used, columns:].reshape(-1, share, lanes)
    part, beside[1] = lax.optimization_barrier((part, beside[1]))
    other = partner(part, 1)
    return jnp.where(core == 0, part, other), jnp.where(core == 0, other, part), values, beside


def body(alignment, left_weight, right_weight, out_weight, out_bias, pair_cotangent):
    row_count = lax.axis_size("row")
    col_count = lax.axis_size("col")
    devices = row_count * col_count
    local, residues, model_width = alignment.shape
    width = left_weight.shape[1]
    row_block, col_block, pair_width = pair_cotangent.shape
    seqs = local * devices

    normed, inv_sigma = layer_norm(alignment.astype(jnp.float32))
    normed_low = normed.astype(jnp.bfloat16)
    left = jnp.einsum("src,ch->shr", normed_low, left_weight, preferred_element_type=jnp.float32).astype(
        jnp.bfloat16
    )
    right = jnp.einsum("src,ch->srh", normed_low, right_weight, preferred_element_type=jnp.float32).astype(
        jnp.bfloat16
    )
    chips = col_count // CORES
    core = lax.axis_index("col") % CORES
    panel = row_block * width // CORES
    left_out = left.reshape(local, CORES, width // CORES, row_count, row_block).transpose(3, 1, 0, 2, 4)
    left_out = left_out.reshape(row_count, CORES, local, panel)
    right_out = right.reshape(local, chips, CORES, col_block * width).transpose(1, 2, 0, 3)
    sent = pack(left_out, right_out)
    columns = sent.shape[4]
    cot = pair_cotangent.transpose(1, 0, 2)
    bias = out_bias.astype(jnp.float32).reshape(1, pair_width)
    weight = own_first(out_weight, core)
    came = exchange(sent.reshape(devices, local, columns))
    came, outer_grad = lax.optimization_barrier((came, outer_grads(weight, cot, width)))
    came = came.reshape(seqs, columns)
    left_other = swap_cores(came[:, :panel])
    left_part, right_partial = left_grads(came, outer_grad)
    left_other, left_part = lax.optimization_barrier((left_other, left_part))
    left_share = swap_cores(left_part[:, panel:])
    right_part = right_grads(left_other, right_partial, outer_grad)
    left_pair = (left_part[:, :panel].astype(jnp.float32) + left_share.astype(jnp.float32)).astype(jnp.bfloat16)
    sent = jnp.concatenate([left_pair, right_part], axis=1).reshape(devices, local, columns)
    sent, left_other = lax.optimization_barrier((sent, left_other))
    back = exchange(sent).reshape(seqs, columns)
    update, weight_term = forward(core, came, left_other, weight.T, bias, cot, width)
    early = 2
    weight_term = weight_term.reshape(devices, -1, pair_width)
    weight_term = sum_scatter(weight_term, permute_groups()[:early])
    back, weight_term, update = lax.optimization_barrier((back, weight_term, update))
    pair_update = row_major(update.transpose(1, 0, 2))

    place = np.indices((row_count, chips, CORES, local)).reshape(4, -1)
    left_place = (place[3] * row_count + place[0]) * CORES + place[2]
    right_place = (place[3] * chips + place[1]) * CORES + place[2]
    left_rows, right_rows = local * row_count * CORES, local * chips * CORES
    left_pick = jnp.asarray(np.arange(left_rows)[:, None] == left_place[None], dtype=jnp.bfloat16)
    right_pick = jnp.asarray(np.arange(right_rows)[:, None] == right_place[None], dtype=jnp.bfloat16)
    left_grad = jnp.dot(left_pick, back[:, :panel], preferred_element_type=jnp.float32).astype(jnp.bfloat16)
    right_grad = jnp.dot(right_pick, back[:, panel:], preferred_element_type=jnp.float32).astype(jnp.bfloat16)
    left_grad = left_grad.reshape(local, row_count, width, row_block).transpose(0, 2, 1, 3)
    left_grad = left_grad.reshape(local, width, residues)
    right_grad = right_grad.reshape(local, residues, width)
    left_wgrad = jnp.einsum("src,shr->hc", normed_low, left_grad, preferred_element_type=jnp.float32)
    right_wgrad = jnp.einsum("src,srh->hc", normed_low, right_grad, preferred_element_type=jnp.float32)
    upstream = jnp.einsum("shr,ch->src", left_grad, left_weight, preferred_element_type=jnp.float32)
    upstream += jnp.einsum("srh,ch->src", right_grad, right_weight, preferred_element_type=jnp.float32)
    grad_alignment = norm_backward(upstream, normed, inv_sigma).astype(jnp.bfloat16)
    grad_alignment = flip(grad_alignment.transpose(0, 2, 1))
    left_wgrad, right_wgrad, weight_term, (grad_alignment, pair_update) = sum_all(
        left_wgrad, right_wgrad, weight_term, early, [grad_alignment, pair_update]
    )
    grad_out_weight = weight_term.reshape(-1, pair_width)
    return (pair_update, grad_alignment, grad_out_weight, left_wgrad.T, right_wgrad.T)


def solution(mesh):
    return jax.shard_map(
        body,
        mesh=mesh,
        in_specs=(P(("row", "col"), None, None), P(), P(), P(), P(), P("row", "col", None)),
        out_specs=(
            P("row", "col", None),
            P(("row", "col"), None, None),
            P(("row", "col"), None),
            P(),
            P(),
        ),
        check_vma=False,
    )
```
